32 devices in a mesh: stream: 4 (over y, x), seq: 8 (over z, core).
Axes of the slice: x: 2, y: 2, z: 4, core: 2. Of those that a mesh axis runs over, the one named last changes fastest.
Arguments:
- frame_rows: bfloat16 [16384, 512], P(('stream', 'seq')), as said below
- row_frame: int32 [16384], P(('stream', 'seq')), may hold values from -1 to 16383, as said below
- frame_owner: int32 [4, 4096], P('stream', 'seq'), may hold values from -1 to 31, as said below
- lengths: int32 [4], P('stream'), may hold values from 1024 to 4096, as said below
- query_weight: bfloat16 [512, 512], replicated
- key_weight: bfloat16 [512, 512], replicated
- value_weight: bfloat16 [512, 512], replicated, may hold values from -0.25 to 0.25
- out_weight: bfloat16 [512, 512], replicated, may hold values from -0.25 to 0.25
- cotangent: bfloat16 [4, 4096, 512], P('stream', 'seq'), may hold values from -6 to 6
Outputs:
- out_frames: bfloat16 [4, 4096, 512], P('stream', 'seq')
- frame_grads: bfloat16 [16384, 512], P(('stream', 'seq'))
- weight_grads: float32 [512, 2048], P(('stream', 'seq'))
The draws below stay inside these ranges and needn't reach their ends.
Inputs may be any that keep to these rules, and one draw needn't show every extreme that they name: Frames at and beyond lengths[s] are padding. The last stream has 4096 valid frames and some other stream 4096 // 4. `frame_owner`: the backbone device (index over stream and seq together, stream slowest) holding each valid frame; -1 exactly at padding frames. At most 16 frames of one time shard of 512 frames lie on one backbone device, and a shard whose frames are all valid puts exactly 16 on each. `row_frame`: the frame s * 4096 + t held by each backbone row, or -1 for an empty row. Every valid frame is held by exactly one row, on the device that frame_owner names; a device's used rows come first, in increasing frame index. `frame_rows`: empty backbone rows are zero.
All inputs are finite; a program needn't handle non-finite values.
Results may differ from the reference program's by a relative error of at most 0.015.
Values may be sent and summed in bfloat16 or wider, within the bound.
No kernel may reach another device: no remote copies, remote signals or barrier semaphores. Data moves between devices by JAX's collectives and lax.ppermute only.
A program may use at most 128 MiB of HBM per device.

```python
import math
import jax
import jax.numpy as jnp
from jax import lax

D = 512
H = 8
WIN = 512
T_DEV = 512
DH = 64
STREAMS = 4
SLAB = 4096
SHARDS = 32


def frame_plan(key):
    key_len, key_pick, key_perm, key_off = jax.random.split(key, 4)
    seqs = SLAB // T_DEV
    total = SHARDS * T_DEV
    lengths = jax.random.randint(key_len, (STREAMS,), SLAB // 4, SLAB + 1)
    order = jax.random.permutation(key_pick, STREAMS - 1)
    lengths = lengths.at[STREAMS - 1].set(SLAB).at[order[0]].set(SLAB // 4)
    dealt = jax.vmap(lambda sub: jax.random.permutation(sub, T_DEV))(jax.random.split(key_perm, SHARDS))
    position = jnp.argsort(dealt, axis=1)
    offset = jax.random.randint(key_off, (SHARDS, 1), 0, SHARDS)
    holder = (offset + position) % SHARDS
    shard_ids = jnp.arange(SHARDS)
    stream_of = shard_ids // seqs
    begin = shard_ids % seqs * T_DEV
    times = begin[:, None] + jnp.arange(T_DEV)[None, :]
    live = times < lengths[stream_of][:, None]
    owner = jnp.where(live, holder, -1).astype(jnp.int32)
    frame_ids = jnp.arange(total).reshape(SHARDS, T_DEV)
    sort_key = jnp.where(live, holder * total + frame_ids, SHARDS * total + frame_ids).reshape(-1)
    sorted_ids = jnp.argsort(sort_key)
    counts = jnp.sum(owner.reshape(-1)[None, :] == shard_ids[:, None], axis=1)
    starts = jnp.cumsum(counts) - counts
    slot = jnp.arange(T_DEV)
    pick = jnp.minimum(starts[:, None] + slot[None, :], total - 1)
    rows = jnp.where(slot[None, :] < counts[:, None], sorted_ids[pick], -1).astype(jnp.int32).reshape(-1)
    return (lengths.astype(jnp.int32), owner.reshape(STREAMS, SLAB), rows)


def draw_lengths(key, part):
    return frame_plan(jax.random.fold_in(key, 71))[0]


def draw_frame_owner(key, part):
    return frame_plan(jax.random.fold_in(key, 71))[1]


def draw_row_frame(key, part):
    return frame_plan(jax.random.fold_in(key, 71))[2]


def draw_frame_rows(key, part):
    rows = frame_plan(jax.random.fold_in(key, 71))[2]
    key_row, key_col, key_val = jax.random.split(jax.random.fold_in(key, 5), 3)
    total = STREAMS * SLAB
    frame_scale = jnp.exp(jax.random.uniform(key_row, (total,), jnp.float32, 0.0, math.log(10.0)))
    feature_scale = jnp.exp(jax.random.uniform(key_col, (D,), jnp.float32, 0.0, math.log(3.0)))
    safe = jnp.maximum(rows, 0)
    values = jax.vmap(lambda ident: jax.random.normal(jax.random.fold_in(key_val, ident), (D,), jnp.float32))(safe)
    scales = frame_scale[safe]
    values = values * scales[:, None] * feature_scale[None, :]
    return jnp.where(rows[:, None] >= 0, values, 0.0).astype(jnp.bfloat16)


def query_key_pair(key):
    key_first, key_second = jax.random.split(key, 2)
    first = jax.random.normal(key_first, (D, D), jnp.float32) * D ** (-0.5)
    second = jax.random.normal(key_second, (D, D), jnp.float32) * D ** (-0.5)
    return (first, second)


def draw_query_weight(key, part):
    return query_key_pair(jax.random.fold_in(key, 29))[0].astype(jnp.bfloat16)


def draw_key_weight(key, part):
    return query_key_pair(jax.random.fold_in(key, 29))[1].astype(jnp.bfloat16)


def block_levels(key, extent, cuts, low, largest):
    level, own = 1.0, jax.random.fold_in(key, 6)
    for dim, parts in cuts:
        steps = jnp.exp(jax.random.uniform(jax.random.fold_in(own, dim), (parts,), jnp.float32, low / len(cuts), largest / len(cuts)))
        level = level * jnp.repeat(steps, extent[dim] // parts).reshape([-1 if axis == dim else 1 for axis in range(len(extent))])
    return level


def normal_values(key, dims, deviation, limit, cuts=(), held_as=jnp.bfloat16):
    factor_of = block_levels(key, dims, cuts, -0.22, 0.18) if cuts else 1.0
    drawn = jax.random.normal(key, dims, jnp.float32) * deviation * factor_of
    return jnp.minimum(jnp.maximum(drawn, -limit), limit).astype(held_as)


def setup_inputs(seed: int = 0) -> dict:
    seeds = jax.random.split(jax.random.key(seed), 10)
    frame_rows = draw_frame_rows(jax.random.fold_in(seeds[9], 71), 0)
    row_frame = draw_row_frame(jax.random.fold_in(seeds[9], 71), 0)
    frame_owner = draw_frame_owner(jax.random.fold_in(seeds[9], 71), 0)
    lengths = draw_lengths(jax.random.fold_in(seeds[9], 71), 0)
    query_weight = draw_query_weight(jax.random.fold_in(seeds[9], 71), 0)
    key_weight = draw_key_weight(jax.random.fold_in(seeds[9], 71), 0)
    value_weight = normal_values(seeds[6], (D, D), D ** -0.5, 0.25)
    out_weight = normal_values(seeds[7], (D, D), D ** -0.5, 0.25)
    cotangent = normal_values(seeds[8], (STREAMS, SLAB, D), 1.0, 6.0, ((0, 4), (1, 8)))
    return {"frame_rows": frame_rows, "row_frame": row_frame, "frame_owner": frame_owner, "lengths": lengths, "query_weight": query_weight, "key_weight": key_weight, "value_weight": value_weight, "out_weight": out_weight, "cotangent": cotangent}


NEG_FILL = -1e+30
EPS_NORM = 1e-06

def window_mask(query_time, key_time, length):
    row_valid = query_time < length
    mask = (key_time[None, :] > query_time[:, None] - WIN) & (key_time[None, :] <= query_time[:, None])
    mask = mask & (key_time[None, :] >= 0) & (key_time[None, :] < length) & row_valid[:, None]
    return (mask, row_valid)

def head_probs(query_block, key_block, mask, row_valid):
    query_count = query_block.shape[0]
    key_count = key_block.shape[0]
    query_heads = query_block.reshape(query_count, H, DH).astype(jnp.float32)
    key_heads = key_block.reshape(key_count, H, DH).astype(jnp.float32)
    scores = jnp.einsum('ahd,ehd->hae', query_heads, key_heads) * DH ** (-0.5)
    masked = jnp.where(mask[None], scores, NEG_FILL)
    highest = lax.optimization_barrier(jnp.max(masked, axis=-1, keepdims=True))
    highest = jnp.where(row_valid[None, :, None], highest, 0.0)
    raised = jnp.where(mask[None], jnp.exp(scores - highest), 0.0)
    denom = lax.optimization_barrier(jnp.sum(raised, axis=-1, keepdims=True)) + jnp.where(row_valid, 0.0, 1.0)[None, :, None]
    return raised / denom

def shard_forward(args):
    queries, keyval_ext, begin, length = args
    span = queries.shape[0]
    block = min(span, 512)
    pieces = []
    for block_num in range(span // block):
        first = block_num * block
        query_block = queries[first:first + block]
        keyval_block = keyval_ext[first:first + block + WIN]
        query_time = begin + first + lax.iota(jnp.int32, block)
        key_time = begin - WIN + first + lax.iota(jnp.int32, block + WIN)
        mask, row_valid = window_mask(query_time, key_time, length)
        probs = head_probs(query_block, keyval_block[:, :D], mask, row_valid)
        probs_low = lax.optimization_barrier(probs.astype(jnp.bfloat16)).astype(jnp.float32)
        value_heads = keyval_block[:, D:].reshape(block + WIN, H, DH).astype(jnp.float32)
        mixed = jnp.einsum('hae,ehd->ahd', probs_low, value_heads)
        pieces.append(mixed.reshape(block, D).astype(jnp.bfloat16))
    return jnp.concatenate(pieces, axis=0)

def shard_backward(args):
    queries, keyval_ext, grads, begin, length = args
    span = queries.shape[0]
    block = min(span, 512)
    query_parts = []
    keyval_grad = jnp.zeros((WIN + span, 2 * D), jnp.float32)
    for block_num in range(span // block):
        first = block_num * block
        query_block = queries[first:first + block]
        keyval_block = keyval_ext[first:first + block + WIN]
        query_time = begin + first + lax.iota(jnp.int32, block)
        key_time = begin - WIN + first + lax.iota(jnp.int32, block + WIN)
        mask, row_valid = window_mask(query_time, key_time, length)
        probs = head_probs(query_block, keyval_block[:, :D], mask, row_valid)
        probs_low = lax.optimization_barrier(probs.astype(jnp.bfloat16)).astype(jnp.float32)
        query_heads = query_block.reshape(block, H, DH).astype(jnp.float32)
        key_heads = keyval_block[:, :D].reshape(block + WIN, H, DH).astype(jnp.float32)
        value_heads = keyval_block[:, D:].reshape(block + WIN, H, DH).astype(jnp.float32)
        grad_heads = grads[first:first + block].reshape(block, H, DH).astype(jnp.float32)
        prob_grad = jnp.einsum('ahd,ehd->hae', grad_heads, value_heads)
        centre = lax.optimization_barrier(jnp.sum(probs * prob_grad, axis=-1, keepdims=True))
        score_grad = (probs * (prob_grad - centre) * DH ** (-0.5)).astype(jnp.bfloat16)
        score_grad = lax.optimization_barrier(score_grad).astype(jnp.float32)
        query_grad = jnp.einsum('hae,ehd->ahd', score_grad, key_heads).reshape(block, D)
        query_parts.append(query_grad.astype(jnp.bfloat16))
        key_grad = jnp.einsum('hae,ahd->ehd', score_grad, query_heads).reshape(block + WIN, D)
        value_grad = jnp.einsum('hae,ahd->ehd', probs_low, grad_heads).reshape(block + WIN, D)
        keyval_grad = keyval_grad.at[first:first + block + WIN].add(jnp.concatenate([key_grad, value_grad], axis=1))
    return (jnp.concatenate(query_parts, axis=0), keyval_grad[WIN:].astype(jnp.bfloat16), keyval_grad[:WIN].astype(jnp.bfloat16))

def reference(frame_rows, row_frame, frame_owner, lengths, query_weight, key_weight, value_weight, out_weight, cotangent):
    seqs = SLAB // T_DEV
    total = STREAMS * SLAB
    row_ids = jnp.arange(total, dtype=jnp.int32)
    target = jnp.where(row_frame >= 0, row_frame, total).astype(jnp.int32)
    source = jnp.full((total,), -1, jnp.int32).at[target].set(row_ids, mode='drop')
    owner = frame_owner.reshape(total)
    accepted = (source >= 0) & (owner == source // T_DEV)
    frames = jnp.where(accepted[:, None], frame_rows[jnp.maximum(source, 0)], jnp.zeros((), jnp.bfloat16))
    frames32 = frames.astype(jnp.float32)
    inverse = lax.rsqrt(lax.optimization_barrier(jnp.mean(frames32 * frames32, axis=1, keepdims=True)) + EPS_NORM)
    normed32 = frames32 * inverse
    normed = normed32.astype(jnp.bfloat16)
    projection = jnp.concatenate([query_weight, key_weight, value_weight], axis=1)
    projected = jnp.dot(normed, projection, preferred_element_type=jnp.float32).astype(jnp.bfloat16)
    queries = projected[:, :D].reshape(SHARDS, T_DEV, D)
    keyvals = projected[:, D:].reshape(SHARDS, T_DEV, 2 * D)
    shard_ids = jnp.arange(SHARDS, dtype=jnp.int32)
    not_first = shard_ids % seqs != 0
    previous = jnp.concatenate([jnp.zeros((1, T_DEV, 2 * D), jnp.bfloat16), keyvals[:-1]], axis=0)[:, T_DEV - WIN:]
    previous = jnp.where(not_first[:, None, None], previous, jnp.zeros((), jnp.bfloat16))
    keyval_ext = jnp.concatenate([previous, keyvals], axis=1)
    begins = (shard_ids % seqs * T_DEV).astype(jnp.int32)
    shard_len = lengths[shard_ids // seqs].astype(jnp.int32)
    attended = lax.map(shard_forward, (queries, keyval_ext, begins, shard_len)).reshape(total, D)
    out_frames = (frames32 + jnp.dot(attended, out_weight, preferred_element_type=jnp.float32)).astype(jnp.bfloat16)
    out_grad = cotangent.reshape(total, D)
    attended_grad = jnp.dot(out_grad, out_weight.T, preferred_element_type=jnp.float32).astype(jnp.bfloat16)
    query_grad, own_grad, prev_grad = lax.map(shard_backward, (queries, keyval_ext, attended_grad.reshape(SHARDS, T_DEV, D), begins, shard_len))
    has_next = shard_ids % seqs != seqs - 1
    later_grad = jnp.concatenate([prev_grad[1:], jnp.zeros((1, WIN, 2 * D), jnp.bfloat16)], axis=0)
    later_grad = jnp.where(has_next[:, None, None], later_grad, jnp.zeros((), jnp.bfloat16))
    keyval_weight = jnp.concatenate([key_weight, value_weight], axis=1)
    query_flat = query_grad.reshape(total, D)
    own_flat = own_grad.reshape(total, 2 * D)
    later_flat = later_grad.reshape(SHARDS * WIN, 2 * D)
    normed_grad = jnp.dot(query_flat, query_weight.T, preferred_element_type=jnp.float32)
    normed_grad = normed_grad + jnp.dot(own_flat, keyval_weight.T, preferred_element_type=jnp.float32)
    tail = jnp.dot(later_flat, keyval_weight.T, preferred_element_type=jnp.float32).reshape(SHARDS, WIN, D)
    normed_grad = normed_grad.reshape(SHARDS, T_DEV, D).at[:, T_DEV - WIN:].add(tail).reshape(total, D)
    centre = lax.optimization_barrier(jnp.mean(normed_grad * normed32, axis=1, keepdims=True))
    frame_grad = (inverse * (normed_grad - normed32 * centre) + out_grad.astype(jnp.float32)).astype(jnp.bfloat16)
    back_ok = (row_frame >= 0) & accepted[jnp.maximum(row_frame, 0)]
    frame_grads = jnp.where(back_ok[:, None], frame_grad[jnp.maximum(row_frame, 0)], jnp.zeros((), jnp.bfloat16))
    tail_normed = normed.reshape(SHARDS, T_DEV, D)[:, T_DEV - WIN:].reshape(SHARDS * WIN, D)
    grad_query = jnp.dot(normed.T, query_flat, preferred_element_type=jnp.float32)
    grad_keyval = jnp.dot(normed.T, own_flat, preferred_element_type=jnp.float32)
    grad_keyval = grad_keyval + jnp.dot(tail_normed.T, later_flat, preferred_element_type=jnp.float32)
    grad_out = jnp.dot(attended.T, out_grad, preferred_element_type=jnp.float32)
    weight_grads = jnp.concatenate([grad_query, grad_keyval, grad_out], axis=1) * SLAB ** (-0.5)
    return (out_frames.reshape(STREAMS, SLAB, D), frame_grads, weight_grads)
```

```python
import math

import jax
import jax.numpy as jnp
from jax import lax
from jax.experimental import pallas as pl
from jax.experimental.pallas import tpu as pltpu
from jax.sharding import PartitionSpec as P

H = 8
WIN = 512
NEG = -1e30
EPS_NORM = 1e-06
AXES = ("stream", "seq")
BF = jnp.bfloat16
F32 = jnp.float32

NN = (((1,), (0,)), ((), ()))
NT = (((1,), (1,)), ((), ()))


def mm(a, b, dims=NN):
    return lax.dot_general(a, b, dims, preferred_element_type=F32)


def iota2(shape, dim):
    return lax.broadcasted_iota(jnp.int32, shape, dim)


def vmem_call(body, outs, args, smem=(), scratch=(), flops=0, limit=32):
    specs = [
        pl.BlockSpec(memory_space=pltpu.SMEM if i in smem else pltpu.VMEM)
        for i in range(len(args))
    ]
    size = sum(math.prod(a.shape) * a.dtype.itemsize for a in list(args) + list(outs))
    return pl.pallas_call(
        body,
        out_shape=tuple(outs),
        in_specs=specs,
        out_specs=tuple(pl.BlockSpec(memory_space=pltpu.VMEM) for _ in outs),
        scratch_shapes=list(scratch),
        compiler_params=pltpu.CompilerParams(vmem_limit_bytes=limit * 2**20),
        cost_estimate=pl.CostEstimate(flops=flops, bytes_accessed=size, transcendentals=0),
    )(*args)


def sds(shape, dtype=BF):
    return jax.ShapeDtypeStruct(shape, dtype)


def outgoing_body(span, slots, rf_ref, rows_ref, out_ref, placing_ref):
    count = rf_ref.shape[1]
    total = out_ref.shape[0]
    rf = rf_ref[...]
    target = jnp.where(rf >= 0, lax.div(rf, span), 1 << 20)
    slot = iota2((total, count), 0)
    owner = lax.div(slot, slots)
    rank = slot - owner * slots
    start = jnp.sum(jnp.where(target < owner, 1.0, 0.0), axis=1, keepdims=True)
    here = iota2((total, count), 1) - start.astype(jnp.int32)
    placing = jnp.where((target == owner) & (here == rank), 1.0, 0.0).astype(BF)
    placing_ref[...] = placing
    out_ref[...] = mm(placing, rows_ref[...]).astype(BF)


def early_body(
    slots, owner_ref, placing_ref, cot_ref, wo_ref, pick_ref, pick_t_ref, placing_t_ref, do_ref, dot_ref
):
    span, lanes = owner_ref.shape[0], 128
    total = pick_ref.shape[1]
    owner = owner_ref[...]
    device = iota2((span, lanes), 1)
    hot = jnp.where(owner == device, 1.0, 0.0)
    strict = jnp.where(iota2((span, span), 1) < iota2((span, span), 0), 1.0, 0.0).astype(BF)
    before = mm(strict, hot.astype(BF))
    slot = jnp.sum(hot * (before + (device * slots).astype(F32)), axis=1, keepdims=True)
    slot = jnp.where(owner >= 0, slot.astype(jnp.int32), -1)
    pick = jnp.where(iota2((span, total), 1) == slot, 1.0, 0.0)
    pick_ref[...] = pick.astype(BF)
    pick_t_ref[...] = pick.T.astype(BF)
    placing_t_ref[...] = placing_ref[...].T
    grad = mm(cot_ref[...], wo_ref[...], NT).astype(BF)
    do_ref[...] = grad
    dot_ref[...] = grad.T


def unit_frames(frames):
    frames32 = frames.astype(F32)
    inverse = lax.rsqrt(jnp.mean(frames32 * frames32, axis=1, keepdims=True) + EPS_NORM)
    return frames32, inverse, frames32 * inverse


def frames_body(pick_ref, in_ref, frames_ref, normed_ref):
    frames = mm(pick_ref[...], in_ref[...]).astype(BF)
    frames_ref[...] = frames
    normed_ref[...] = unit_frames(frames)[2].astype(BF)


def project_body(
    query_scale, normed_ref, wq_ref, wk_ref, wv_ref, q_ref, qt_ref, k_ref, kt_ref, v_ref, vt_ref
):
    normed = normed_ref[...]
    q = (mm(normed, wq_ref[...]) * query_scale).astype(BF)
    q_ref[...] = q
    qt_ref[...] = q.T
    k = mm(normed, wk_ref[...]).astype(BF)
    k_ref[...] = k
    kt_ref[...] = k.T
    v = mm(normed, wv_ref[...]).astype(BF)
    v_ref[...] = v
    vt_ref[...] = v.T


def attend_body(
    head_size, meta_ref, halo_ref, wk_ref, wv_ref,
    q_ref, qt_ref, k_ref, kt_ref, v_ref, vt_ref, do_ref, dot_ref,
    ot_ref, dqt_ref, dk_ref, dv_ref, dkh_ref, dvh_ref, back_ref,
    kx, vx, ktx, vtx,
):
    span, width = q_ref.shape
    begin, length = meta_ref[0], meta_ref[1]
    halo = halo_ref[...]
    kh = mm(halo, wk_ref[...]).astype(BF)
    kx[:WIN] = kh
    ktx[:, :WIN] = kh.T
    vh = mm(halo, wv_ref[...]).astype(BF)
    vx[:WIN] = vh
    vtx[:, :WIN] = vh.T
    kx[WIN:] = k_ref[...]
    vx[WIN:] = v_ref[...]
    ktx[:, WIN:] = kt_ref[...]
    vtx[:, WIN:] = vt_ref[...]

    block, tile, pair = 256, 128, 2 * head_size
    reach = WIN + block
    row = iota2((tile, tile), 0)
    col = iota2((tile, tile), 1)
    halo_bias = jnp.where(begin == 0, NEG, 0.0)
    lane = iota2((block, pair), 1)
    zeros_half = jnp.zeros((head_size, block), BF)
    zero_tile = jnp.zeros((tile, tile), BF)

    def one_pair(p, carry):
        cols = pl.ds(pl.multiple_of(p * pair, pair), pair)
        dks, dvs = [], []
        for b in range(span // block):
            first = b * block
            keys = kx[first : first + reach, cols]
            vals = vx[first : first + reach, cols]
            queries = q_ref[first : first + block, cols]
            grads = do_ref[first : first + block, cols]
            dk_block = dv_block = None
            for h in range(2):
                feats = pl.ds(pl.multiple_of(p * pair + h * head_size, head_size), head_size)
                halves = [zeros_half, zeros_half]
                halves[h] = qt_ref[feats, first : first + block]
                scores = mm(keys, jnp.concatenate(halves, axis=0))
                halves[h] = dot_ref[feats, first : first + block]
                slopes = mm(vals, jnp.concatenate(halves, axis=0))
                prob_cols, grad_cols = [], []
                for a in range(block // tile):
                    at = slice(a * tile, (a + 1) * tile)
                    count = WIN // tile + 1
                    parts = []
                    for n in range(count):
                        low = a * tile + n * tile
                        part = scores[low : low + tile, at]
                        if n == 0:
                            part = jnp.where(row > col, part, NEG)
                        if n == count - 1:
                            part = jnp.where(row <= col, part, NEG)
                        elif first + low < WIN:
                            part = part + halo_bias
                        parts.append(part)
                    peak = parts[0]
                    for part in parts[1:]:
                        peak = jnp.maximum(peak, part)
                    peak = jnp.max(peak, axis=0, keepdims=True)
                    parts = [jnp.exp2(part - peak) for part in parts]
                    denom = parts[0]
                    for part in parts[1:]:
                        denom = denom + part
                    denom = jnp.sum(denom, axis=0, keepdims=True)
                    time = begin + first + a * tile + iota2((1, tile), 1)
                    scale = jnp.where(time < length, 1.0 / denom, 0.0)
                    parts = [part * scale for part in parts]
                    moved = [
                        part * slopes[(a + n) * tile : (a + n + 1) * tile, at]
                        for n, part in enumerate(parts)
                    ]
                    centre = moved[0]
                    for part in moved[1:]:
                        centre = centre + part
                    centre = jnp.sum(centre, axis=0, keepdims=True)
                    low_parts = [part.astype(BF) for part in parts]
                    grad_parts = [
                        (move - part * centre).astype(BF) for part, move in zip(parts, moved)
                    ]
                    before = [zero_tile] * a
                    after = [zero_tile] * (block // tile - 1 - a)
                    prob_cols.append(jnp.concatenate(before + low_parts + after, axis=0))
                    grad_cols.append(jnp.concatenate(before + grad_parts + after, axis=0))
                probs = jnp.concatenate(prob_cols, axis=1)
                score_grad = jnp.concatenate(grad_cols, axis=1)
                span_keys = slice(first, first + reach)
                ot_ref[feats, first : first + block] = mm(vtx[feats, span_keys], probs).astype(BF)
                dqt_ref[feats, first : first + block] = (
                    mm(ktx[feats, span_keys], score_grad) * head_size ** (-0.5)
                ).astype(BF)
                mine = (lane >= h * head_size) & (lane < (h + 1) * head_size)
                zero = jnp.zeros((), BF)
                dk_part = mm(score_grad, jnp.where(mine, queries, zero))
                dv_part = mm(probs, jnp.where(mine, grads, zero))
                dk_block = dk_part if dk_block is None else dk_block + dk_part
                dv_block = dv_part if dv_block is None else dv_block + dv_part
            dks.append(dk_block)
            dvs.append(dv_block)
        for parts, scale, far_ref, near_ref in (
            (dks, math.log(2.0), dkh_ref, dk_ref),
            (dvs, 1.0, dvh_ref, dv_ref),
        ):
            for low in range(0, WIN + span, block):
                total = None
                for b, part in enumerate(parts):
                    at = low - b * block
                    if 0 <= at < reach:
                        piece = part[at : at + block]
                        total = piece if total is None else total + piece
                total = (total * scale).astype(BF)
                if low < WIN:
                    far_ref[low : low + block, cols] = total
                else:
                    near_ref[low - WIN : low - WIN + block, cols] = total
        return carry

    lax.fori_loop(0, width // pair, one_pair, 0)
    back_ref[...] = (mm(dkh_ref[...], wk_ref[...], NT) + mm(dvh_ref[...], wv_ref[...], NT)).astype(BF)


def weights_body(
    scale, normed_ref, halo_ref, frames_ref, cot_ref, wq_ref, wk_ref, wv_ref, wo_ref,
    ot_ref, dqt_ref, dk_ref, dv_ref, dkh_ref, dvh_ref,
    sums_ref, out_ref, slope_ref,
):
    width = wq_ref.shape[0]
    normed_t = normed_ref[...].T
    halo_t = halo_ref[...].T
    sums_ref[:, :width] = (mm(normed_t, dqt_ref[...], NT) * scale).astype(BF)
    own = mm(normed_t, dk_ref[...]) + mm(halo_t, dkh_ref[...])
    sums_ref[:, width : 2 * width] = (own * scale).astype(BF)
    own = mm(normed_t, dv_ref[...]) + mm(halo_t, dvh_ref[...])
    sums_ref[:, 2 * width : 3 * width] = (own * scale).astype(BF)
    sums_ref[:, 3 * width :] = (mm(ot_ref[...], cot_ref[...]) * scale).astype(BF)
    slope = mm(dqt_ref[...].T, wq_ref[...], NT)
    slope = slope + mm(dk_ref[...], wk_ref[...], NT)
    slope_ref[...] = slope + mm(dv_ref[...], wv_ref[...], NT)
    out = mm(ot_ref[...].T, wo_ref[...]) + frames_ref[...].astype(F32)
    out_ref[...] = out.astype(BF)


def returning_body(frames_ref, slope_ref, extra_ref, cot_ref, pick_t_ref, out_ref):
    _, inverse, normed32 = unit_frames(frames_ref[...])
    slope = slope_ref[...] + extra_ref[...].astype(F32)
    centre = jnp.mean(slope * normed32, axis=1, keepdims=True)
    grad = inverse * (slope - normed32 * centre) + cot_ref[...].astype(F32)
    out_ref[...] = mm(pick_t_ref[...], grad.astype(BF)).astype(BF)


def arrived_body(placing_t_ref, in_ref, out_ref):
    out_ref[...] = mm(placing_t_ref[...], in_ref[...]).astype(BF)


def passed_along(shard, by):
    devices = lax.axis_size("seq")
    pairs = [(i, i + by) for i in range(devices) if 0 <= i + by < devices]
    return lax.ppermute(shard, "seq", pairs)


def swap(shard, bit):
    devices = lax.axis_size(AXES)
    return lax.ppermute(shard, AXES, [(i, i ^ bit) for i in range(devices)])


def halve(sums, place, bits, bit):
    dim = bits.index(bit)
    mine = (place >> (bit.bit_length() - 1)) & 1
    keep = lax.dynamic_index_in_dim(sums, mine, dim, keepdims=False)
    send = lax.dynamic_index_in_dim(sums, 1 - mine, dim, keepdims=False)
    return keep, swap(send, bit), bits[:dim] + bits[dim + 1 :]


def scatter_sums(sums):
    devices = lax.axis_size(AXES)
    place = lax.axis_index(AXES)
    rows, columns = sums.shape
    bits = [1 << n for n in reversed(range(devices.bit_length() - 1))]
    sums = sums.reshape([2] * len(bits) + [rows // devices, columns])
    keep, got, left = halve(sums, place, bits, 1)
    half = columns // 2
    lanes = []
    for lane in range(2):
        at = slice(lane * half, (lane + 1) * half)
        order = list(left)
        if lane:
            order[0], order[1] = order[1], order[0]
        lanes.append([keep[..., at], got[..., at], left, order])
    while lanes[0][3]:
        for lane in lanes:
            keep, got, left, order = lane
            total = (keep.astype(F32) + got.astype(F32)).astype(BF)
            lane[:3] = halve(total, place, left, order[0])
            lane[3] = order[1:]
    parts = [keep.astype(F32) + got.astype(F32) for keep, got, _, _ in lanes]
    return jnp.concatenate(parts, axis=1)


def shards(
    frame_rows, row_frame, frame_owner, lengths,
    query_weight, key_weight, value_weight, out_weight, cotangent,
):
    devices = lax.axis_size(AXES)
    row_count, width = frame_rows.shape
    span = frame_owner.shape[1]
    slots = row_count // devices
    slab = span * lax.axis_size("seq")
    head_size = width // H
    cube = 2 * span * width * width
    square = sds((span, width))
    begin = (lax.axis_index("seq") * span).astype(jnp.int32)
    meta = jnp.stack([begin, lengths[0]])
    cot = cotangent[0]

    def exchanged(shard):
        got = lax.all_to_all(
            shard.reshape(devices, slots, width), AXES, split_axis=0, concat_axis=0, tiled=True
        )
        return got.reshape(devices * slots, width)

    outgoing, placing = vmem_call(
        lambda *refs: outgoing_body(span, slots, *refs),
        [square, sds((devices * slots, row_count))],
        [row_frame.reshape(1, row_count), frame_rows],
        flops=cube,
    )
    incoming = exchanged(outgoing)
    pick, pick_t, placing_t, do, dot = vmem_call(
        lambda *refs: early_body(slots, *refs),
        [square, square, square, square, sds((width, span))],
        [frame_owner.reshape(span, 1), placing, cot, out_weight],
        flops=2 * cube,
    )
    frames, normed = vmem_call(frames_body, [square, square], [pick, incoming], flops=cube)
    halo = passed_along(normed, 1)
    query_scale = head_size ** (-0.5) * math.log2(math.e)
    q, qt, k, kt, v, vt = vmem_call(
        lambda *refs: project_body(query_scale, *refs),
        [square] * 6,
        [normed, query_weight, key_weight, value_weight],
        flops=3 * cube,
    )
    ot, dqt, dk, dv, dkh, dvh, back = vmem_call(
        lambda *refs: attend_body(head_size, *refs),
        [square] * 7,
        [meta, halo, key_weight, value_weight, q, qt, k, kt, v, vt, do, dot],
        smem=(0,),
        scratch=[
            pltpu.VMEM((WIN + span, width), BF),
            pltpu.VMEM((WIN + span, width), BF),
            pltpu.VMEM((width, WIN + span), BF),
            pltpu.VMEM((width, WIN + span), BF),
        ],
        flops=20 * cube,
        limit=40,
    )
    extra = passed_along(back, -1)
    sums, out_frames, slope = vmem_call(
        lambda *refs: weights_body(slab ** (-0.5), *refs),
        [sds((width, 4 * width)), square, sds((span, width), F32)],
        [normed, halo, frames, cot, query_weight, key_weight, value_weight, out_weight,
         ot, dqt, dk, dv, dkh, dvh],
        flops=10 * cube,
    )
    returning, = vmem_call(
        returning_body, [square], [frames, slope, extra, cot, pick_t], flops=cube
    )
    arrived = exchanged(returning)
    frame_grads, = vmem_call(arrived_body, [square], [placing_t, arrived], flops=cube)
    weight_grads = scatter_sums(sums)
    return (out_frames[None], frame_grads, weight_grads)


def solution(mesh):
    return jax.shard_map(
        shards,
        mesh=mesh,
        in_specs=(
            P(AXES, None), P(AXES), P("stream", "seq"), P("stream"),
            P(), P(), P(), P(), P("stream", "seq", None),
        ),
        out_specs=(P("stream", "seq", None), P(AXES, None), P(AXES, None)),
        check_vma=False,
    )
```

```python
import math

import jax
import jax.numpy as jnp
from jax import lax
from jax.experimental import pallas as pl
from jax.experimental.pallas import tpu as pltpu
from jax.sharding import PartitionSpec as P

H = 8
WIN = 512
NEG = -1e30
EPS_NORM = 1e-06
AXES = ("stream", "seq")
BF = jnp.bfloat16
F32 = jnp.float32

NN = (((1,), (0,)), ((), ()))
NT = (((1,), (1,)), ((), ()))


def mm(a, b, dims=NN):
    return lax.dot_general(a, b, dims, preferred_element_type=F32)


def iota2(shape, dim):
    return lax.broadcasted_iota(jnp.int32, shape, dim)


def vmem_call(body, outs, args, smem=(), scratch=(), flops=0, limit=12):
    specs = [
        pl.BlockSpec(memory_space=pltpu.SMEM if i in smem else pltpu.VMEM)
        for i in range(len(args))
    ]
    size = sum(math.prod(a.shape) * a.dtype.itemsize for a in list(args) + list(outs))
    return pl.pallas_call(
        body,
        out_shape=tuple(outs),
        in_specs=specs,
        out_specs=tuple(pl.BlockSpec(memory_space=pltpu.VMEM) for _ in outs),
        scratch_shapes=list(scratch),
        compiler_params=pltpu.CompilerParams(vmem_limit_bytes=limit * 2**20),
        cost_estimate=pl.CostEstimate(flops=flops, bytes_accessed=size, transcendentals=0),
    )(*args)


def sds(shape, dtype=BF):
    return jax.ShapeDtypeStruct(shape, dtype)


def outgoing_body(span, slots, rf_ref, rows_ref, out_ref, placing_ref):
    count = rf_ref.shape[1]
    total = out_ref.shape[0]
    rf = rf_ref[...]
    target = jnp.where(rf >= 0, lax.div(rf, span), 1 << 20)
    slot = iota2((total, count), 0)
    owner = lax.div(slot, slots)
    rank = slot - owner * slots
    start = jnp.sum(jnp.where(target < owner, 1.0, 0.0), axis=1, keepdims=True)
    here = iota2((total, count), 1) - start.astype(jnp.int32)
    placing = jnp.where((target == owner) & (here == rank), 1.0, 0.0).astype(BF)
    placing_ref[...] = placing
    out_ref[...] = mm(placing, rows_ref[...]).astype(BF)


def early_body(
    slots, owner_ref, placing_ref, cot_ref, wo_ref, pick_ref, pick_t_ref, placing_t_ref, do_ref, dot_ref
):
    span, lanes = owner_ref.shape[0], 128
    total = pick_ref.shape[1]
    owner = owner_ref[...]
    device = iota2((span, lanes), 1)
    hot = jnp.where(owner == device, 1.0, 0.0)
    strict = jnp.where(iota2((span, span), 1) < iota2((span, span), 0), 1.0, 0.0).astype(BF)
    before = mm(strict, hot.astype(BF))
    slot = jnp.sum(hot * (before + (device * slots).astype(F32)), axis=1, keepdims=True)
    slot = jnp.where(owner >= 0, slot.astype(jnp.int32), -1)
    pick = jnp.where(iota2((span, total), 1) == slot, 1.0, 0.0)
    pick_ref[...] = pick.astype(BF)
    pick_t_ref[...] = pick.T.astype(BF)
    placing_t_ref[...] = placing_ref[...].T
    grad = mm(cot_ref[...], wo_ref[...], NT).astype(BF)
    do_ref[...] = grad
    dot_ref[...] = grad.T


def unit_frames(frames):
    frames32 = frames.astype(F32)
    inverse = lax.rsqrt(jnp.mean(frames32 * frames32, axis=1, keepdims=True) + EPS_NORM)
    return frames32, inverse, frames32 * inverse


def frames_body(pick_ref, in_ref, frames_ref, normed_ref):
    frames = mm(pick_ref[...], in_ref[...]).astype(BF)
    frames_ref[...] = frames
    normed_ref[...] = unit_frames(frames)[2].astype(BF)


def project_body(
    query_scale, normed_ref, wq_ref, wk_ref, wv_ref, q_ref, qt_ref, k_ref, kt_ref, v_ref, vt_ref
):
    normed = normed_ref[...]
    q = (mm(normed, wq_ref[...]) * query_scale).astype(BF)
    q_ref[...] = q
    qt_ref[...] = q.T
    k = mm(normed, wk_ref[...]).astype(BF)
    k_ref[...] = k
    kt_ref[...] = k.T
    v = mm(normed, wv_ref[...]).astype(BF)
    v_ref[...] = v
    vt_ref[...] = v.T


def attend_body(
    head_size, meta_ref, halo_ref, wk_ref, wv_ref,
    q_ref, qt_ref, k_ref, kt_ref, v_ref, vt_ref, do_ref, dot_ref,
    ot_ref, dqt_ref, dk_ref, dv_ref, dkh_ref, dvh_ref, back_ref,
    kx, vx, ktx, vtx,
):
    span, width = q_ref.shape
    begin, length = meta_ref[0], meta_ref[1]
    halo = halo_ref[...]
    kh = mm(halo, wk_ref[...]).astype(BF)
    kx[:WIN] = kh
    ktx[:, :WIN] = kh.T
    vh = mm(halo, wv_ref[...]).astype(BF)
    vx[:WIN] = vh
    vtx[:, :WIN] = vh.T
    kx[WIN:] = k_ref[...]
    vx[WIN:] = v_ref[...]
    ktx[:, WIN:] = kt_ref[...]
    vtx[:, WIN:] = vt_ref[...]

    block, tile, pair = 256, 128, 2 * head_size
    reach = WIN + block
    row = iota2((tile, tile), 0)
    col = iota2((tile, tile), 1)
    halo_bias = jnp.where(begin == 0, NEG, 0.0)
    lane = iota2((block, pair), 1)
    zeros_half = jnp.zeros((head_size, block), BF)
    zero_tile = jnp.zeros((tile, tile), BF)

    def one_pair(p, carry):
        cols = pl.ds(pl.multiple_of(p * pair, pair), pair)
        dks, dvs = [], []
        for b in range(span // block):
            first = b * block
            keys = kx[first : first + reach, cols]
            vals = vx[first : first + reach, cols]
            queries = q_ref[first : first + block, cols]
            grads = do_ref[first : first + block, cols]
            dk_block = dv_block = None
            for h in range(2):
                feats = pl.ds(pl.multiple_of(p * pair + h * head_size, head_size), head_size)
                halves = [zeros_half, zeros_half]
                halves[h] = qt_ref[feats, first : first + block]
                scores = mm(keys, jnp.concatenate(halves, axis=0))
                halves[h] = dot_ref[feats, first : first + block]
                slopes = mm(vals, jnp.concatenate(halves, axis=0))
                prob_cols, grad_cols = [], []
                for a in range(block // tile):
                    at = slice(a * tile, (a + 1) * tile)
                    count = WIN // tile + 1
                    parts = []
                    for n in range(count):
                        low = a * tile + n * tile
                        part = scores[low : low + tile, at]
                        if n == 0:
                            part = jnp.where(row > col, part, NEG)
                        if n == count - 1:
                            part = jnp.where(row <= col, part, NEG)
                        elif first + low < WIN:
                            part = part + halo_bias
                        parts.append(part)
                    peak = parts[0]
                    for part in parts[1:]:
                        peak = jnp.maximum(peak, part)
                    peak = jnp.max(peak, axis=0, keepdims=True)
                    parts = [jnp.exp2(part - peak) for part in parts]
                    denom = parts[0]
                    for part in parts[1:]:
                        denom = denom + part
                    denom = jnp.sum(denom, axis=0, keepdims=True)
                    time = begin + first + a * tile + iota2((1, tile), 1)
                    scale = jnp.where(time < length, 1.0 / denom, 0.0)
                    parts = [part * scale for part in parts]
                    moved = [
                        part * slopes[(a + n) * tile : (a + n + 1) * tile, at]
                        for n, part in enumerate(parts)
                    ]
                    centre = moved[0]
                    for part in moved[1:]:
                        centre = centre + part
                    centre = jnp.sum(centre, axis=0, keepdims=True)
                    low_parts = [part.astype(BF) for part in parts]
                    grad_parts = [
                        (move - part * centre).astype(BF) for part, move in zip(parts, moved)
                    ]
                    before = [zero_tile] * a
                    after = [zero_tile] * (block // tile - 1 - a)
                    prob_cols.append(jnp.concatenate(before + low_parts + after, axis=0))
                    grad_cols.append(jnp.concatenate(before + grad_parts + after, axis=0))
                probs = jnp.concatenate(prob_cols, axis=1)
                score_grad = jnp.concatenate(grad_cols, axis=1)
                span_keys = slice(first, first + reach)
                ot_ref[feats, first : first + block] = mm(vtx[feats, span_keys], probs).astype(BF)
                dqt_ref[feats, first : first + block] = (
                    mm(ktx[feats, span_keys], score_grad) * head_size ** (-0.5)
                ).astype(BF)
                mine = (lane >= h * head_size) & (lane < (h + 1) * head_size)
                zero = jnp.zeros((), BF)
                dk_part = mm(score_grad, jnp.where(mine, queries, zero))
                dv_part = mm(probs, jnp.where(mine, grads, zero))
                dk_block = dk_part if dk_block is None else dk_block + dk_part
                dv_block = dv_part if dv_block is None else dv_block + dv_part
            dks.append(dk_block)
            dvs.append(dv_block)
        for parts, scale, far_ref, near_ref in (
            (dks, math.log(2.0), dkh_ref, dk_ref),
            (dvs, 1.0, dvh_ref, dv_ref),
        ):
            for low in range(0, WIN + span, block):
                total = None
                for b, part in enumerate(parts):
                    at = low - b * block
                    if 0 <= at < reach:
                        piece = part[at : at + block]
                        total = piece if total is None else total + piece
                total = (total * scale).astype(BF)
                if low < WIN:
                    far_ref[low : low + block, cols] = total
                else:
                    near_ref[low - WIN : low - WIN + block, cols] = total
        return carry

    lax.fori_loop(0, width // pair, one_pair, 0)
    back_ref[...] = (mm(dkh_ref[...], wk_ref[...], NT) + mm(dvh_ref[...], wv_ref[...], NT)).astype(BF)


def weights_body(
    scale, rows, meta_ref, normed_ref, halo_ref, frames_ref, cot_ref, wq_ref, wk_ref, wv_ref, wo_ref,
    ot_ref, dqt_ref, dk_ref, dv_ref, dkh_ref, dvh_ref,
    keep_ref, send_ref, out_ref, slope_ref,
    normed_t, halo_t, mixed_t,
):
    width, span = ot_ref.shape
    chunks = width // (2 * rows)
    split = (chunks, 2, rows, span)
    normed_t[...] = normed_ref[...].T.reshape(split)
    halo_t[...] = halo_ref[...].T.reshape(split)
    mixed_t[...] = ot_ref[...].reshape(split)
    mine = meta_ref[2]
    for side, out in ((1 - mine, send_ref), (mine, keep_ref)):
        own = normed_t[:, side].reshape(width // 2, span)
        far = halo_t[:, side].reshape(width // 2, span)
        mixed = mixed_t[:, side].reshape(width // 2, span)
        for n, total in enumerate((
            mm(own, dqt_ref[...], NT),
            mm(own, dk_ref[...]) + mm(far, dkh_ref[...]),
            mm(own, dv_ref[...]) + mm(far, dvh_ref[...]),
            mm(mixed, cot_ref[...]),
        )):
            out[:, n * width : (n + 1) * width] = (total * scale).astype(BF)
    slope = mm(dqt_ref[...].T, wq_ref[...], NT)
    slope = slope + mm(dk_ref[...], wk_ref[...], NT)
    slope_ref[...] = slope + mm(dv_ref[...], wv_ref[...], NT)
    out = mm(ot_ref[...].T, wo_ref[...]) + frames_ref[...].astype(F32)
    out_ref[...] = out.astype(BF)


def returning_body(frames_ref, slope_ref, extra_ref, cot_ref, pick_t_ref, out_ref):
    _, inverse, normed32 = unit_frames(frames_ref[...])
    slope = slope_ref[...] + extra_ref[...].astype(F32)
    centre = jnp.mean(slope * normed32, axis=1, keepdims=True)
    grad = inverse * (slope - normed32 * centre) + cot_ref[...].astype(F32)
    out_ref[...] = mm(pick_t_ref[...], grad.astype(BF)).astype(BF)


def arrived_body(placing_t_ref, in_ref, out_ref):
    out_ref[...] = mm(placing_t_ref[...], in_ref[...]).astype(BF)


def passed_along(shard, by):
    devices = lax.axis_size("seq")
    pairs = [(i, i + by) for i in range(devices) if 0 <= i + by < devices]
    return lax.ppermute(shard, "seq", pairs)


def summed(shard, axis, groups=None):
    got = lax.all_to_all(
        shard, axis, split_axis=0, concat_axis=0, axis_index_groups=groups, tiled=True
    )
    return jnp.sum(got.astype(F32), axis=0)


def scatter_sums(keep, send):
    devices, seqs = lax.axis_size(AXES), lax.axis_size("seq")
    streams, chips = devices // seqs, seqs // 2
    columns = keep.shape[1]
    rows = keep.shape[0] // (streams * chips)
    got = lax.ppermute(send, "seq", [(i, i ^ 1) for i in range(seqs)])
    total = (keep.astype(F32) + got.astype(F32)).astype(BF)
    total = summed(total.reshape(streams, chips * rows, columns), "stream").astype(BF)
    groups = [list(range(core, seqs, 2)) for core in range(2)]
    return summed(total.reshape(chips, rows, columns), "seq", groups)


def shards(
    frame_rows, row_frame, frame_owner, lengths,
    query_weight, key_weight, value_weight, out_weight, cotangent,
):
    devices = lax.axis_size(AXES)
    row_count, width = frame_rows.shape
    span = frame_owner.shape[1]
    slots = row_count // devices
    slab = span * lax.axis_size("seq")
    head_size = width // H
    cube = 2 * span * width * width
    square = sds((span, width))
    begin = (lax.axis_index("seq") * span).astype(jnp.int32)
    rows = width // devices
    in_kernel = rows % 16 == 0
    core = (lax.axis_index("seq") & 1).astype(jnp.int32)
    meta = jnp.stack([begin, lengths[0], core if in_kernel else jnp.zeros((), jnp.int32)])
    cot = cotangent[0]

    def exchanged(shard):
        got = lax.all_to_all(
            shard.reshape(devices, slots, width), AXES, split_axis=0, concat_axis=0, tiled=True
        )
        return got.reshape(devices * slots, width)

    outgoing, placing = vmem_call(
        lambda *refs: outgoing_body(span, slots, *refs),
        [square, sds((devices * slots, row_count))],
        [row_frame.reshape(1, row_count), frame_rows],
        flops=cube,
    )
    incoming = exchanged(outgoing)
    pick, pick_t, placing_t, do, dot = vmem_call(
        lambda *refs: early_body(slots, *refs),
        [square, square, square, square, sds((width, span))],
        [frame_owner.reshape(span, 1), placing, cot, out_weight],
        flops=2 * cube,
    )
    frames, normed = vmem_call(frames_body, [square, square], [pick, incoming], flops=cube)
    halo = passed_along(normed, 1)
    query_scale = head_size ** (-0.5) * math.log2(math.e)
    q, qt, k, kt, v, vt = vmem_call(
        lambda *refs: project_body(query_scale, *refs),
        [square] * 6,
        [normed, query_weight, key_weight, value_weight],
        flops=3 * cube,
    )
    ot, dqt, dk, dv, dkh, dvh, back = vmem_call(
        lambda *refs: attend_body(head_size, *refs),
        [square] * 7,
        [meta, halo, key_weight, value_weight, q, qt, k, kt, v, vt, do, dot],
        smem=(0,),
        scratch=[
            pltpu.VMEM((WIN + span, width), BF),
            pltpu.VMEM((WIN + span, width), BF),
            pltpu.VMEM((width, WIN + span), BF),
            pltpu.VMEM((width, WIN + span), BF),
        ],
        flops=20 * cube,
        limit=22,
    )
    extra = passed_along(back, -1)
    chunk = rows if in_kernel else width // 2
    split = pltpu.VMEM((width // (2 * chunk), 2, chunk, span), BF)
    half = sds((width // 2, 4 * width))
    keep, send, out_frames, slope = vmem_call(
        lambda *refs: weights_body(slab ** (-0.5), chunk, *refs),
        [half, half, square, sds((span, width), F32)],
        [meta, normed, halo, frames, cot, query_weight, key_weight, value_weight, out_weight,
         ot, dqt, dk, dv, dkh, dvh],
        smem=(0,),
        scratch=[split, split, split],
        flops=10 * cube,
        limit=20,
    )
    send, extra = lax.optimization_barrier((send, extra))
    if not in_kernel:
        sums = jnp.concatenate([keep, send], axis=0).reshape(-1, 2, rows, 4 * width)
        keep = lax.dynamic_index_in_dim(sums, core, 1, keepdims=False).reshape(half.shape)
        send = lax.dynamic_index_in_dim(sums, 1 - core, 1, keepdims=False).reshape(half.shape)
    returning, = vmem_call(
        returning_body, [square], [frames, slope, extra, cot, pick_t], flops=cube
    )
    arrived = exchanged(returning)
    frame_grads, = vmem_call(arrived_body, [square], [placing_t, arrived], flops=cube)
    weight_grads = scatter_sums(keep, send)
    return (out_frames[None], frame_grads, weight_grads)


def solution(mesh):
    return jax.shard_map(
        shards,
        mesh=mesh,
        in_specs=(
            P(AXES, None), P(AXES), P("stream", "seq"), P("stream"),
            P(), P(), P(), P(), P("stream", "seq", None),
        ),
        out_specs=(P("stream", "seq", None), P(AXES, None), P(AXES, None)),
        check_vma=False,
    )
```

```python
import math

import jax
import jax.numpy as jnp
from jax import lax
from jax.experimental import pallas as pl
from jax.experimental.pallas import tpu as pltpu
from jax.sharding import PartitionSpec as P

H = 8
WIN = 512
NEG = -1e30
EPS_NORM = 1e-06
AXES = ("stream", "seq")
BF = jnp.bfloat16
F32 = jnp.float32

NN = (((1,), (0,)), ((), ()))
NT = (((1,), (1,)), ((), ()))


def mm(a, b, dims=NN):
    return lax.dot_general(a, b, dims, preferred_element_type=F32)


def iota2(shape, dim):
    return lax.broadcasted_iota(jnp.int32, shape, dim)


def vmem_call(body, outs, args, smem=(), hbm=(), scratch=(), flops=0, limit=12):
    spaces = [pltpu.SMEM if i in smem else pltpu.HBM if i in hbm else pltpu.VMEM for i in range(len(args))]
    size = sum(math.prod(a.shape) * a.dtype.itemsize for a in list(args) + list(outs))
    return pl.pallas_call(
        body,
        out_shape=tuple(outs),
        in_specs=[pl.BlockSpec(memory_space=space) for space in spaces],
        out_specs=tuple(pl.BlockSpec(memory_space=pltpu.VMEM) for _ in outs),
        scratch_shapes=list(scratch),
        compiler_params=pltpu.CompilerParams(vmem_limit_bytes=limit * 2**20),
        cost_estimate=pl.CostEstimate(flops=flops, bytes_accessed=size, transcendentals=0),
    )(*args)


def fetch(sources, targets, sems):
    copies = [
        pltpu.make_async_copy(source, target, sems.at[n])
        for n, (source, target) in enumerate(zip(sources, targets))
    ]
    for copy in copies:
        copy.start()
    return copies


def sds(shape, dtype=BF):
    return jax.ShapeDtypeStruct(shape, dtype)


def outgoing_body(span, slots, rf_ref, rows_hbm, out_ref, placing_ref, rows_ref, sems):
    (rows_copy,) = fetch([rows_hbm], [rows_ref], sems)
    count = rf_ref.shape[1]
    total = out_ref.shape[0]
    rf = rf_ref[...]
    target = jnp.where(rf >= 0, lax.div(rf, span), 1 << 20)
    slot = iota2((total, count), 0)
    owner = lax.div(slot, slots)
    rank = slot - owner * slots
    start = jnp.sum(jnp.where(target < owner, 1.0, 0.0), axis=1, keepdims=True)
    here = iota2((total, count), 1) - start.astype(jnp.int32)
    placing = jnp.where((target == owner) & (here == rank), 1.0, 0.0).astype(BF)
    placing_ref[...] = placing
    rows_copy.wait()
    out_ref[...] = mm(placing, rows_ref[...]).astype(BF)


def early_body(
    slots, owner_ref, placing_ref, cot_ref, wo_ref, pick_ref, pick_t_ref, placing_t_ref, do_ref, dot_ref
):
    span, lanes = owner_ref.shape[0], 128
    total = pick_ref.shape[1]
    owner = owner_ref[...]
    device = iota2((span, lanes), 1)
    hot = jnp.where(owner == device, 1.0, 0.0)
    strict = jnp.where(iota2((span, span), 1) < iota2((span, span), 0), 1.0, 0.0).astype(BF)
    before = mm(strict, hot.astype(BF))
    slot = jnp.sum(hot * (before + (device * slots).astype(F32)), axis=1, keepdims=True)
    slot = jnp.where(owner >= 0, slot.astype(jnp.int32), -1)
    pick = jnp.where(iota2((span, total), 1) == slot, 1.0, 0.0)
    pick_ref[...] = pick.astype(BF)
    pick_t_ref[...] = pick.T.astype(BF)
    placing_t_ref[...] = placing_ref[...].T
    grad = mm(cot_ref[...], wo_ref[...], NT).astype(BF)
    do_ref[...] = grad
    dot_ref[...] = grad.T


def unit_frames(frames):
    frames32 = frames.astype(F32)
    inverse = lax.rsqrt(jnp.mean(frames32 * frames32, axis=1, keepdims=True) + EPS_NORM)
    return frames32, inverse, frames32 * inverse


def frames_body(pick_ref, in_ref, frames_ref, normed_ref):
    frames = mm(pick_ref[...], in_ref[...]).astype(BF)
    frames_ref[...] = frames
    normed_ref[...] = unit_frames(frames)[2].astype(BF)


def project_body(
    query_scale, normed_ref, wq_hbm, wk_hbm, wv_hbm,
    q_ref, qt_ref, k_ref, kt_ref, v_ref, vt_ref, wk_ref, wv_ref, wq_ref, sems,
):
    copies = fetch([wq_hbm, wk_hbm, wv_hbm], [wq_ref, wk_ref, wv_ref], sems)
    normed = normed_ref[...]
    copies[0].wait()
    q = (mm(normed, wq_ref[...]) * query_scale).astype(BF)
    q_ref[...] = q
    qt_ref[...] = q.T
    copies[1].wait()
    k = mm(normed, wk_ref[...]).astype(BF)
    k_ref[...] = k
    kt_ref[...] = k.T
    copies[2].wait()
    v = mm(normed, wv_ref[...]).astype(BF)
    v_ref[...] = v
    vt_ref[...] = v.T


BLOCK = 256
TILE = 128


def softmax_parts(scores, slopes, first, begin, length):
    row = iota2((TILE, TILE), 0)
    col = iota2((TILE, TILE), 1)
    halo_bias = jnp.where(begin == 0, NEG, 0.0)
    zero_tile = jnp.zeros((TILE, TILE), BF)
    count = WIN // TILE + 1
    prob_cols, grad_cols = [], []
    for a in range(BLOCK // TILE):
        at = slice(a * TILE, (a + 1) * TILE)
        parts = []
        for n in range(count):
            low = (a + n) * TILE
            part = scores[low : low + TILE, at]
            if n == 0:
                part = jnp.where(row > col, part, NEG)
            if n == count - 1:
                part = jnp.where(row <= col, part, NEG)
            elif first + low < WIN:
                part = part + halo_bias
            parts.append(part)
        peak = parts[0]
        for part in parts[1:]:
            peak = jnp.maximum(peak, part)
        peak = jnp.max(peak, axis=0, keepdims=True)
        parts = [jnp.exp2(part - peak) for part in parts]
        denom = parts[0]
        for part in parts[1:]:
            denom = denom + part
        denom = jnp.sum(denom, axis=0, keepdims=True)
        time = begin + first + a * TILE + iota2((1, TILE), 1)
        scale = jnp.where(time < length, 1.0 / denom, 0.0)
        parts = [part * scale for part in parts]
        moved = [part * slopes[(a + n) * TILE : (a + n + 1) * TILE, at] for n, part in enumerate(parts)]
        centre = moved[0]
        for part in moved[1:]:
            centre = centre + part
        centre = jnp.sum(centre, axis=0, keepdims=True)
        grads = [(move - part * centre).astype(BF) for part, move in zip(parts, moved)]
        before = [zero_tile] * a
        after = [zero_tile] * (BLOCK // TILE - 1 - a)
        prob_cols.append(jnp.concatenate(before + [part.astype(BF) for part in parts] + after, axis=0))
        grad_cols.append(jnp.concatenate(before + grads + after, axis=0))
    return jnp.concatenate(prob_cols, axis=1), jnp.concatenate(grad_cols, axis=1)


def one_head(value, h, head_size):
    lane = iota2(value.shape, 1)
    mine = (lane >= h * head_size) & (lane < (h + 1) * head_size)
    return jnp.where(mine, value, jnp.zeros((), value.dtype))


def scores_body(
    head_size, meta_ref, halo_ref, wk_ref, wv_ref, q_ref, qt_ref, k_ref, v_ref, do_ref, dot_ref,
    probs_ref, grads_ref, dkh_ref, dvh_ref, khalo_t_ref, vhalo_t_ref, back_ref,
    kx, vx,
):
    span, width = q_ref.shape
    begin, length = meta_ref[0], meta_ref[1]
    halo = halo_ref[...]
    kh = mm(halo, wk_ref[...]).astype(BF)
    kx[:WIN] = kh
    khalo_t_ref[...] = kh.T
    vh = mm(halo, wv_ref[...]).astype(BF)
    vx[:WIN] = vh
    vhalo_t_ref[...] = vh.T
    kx[WIN:] = k_ref[...]
    vx[WIN:] = v_ref[...]

    pair = 2 * head_size
    reach = WIN + BLOCK
    blocks = span // BLOCK
    zeros_half = jnp.zeros((head_size, BLOCK), BF)
    units = [(b, h) for b in range(blocks) for h in range(2)]

    def one_pair(p, carry):
        cols = pl.ds(pl.multiple_of(p * pair, pair), pair)

        def multiply(b, h):
            first = b * BLOCK
            feats = pl.ds(pl.multiple_of(p * pair + h * head_size, head_size), head_size)
            halves = [zeros_half, zeros_half]
            halves[h] = qt_ref[feats, first : first + BLOCK]
            scores = mm(kx[first : first + reach, cols], jnp.concatenate(halves, axis=0))
            halves[h] = dot_ref[feats, first : first + BLOCK]
            slopes = mm(vx[first : first + reach, cols], jnp.concatenate(halves, axis=0))
            return scores, slopes

        totals = {}

        def finish(b, h, probs, grads):
            first = b * BLOCK
            at = (p * 2 + h) * blocks + b
            probs_ref[at] = probs
            grads_ref[at] = grads
            far = WIN - first
            queries = one_head(q_ref[first : first + BLOCK, cols], h, head_size)
            slopes = one_head(do_ref[first : first + BLOCK, cols], h, head_size)
            for name, part in (("k", mm(grads[:far], queries)), ("v", mm(probs[:far], slopes))):
                totals[name, b] = totals[name, b] + part if (name, b) in totals else part

        products = {0: multiply(*units[0])}
        for n, (b, h) in enumerate(units):
            if n + 1 < len(units):
                products[n + 1] = multiply(*units[n + 1])
            probs, grads = softmax_parts(*products.pop(n), b * BLOCK, begin, length)
            finish(b, h, probs, grads)

        for name, scale, out in (("k", math.log(2.0), dkh_ref), ("v", 1.0, dvh_ref)):
            for low in range(0, WIN, BLOCK):
                total = None
                for b in range(blocks):
                    at = low - b * BLOCK
                    if 0 <= at:
                        piece = totals[name, b][at : at + BLOCK]
                        total = piece if total is None else total + piece
                out[low : low + BLOCK, cols] = (total * scale).astype(BF)
        return carry

    lax.fori_loop(0, width // pair, one_pair, 0)
    back_ref[...] = (mm(dkh_ref[...], wk_ref[...], NT) + mm(dvh_ref[...], wv_ref[...], NT)).astype(BF)


def weights_body(
    scale, rows, head_size, meta_ref, normed_ref, halo_ref, frames_ref, cot_ref,
    wq_hbm, wk_hbm, wv_hbm, wo_hbm,
    q_ref, kt_ref, vt_ref, khalo_t_ref, vhalo_t_ref, do_ref, probs_ref, grads_ref, dkh_ref, dvh_ref,
    keep_ref, send_ref, out_ref, slope_ref,
    normed_t, halo_t, mixed_t, ktx, vtx, ot, dqt, dk, dv, wq, wk, wv, wo, sems,
):
    span, width = q_ref.shape
    copies = fetch([wq_hbm, wk_hbm, wv_hbm, wo_hbm], [wq, wk, wv, wo], sems)
    ktx[:, :WIN] = khalo_t_ref[...]
    ktx[:, WIN:] = kt_ref[...]
    vtx[:, :WIN] = vhalo_t_ref[...]
    vtx[:, WIN:] = vt_ref[...]
    pair = 2 * head_size
    reach = WIN + BLOCK
    blocks = span // BLOCK

    def one_pair(p, carry):
        cols = pl.ds(pl.multiple_of(p * pair, pair), pair)
        totals = {}
        for b in range(blocks):
            first = b * BLOCK
            span_keys = slice(first, first + reach)
            for h in range(2):
                feats = pl.ds(pl.multiple_of(p * pair + h * head_size, head_size), head_size)
                at = (p * 2 + h) * blocks + b
                ot[feats, first : first + BLOCK] = mm(vtx[feats, span_keys], probs_ref[at]).astype(BF)
                dqt[feats, first : first + BLOCK] = (
                    mm(ktx[feats, span_keys], grads_ref[at]) * head_size ** (-0.5)
                ).astype(BF)
                queries = one_head(q_ref[first : first + BLOCK, cols], h, head_size)
                slopes = one_head(do_ref[first : first + BLOCK, cols], h, head_size)
                near = slice(WIN - first, reach)
                for name, part in (
                    ("k", mm(grads_ref[at, near], queries)),
                    ("v", mm(probs_ref[at, near], slopes)),
                ):
                    totals[name, b] = totals[name, b] + part if (name, b) in totals else part
        for name, factor, out in (("k", math.log(2.0), dk), ("v", 1.0, dv)):
            for low in range(0, span, BLOCK):
                total = None
                for b in range(blocks):
                    piece = totals[name, b]
                    if low + BLOCK <= piece.shape[0]:
                        piece = piece[low : low + BLOCK]
                        total = piece if total is None else total + piece
                out[low : low + BLOCK, cols] = (total * factor).astype(BF)
        return carry

    lax.fori_loop(0, width // pair, one_pair, 0)

    chunks = width // (2 * rows)
    split = (chunks, 2, rows, span)
    normed_t[...] = normed_ref[...].T.reshape(split)
    halo_t[...] = halo_ref[...].T.reshape(split)
    mixed_t[...] = ot[...].reshape(split)
    mine = meta_ref[2]
    for side, out in ((1 - mine, send_ref), (mine, keep_ref)):
        own = normed_t[:, side].reshape(width // 2, span)
        far = halo_t[:, side].reshape(width // 2, span)
        mixed = mixed_t[:, side].reshape(width // 2, span)
        for n, total in enumerate((
            mm(own, dqt[...], NT),
            mm(own, dk[...]) + mm(far, dkh_ref[...]),
            mm(own, dv[...]) + mm(far, dvh_ref[...]),
            mm(mixed, cot_ref[...]),
        )):
            out[:, n * width : (n + 1) * width] = (total * scale).astype(BF)
    for copy in copies:
        copy.wait()
    slope = mm(dqt[...].T, wq[...], NT)
    slope = slope + mm(dk[...], wk[...], NT)
    slope_ref[...] = slope + mm(dv[...], wv[...], NT)
    out = mm(ot[...].T, wo[...]) + frames_ref[...].astype(F32)
    out_ref[...] = out.astype(BF)


def returning_body(frames_ref, slope_ref, extra_ref, cot_ref, pick_t_ref, out_ref):
    _, inverse, normed32 = unit_frames(frames_ref[...])
    slope = slope_ref[...] + extra_ref[...].astype(F32)
    centre = jnp.mean(slope * normed32, axis=1, keepdims=True)
    grad = inverse * (slope - normed32 * centre) + cot_ref[...].astype(F32)
    out_ref[...] = mm(pick_t_ref[...], grad.astype(BF)).astype(BF)


def arrived_body(placing_t_ref, in_ref, out_ref):
    out_ref[...] = mm(placing_t_ref[...], in_ref[...]).astype(BF)


def passed_along(shard, by):
    devices = lax.axis_size("seq")
    pairs = [(i, i + by) for i in range(devices) if 0 <= i + by < devices]
    return lax.ppermute(shard, "seq", pairs)


def spread_body(place_ref, *refs):
    parts = refs[0].shape[0]
    inputs, outs = refs[:-parts], refs[-parts:]
    for k, out in enumerate(outs):
        at = place_ref[0] ^ k
        total = inputs[0][at].astype(F32)
        for ref in inputs[1:]:
            total = total + ref[at].astype(F32)
        out[...] = total.astype(BF)


def scattered(inputs, place, axis, parts, step):
    columns = inputs[0].shape[-1]
    inputs = [shard.reshape(parts, -1, columns) for shard in inputs]
    piece = sds(inputs[0].shape[1:])
    pieces = vmem_call(
        spread_body, [piece] * parts, [place.reshape(1)] + inputs, smem=(0,)
    )
    count = lax.axis_size(axis)
    return [pieces[0]] + [
        lax.ppermute(pieces[k], axis, [(i, i ^ (k * step)) for i in range(count)])
        for k in range(1, parts)
    ]


def scatter_sums(keep, got):
    seqs, streams = lax.axis_size("seq"), lax.axis_size("stream")
    pieces = scattered([keep, got], lax.axis_index("stream"), "stream", streams, 1)
    pieces = scattered(pieces, lax.axis_index("seq") >> 1, "seq", seqs // 2, 2)
    total = pieces[0].astype(F32)
    for piece in pieces[1:]:
        total = total + piece.astype(F32)
    return total


def shards(
    frame_rows, row_frame, frame_owner, lengths,
    query_weight, key_weight, value_weight, out_weight, cotangent,
):
    devices = lax.axis_size(AXES)
    row_count, width = frame_rows.shape
    span = frame_owner.shape[1]
    slots = row_count // devices
    slab = span * lax.axis_size("seq")
    head_size = width // H
    cube = 2 * span * width * width
    square = sds((span, width))
    begin = (lax.axis_index("seq") * span).astype(jnp.int32)
    rows = width // devices
    in_kernel = rows % 16 == 0
    core = (lax.axis_index("seq") & 1).astype(jnp.int32)
    meta = jnp.stack([begin, lengths[0], core if in_kernel else jnp.zeros((), jnp.int32)])
    cot = cotangent[0]

    def exchanged(shard):
        got = lax.all_to_all(
            shard.reshape(devices, slots, width), AXES, split_axis=0, concat_axis=0, tiled=True
        )
        return got.reshape(devices * slots, width)

    outgoing, placing = vmem_call(
        lambda *refs: outgoing_body(span, slots, *refs),
        [square, sds((devices * slots, row_count))],
        [row_frame.reshape(1, row_count), frame_rows],
        hbm=(1,),
        scratch=[pltpu.VMEM((row_count, width), BF), pltpu.SemaphoreType.DMA((1,))],
        flops=cube,
    )
    incoming = exchanged(outgoing)
    pick, pick_t, placing_t, do, dot = vmem_call(
        lambda *refs: early_body(slots, *refs),
        [square, square, square, square, sds((width, span))],
        [frame_owner.reshape(span, 1), placing, cot, out_weight],
        flops=2 * cube,
    )
    frames, normed = vmem_call(frames_body, [square, square], [pick, incoming], flops=cube)
    halo = passed_along(normed, 1)
    query_scale = head_size ** (-0.5) * math.log2(math.e)
    q, qt, k, kt, v, vt, wk, wv = vmem_call(
        lambda *refs: project_body(query_scale, *refs),
        [square] * 8,
        [normed, query_weight, key_weight, value_weight],
        hbm=(1, 2, 3),
        scratch=[pltpu.VMEM((width, width), BF), pltpu.SemaphoreType.DMA((3,))],
        flops=3 * cube,
    )
    saved = sds((H * (span // BLOCK), WIN + BLOCK, BLOCK))
    probs, grads, dkh, dvh, khalo_t, vhalo_t, back = vmem_call(
        lambda *refs: scores_body(head_size, *refs),
        [saved, saved] + [square] * 5,
        [meta, halo, wk, wv, q, qt, k, v, do, dot],
        smem=(0,),
        scratch=[pltpu.VMEM((WIN + span, width), BF)] * 2,
        flops=12 * cube,
        limit=24,
    )
    extra = passed_along(back, -1)
    chunk = rows if in_kernel else width // 2
    split = pltpu.VMEM((width // (2 * chunk), 2, chunk, span), BF)
    whole = pltpu.VMEM((width, width), BF)
    half = sds((width // 2, 4 * width))
    keep, send, out_frames, slope = vmem_call(
        lambda *refs: weights_body(slab ** (-0.5), chunk, head_size, *refs),
        [half, half, square, sds((span, width), F32)],
        [meta, normed, halo, frames, cot, query_weight, key_weight, value_weight, out_weight,
         q, kt, vt, khalo_t, vhalo_t, do, probs, grads, dkh, dvh],
        smem=(0,),
        hbm=(5, 6, 7, 8),
        scratch=[split] * 3 + [pltpu.VMEM((width, WIN + span), BF)] * 2 + [whole] * 8
        + [pltpu.SemaphoreType.DMA((4,))],
        flops=18 * cube,
        limit=26,
    )
    send, extra = lax.optimization_barrier((send, extra))
    if not in_kernel:
        sums = jnp.concatenate([keep, send], axis=0).reshape(-1, 2, rows, 4 * width)
        keep = lax.dynamic_index_in_dim(sums, core, 1, keepdims=False).reshape(half.shape)
        send = lax.dynamic_index_in_dim(sums, 1 - core, 1, keepdims=False).reshape(half.shape)
    seqs = lax.axis_size("seq")
    got = lax.ppermute(send, "seq", [(i, i ^ 1) for i in range(seqs)])
    returning, = vmem_call(
        returning_body, [square], [frames, slope, extra, cot, pick_t], flops=cube
    )
    got, _ = lax.optimization_barrier((got, returning))
    arrived = exchanged(returning)
    frame_grads, = vmem_call(arrived_body, [square], [placing_t, arrived], flops=cube)
    weight_grads = scatter_sums(keep, got)
    return (out_frames[None], frame_grads, weight_grads)


def solution(mesh):
    return jax.shard_map(
        shards,
        mesh=mesh,
        in_specs=(
            P(AXES, None), P(AXES), P("stream", "seq"), P("stream"),
            P(), P(), P(), P(), P("stream", "seq", None),
        ),
        out_specs=(P("stream", "seq", None), P(AXES, None), P(AXES, None)),
        check_vma=False,
    )
```

```python
import math

import jax
import jax.numpy as jnp
from jax import lax
from jax.experimental import pallas as pl
from jax.experimental.pallas import tpu as pltpu
from jax.sharding import PartitionSpec as P

H = 8
WIN = 512
NEG = -1e30
EPS_NORM = 1e-06
AXES = ("stream", "seq")
BF = jnp.bfloat16
F32 = jnp.float32

NN = (((1,), (0,)), ((), ()))
NT = (((1,), (1,)), ((), ()))


def mm(a, b, dims=NN):
    return lax.dot_general(a, b, dims, preferred_element_type=F32)


def iota2(shape, dim):
    return lax.broadcasted_iota(jnp.int32, shape, dim)


def vmem_call(body, outs, args, smem=(), hbm=(), scratch=(), flops=0, limit=12):
    spaces = [pltpu.SMEM if i in smem else pltpu.HBM if i in hbm else pltpu.VMEM for i in range(len(args))]
    size = sum(math.prod(a.shape) * a.dtype.itemsize for a in list(args) + list(outs))
    return pl.pallas_call(
        body,
        out_shape=tuple(outs),
        in_specs=[pl.BlockSpec(memory_space=space) for space in spaces],
        out_specs=tuple(pl.BlockSpec(memory_space=pltpu.VMEM) for _ in outs),
        scratch_shapes=list(scratch),
        compiler_params=pltpu.CompilerParams(vmem_limit_bytes=limit * 2**20),
        cost_estimate=pl.CostEstimate(flops=flops, bytes_accessed=size, transcendentals=0),
    )(*args)


def fetch(sources, targets, sems):
    copies = [
        pltpu.make_async_copy(source, target, sems.at[n])
        for n, (source, target) in enumerate(zip(sources, targets))
    ]
    for copy in copies:
        copy.start()
    return copies


def sds(shape, dtype=BF):
    return jax.ShapeDtypeStruct(shape, dtype)


def outgoing_body(span, slots, rf_ref, rows_hbm, out_ref, placing_ref, rows_ref, sems):
    (rows_copy,) = fetch([rows_hbm], [rows_ref], sems)
    count = rf_ref.shape[1]
    total = out_ref.shape[0]
    rf = rf_ref[...]
    target = jnp.where(rf >= 0, lax.div(rf, span), 1 << 20)
    slot = iota2((total, count), 0)
    owner = lax.div(slot, slots)
    rank = slot - owner * slots
    start = jnp.sum(jnp.where(target < owner, 1.0, 0.0), axis=1, keepdims=True)
    here = iota2((total, count), 1) - start.astype(jnp.int32)
    placing = jnp.where((target == owner) & (here == rank), 1.0, 0.0).astype(BF)
    placing_ref[...] = placing
    rows_copy.wait()
    out_ref[...] = mm(placing, rows_ref[...]).astype(BF)


def early_body(
    slots, owner_ref, placing_ref, cot_ref, wo_ref, pick_ref, pick_t_ref, placing_t_ref, do_ref, dot_ref
):
    span, lanes = owner_ref.shape[0], 128
    total = pick_ref.shape[1]
    owner = owner_ref[...]
    device = iota2((span, lanes), 1)
    hot = jnp.where(owner == device, 1.0, 0.0)
    strict = jnp.where(iota2((span, span), 1) < iota2((span, span), 0), 1.0, 0.0).astype(BF)
    before = mm(strict, hot.astype(BF))
    slot = jnp.sum(hot * (before + (device * slots).astype(F32)), axis=1, keepdims=True)
    slot = jnp.where(owner >= 0, slot.astype(jnp.int32), -1)
    pick = jnp.where(iota2((span, total), 1) == slot, 1.0, 0.0)
    pick_ref[...] = pick.astype(BF)
    pick_t_ref[...] = pick.T.astype(BF)
    placing_t_ref[...] = placing_ref[...].T
    grad = mm(cot_ref[...], wo_ref[...], NT).astype(BF)
    do_ref[...] = grad
    dot_ref[...] = grad.T


def unit_frames(frames):
    frames32 = frames.astype(F32)
    inverse = lax.rsqrt(jnp.mean(frames32 * frames32, axis=1, keepdims=True) + EPS_NORM)
    return frames32, inverse, frames32 * inverse


def frames_body(pick_ref, in_ref, frames_ref, normed_ref):
    frames = mm(pick_ref[...], in_ref[...]).astype(BF)
    frames_ref[...] = frames
    normed_ref[...] = unit_frames(frames)[2].astype(BF)


def project_body(
    query_scale, normed_ref, wq_hbm, wk_hbm, wv_hbm,
    q_ref, qt_ref, k_ref, kt_ref, v_ref, vt_ref, wk_ref, wv_ref, wq_ref, sems,
):
    copies = fetch([wq_hbm, wk_hbm, wv_hbm], [wq_ref, wk_ref, wv_ref], sems)
    normed = normed_ref[...]
    copies[0].wait()
    q = (mm(normed, wq_ref[...]) * query_scale).astype(BF)
    q_ref[...] = q
    qt_ref[...] = q.T
    copies[1].wait()
    k = mm(normed, wk_ref[...]).astype(BF)
    k_ref[...] = k
    kt_ref[...] = k.T
    copies[2].wait()
    v = mm(normed, wv_ref[...]).astype(BF)
    v_ref[...] = v
    vt_ref[...] = v.T


TILE = 128
REACH = WIN + TILE


def softmax_parts(scores, slopes, first, begin, length):
    row = iota2((TILE, TILE), 0)
    col = iota2((TILE, TILE), 1)
    halo_bias = jnp.where(begin == 0, NEG, 0.0)
    count = REACH // TILE
    time = begin + first + iota2((1, TILE), 1)
    prob_cols, grad_cols = [], []
    for h in range(2):
        at = slice(h * TILE, (h + 1) * TILE)
        parts = []
        for n in range(count):
            part = scores[n * TILE : (n + 1) * TILE, at]
            if n == 0:
                part = jnp.where(row > col, part, NEG)
            if n == count - 1:
                part = jnp.where(row <= col, part, NEG)
            elif first + n * TILE < WIN:
                part = part + halo_bias
            parts.append(part)
        peak = parts[0]
        for part in parts[1:]:
            peak = jnp.maximum(peak, part)
        peak = jnp.max(peak, axis=0, keepdims=True)
        parts = [jnp.exp2(part - peak) for part in parts]
        denom = parts[0]
        for part in parts[1:]:
            denom = denom + part
        denom = jnp.sum(denom, axis=0, keepdims=True)
        scale = jnp.where(time < length, 1.0 / denom, 0.0)
        parts = [part * scale for part in parts]
        moved = [part * slopes[n * TILE : (n + 1) * TILE, at] for n, part in enumerate(parts)]
        centre = moved[0]
        for part in moved[1:]:
            centre = centre + part
        centre = jnp.sum(centre, axis=0, keepdims=True)
        grads = [(move - part * centre).astype(BF) for part, move in zip(parts, moved)]
        prob_cols.append(jnp.concatenate([part.astype(BF) for part in parts], axis=0))
        grad_cols.append(jnp.concatenate(grads, axis=0))
    return jnp.concatenate(prob_cols, axis=1), jnp.concatenate(grad_cols, axis=1)


def both_heads(value, axis, along):
    place = iota2(value.shape, axis)
    half = value.shape[axis] // 2
    zero = jnp.zeros((), value.dtype)
    return jnp.concatenate([jnp.where(place < half, value, zero), jnp.where(place < half, zero, value)], axis=along)


def scores_body(
    head_size, meta_ref, halo_ref, wk_ref, wv_ref, q_ref, qt_ref, k_ref, v_ref, do_ref, dot_ref,
    probs_ref, grads_ref, dkh_ref, dvh_ref, khalo_t_ref, vhalo_t_ref, back_ref,
    kx, vx,
):
    span, width = q_ref.shape
    begin, length = meta_ref[0], meta_ref[1]
    halo = halo_ref[...]
    kh = mm(halo, wk_ref[...]).astype(BF)
    kx[:WIN] = kh
    khalo_t_ref[...] = kh.T
    vh = mm(halo, wv_ref[...]).astype(BF)
    vx[:WIN] = vh
    vhalo_t_ref[...] = vh.T
    kx[WIN:] = k_ref[...]
    vx[WIN:] = v_ref[...]

    pair = 2 * head_size
    tiles = span // TILE

    def one_pair(p, carry):
        cols = pl.ds(pl.multiple_of(p * pair, pair), pair)

        def multiply(a):
            here = slice(a * TILE, (a + 1) * TILE)
            keys = slice(a * TILE, a * TILE + REACH)
            scores = mm(kx[keys, cols], both_heads(qt_ref[cols, here], 0, 1))
            slopes = mm(vx[keys, cols], both_heads(dot_ref[cols, here], 0, 1))
            return scores, slopes

        halo_grads = []
        products = {0: multiply(0)}
        for a in range(tiles):
            if a + 1 < tiles:
                products[a + 1] = multiply(a + 1)
            probs, grads = softmax_parts(*products.pop(a), a * TILE, begin, length)
            probs_ref[p * tiles + a] = probs
            grads_ref[p * tiles + a] = grads
            here = slice(a * TILE, (a + 1) * TILE)
            far = WIN - a * TILE
            halo_grads.append((
                mm(grads[:far], both_heads(q_ref[here, cols], 1, 0)),
                mm(probs[:far], both_heads(do_ref[here, cols], 1, 0)),
            ))
        for which, scale, out in ((0, math.log(2.0), dkh_ref), (1, 1.0, dvh_ref)):
            for j in range(WIN // TILE):
                total = None
                for a in range(min(j + 1, tiles)):
                    piece = halo_grads[a][which][(j - a) * TILE : (j - a + 1) * TILE]
                    total = piece if total is None else total + piece
                out[j * TILE : (j + 1) * TILE, cols] = (total * scale).astype(BF)
        return carry

    lax.fori_loop(0, width // pair, one_pair, 0)
    back_ref[...] = (mm(dkh_ref[...], wk_ref[...], NT) + mm(dvh_ref[...], wv_ref[...], NT)).astype(BF)


def weights_body(
    scale, rows, head_size, meta_ref, normed_ref, halo_ref, frames_ref, cot_ref,
    wq_hbm, wk_hbm, wv_hbm, wo_hbm,
    q_ref, kt_ref, vt_ref, khalo_t_ref, vhalo_t_ref, do_ref, probs_ref, grads_ref, dkh_ref, dvh_ref,
    keep_ref, send_ref, out_ref, slope_ref,
    normed_t, halo_t, mixed_t, ktx, vtx, ot, dqt, dk, dv, wq, wk, wv, wo, sems,
):
    span, width = q_ref.shape
    copies = fetch([wq_hbm, wk_hbm, wv_hbm, wo_hbm], [wq, wk, wv, wo], sems)
    ktx[:, :WIN] = khalo_t_ref[...]
    ktx[:, WIN:] = kt_ref[...]
    vtx[:, :WIN] = vhalo_t_ref[...]
    vtx[:, WIN:] = vt_ref[...]
    pair = 2 * head_size
    tiles = span // TILE
    upper = iota2((pair, TILE), 0) < head_size

    def one_pair(p, carry):
        cols = pl.ds(pl.multiple_of(p * pair, pair), pair)
        own_grads = []
        for a in range(tiles):
            here = slice(a * TILE, (a + 1) * TILE)
            keys = slice(a * TILE, a * TILE + REACH)
            at = p * tiles + a
            mixed = mm(vtx[cols, keys], probs_ref[at])
            ot[cols, here] = jnp.where(upper, mixed[:, :TILE], mixed[:, TILE:]).astype(BF)
            moved = mm(ktx[cols, keys], grads_ref[at]) * head_size ** (-0.5)
            dqt[cols, here] = jnp.where(upper, moved[:, :TILE], moved[:, TILE:]).astype(BF)
            near = slice(WIN - a * TILE, REACH)
            own_grads.append((
                mm(grads_ref[at, near], both_heads(q_ref[here, cols], 1, 0)),
                mm(probs_ref[at, near], both_heads(do_ref[here, cols], 1, 0)),
            ))
        for which, factor, out in ((0, math.log(2.0), dk), (1, 1.0, dv)):
            for j in range(tiles):
                total = None
                for a in range(j, tiles):
                    piece = own_grads[a][which][j * TILE : (j + 1) * TILE]
                    total = piece if total is None else total + piece
                out[j * TILE : (j + 1) * TILE, cols] = (total * factor).astype(BF)
        return carry

    lax.fori_loop(0, width // pair, one_pair, 0)

    chunks = width // (2 * rows)
    split = (chunks, 2, rows, span)
    normed_t[...] = normed_ref[...].T.reshape(split)
    halo_t[...] = halo_ref[...].T.reshape(split)
    mixed_t[...] = ot[...].reshape(split)
    mine = meta_ref[2]
    for side, out in ((1 - mine, send_ref), (mine, keep_ref)):
        own = normed_t[:, side].reshape(width // 2, span)
        far = halo_t[:, side].reshape(width // 2, span)
        mixed = mixed_t[:, side].reshape(width // 2, span)
        for n, total in enumerate((
            mm(own, dqt[...], NT),
            mm(own, dk[...]) + mm(far, dkh_ref[...]),
            mm(own, dv[...]) + mm(far, dvh_ref[...]),
            mm(mixed, cot_ref[...]),
        )):
            out[:, n * width : (n + 1) * width] = (total * scale).astype(BF)
    for copy in copies:
        copy.wait()
    slope = mm(dqt[...].T, wq[...], NT)
    slope = slope + mm(dk[...], wk[...], NT)
    slope_ref[...] = slope + mm(dv[...], wv[...], NT)
    out = mm(ot[...].T, wo[...]) + frames_ref[...].astype(F32)
    out_ref[...] = out.astype(BF)


def returning_body(frames_ref, slope_ref, extra_ref, cot_ref, pick_t_ref, out_ref):
    _, inverse, normed32 = unit_frames(frames_ref[...])
    slope = slope_ref[...] + extra_ref[...].astype(F32)
    centre = jnp.mean(slope * normed32, axis=1, keepdims=True)
    grad = inverse * (slope - normed32 * centre) + cot_ref[...].astype(F32)
    out_ref[...] = mm(pick_t_ref[...], grad.astype(BF)).astype(BF)


def arrived_body(placing_t_ref, in_ref, out_ref):
    out_ref[...] = mm(placing_t_ref[...], in_ref[...]).astype(BF)


def passed_along(shard, by):
    devices = lax.axis_size("seq")
    pairs = [(i, i + by) for i in range(devices) if 0 <= i + by < devices]
    return lax.ppermute(shard, "seq", pairs)


def spread_body(place_ref, *refs):
    parts = refs[0].shape[0]
    inputs, outs = refs[:-parts], refs[-parts:]
    for k, out in enumerate(outs):
        at = place_ref[0] ^ k
        total = inputs[0][at].astype(F32)
        for ref in inputs[1:]:
            total = total + ref[at].astype(F32)
        out[...] = total.astype(BF)


def spread(inputs, place, parts):
    columns = inputs[0].shape[-1]
    inputs = [shard.reshape(parts, -1, columns) for shard in inputs]
    piece = sds(inputs[0].shape[1:])
    return vmem_call(spread_body, [piece] * parts, [place.reshape(1)] + inputs, smem=(0,))


def swapped(pieces, axis, step):
    count = lax.axis_size(axis)
    return [pieces[0]] + [
        lax.ppermute(piece, axis, [(i, i ^ (k * step)) for i in range(count)])
        for k, piece in enumerate(pieces[1:], 1)
    ]


def shards(
    frame_rows, row_frame, frame_owner, lengths,
    query_weight, key_weight, value_weight, out_weight, cotangent,
):
    devices = lax.axis_size(AXES)
    row_count, width = frame_rows.shape
    span = frame_owner.shape[1]
    slots = row_count // devices
    slab = span * lax.axis_size("seq")
    head_size = width // H
    cube = 2 * span * width * width
    square = sds((span, width))
    begin = (lax.axis_index("seq") * span).astype(jnp.int32)
    rows = width // devices
    in_kernel = rows % 16 == 0
    core = (lax.axis_index("seq") & 1).astype(jnp.int32)
    meta = jnp.stack([begin, lengths[0], core if in_kernel else jnp.zeros((), jnp.int32)])
    cot = cotangent[0]

    def exchanged(shard):
        got = lax.all_to_all(
            shard.reshape(devices, slots, width), AXES, split_axis=0, concat_axis=0, tiled=True
        )
        return got.reshape(devices * slots, width)

    outgoing, placing = vmem_call(
        lambda *refs: outgoing_body(span, slots, *refs),
        [square, sds((devices * slots, row_count))],
        [row_frame.reshape(1, row_count), frame_rows],
        hbm=(1,),
        scratch=[pltpu.VMEM((row_count, width), BF), pltpu.SemaphoreType.DMA((1,))],
        flops=cube,
        limit=60,
    )
    incoming = exchanged(outgoing)
    pick, pick_t, placing_t, do, dot = vmem_call(
        lambda *refs: early_body(slots, *refs),
        [square, square, square, square, sds((width, span))],
        [frame_owner.reshape(span, 1), placing, cot, out_weight],
        flops=2 * cube,
    )
    frames, normed = vmem_call(frames_body, [square, square], [pick, incoming], flops=cube)
    halo = passed_along(normed, 1)
    query_scale = head_size ** (-0.5) * math.log2(math.e)
    q, qt, k, kt, v, vt, wk, wv = vmem_call(
        lambda *refs: project_body(query_scale, *refs),
        [square] * 8,
        [normed, query_weight, key_weight, value_weight],
        hbm=(1, 2, 3),
        scratch=[pltpu.VMEM((width, width), BF), pltpu.SemaphoreType.DMA((3,))],
        flops=3 * cube,
    )
    saved = sds((H // 2 * (span // TILE), REACH, 2 * TILE))
    probs, grads, dkh, dvh, khalo_t, vhalo_t, back = vmem_call(
        lambda *refs: scores_body(head_size, *refs),
        [saved, saved] + [square] * 5,
        [meta, halo, wk, wv, q, qt, k, v, do, dot],
        smem=(0,),
        scratch=[pltpu.VMEM((WIN + span, width), BF)] * 2,
        flops=12 * cube,
        limit=24,
    )
    extra = passed_along(back, -1)
    chunk = rows if in_kernel else width // 2
    split = pltpu.VMEM((width // (2 * chunk), 2, chunk, span), BF)
    whole = pltpu.VMEM((width, width), BF)
    half = sds((width // 2, 4 * width))
    keep, send, out_frames, slope = vmem_call(
        lambda *refs: weights_body(slab ** (-0.5), chunk, head_size, *refs),
        [half, half, square, sds((span, width), F32)],
        [meta, normed, halo, frames, cot, query_weight, key_weight, value_weight, out_weight,
         q, kt, vt, khalo_t, vhalo_t, do, probs, grads, dkh, dvh],
        smem=(0,),
        hbm=(5, 6, 7, 8),
        scratch=[split] * 3 + [pltpu.VMEM((width, WIN + span), BF)] * 2 + [whole] * 8
        + [pltpu.SemaphoreType.DMA((4,))],
        flops=18 * cube,
        limit=26,
    )
    send, extra = lax.optimization_barrier((send, extra))
    if not in_kernel:
        sums = jnp.concatenate([keep, send], axis=0).reshape(-1, 2, rows, 4 * width)
        keep = lax.dynamic_index_in_dim(sums, core, 1, keepdims=False).reshape(half.shape)
        send = lax.dynamic_index_in_dim(sums, 1 - core, 1, keepdims=False).reshape(half.shape)
    seqs = lax.axis_size("seq")
    got = lax.ppermute(send, "seq", [(i, i ^ 1) for i in range(seqs)])
    returning, = vmem_call(
        returning_body, [square], [frames, slope, extra, cot, pick_t], flops=cube
    )
    got, returning = lax.optimization_barrier((got, returning))
    pieces = spread([keep, got], lax.axis_index("stream"), lax.axis_size("stream"))
    *pieces, returning = lax.optimization_barrier((*pieces, returning))
    pieces = swapped(pieces, "stream", 1)
    arrived = exchanged(returning)
    frame_grads, = vmem_call(arrived_body, [square], [placing_t, arrived], flops=cube)
    pieces = swapped(spread(pieces, lax.axis_index("seq") >> 1, seqs // 2), "seq", 2)
    weight_grads = pieces[0].astype(F32)
    for piece in pieces[1:]:
        weight_grads = weight_grads + piece.astype(F32)
    return (out_frames[None], frame_grads, weight_grads)


def solution(mesh):
    return jax.shard_map(
        shards,
        mesh=mesh,
        in_specs=(
            P(AXES, None), P(AXES), P("stream", "seq"), P("stream"),
            P(), P(), P(), P(), P("stream", "seq", None),
        ),
        out_specs=(P("stream", "seq", None), P(AXES, None), P(AXES, None)),
        check_vma=False,
    )
```

```python
import math

import jax
import jax.numpy as jnp
from jax import lax
from jax.experimental import pallas as pl
from jax.experimental.pallas import tpu as pltpu
from jax.sharding import PartitionSpec as P

H = 8
WIN = 512
NEG = -1e30
EPS_NORM = 1e-06
AXES = ("stream", "seq")
BF = jnp.bfloat16
F32 = jnp.float32

NN = (((1,), (0,)), ((), ()))
NT = (((1,), (1,)), ((), ()))


def mm(a, b, dims=NN):
    return lax.dot_general(a, b, dims, preferred_element_type=F32)


def iota2(shape, dim):
    return lax.broadcasted_iota(jnp.int32, shape, dim)


def vmem_call(body, outs, args, smem=(), hbm=(), scratch=(), flops=0, limit=12):
    spaces = [pltpu.SMEM if i in smem else pltpu.HBM if i in hbm else pltpu.VMEM for i in range(len(args))]
    size = sum(math.prod(a.shape) * a.dtype.itemsize for a in list(args) + list(outs))
    return pl.pallas_call(
        body,
        out_shape=tuple(outs),
        in_specs=[pl.BlockSpec(memory_space=space) for space in spaces],
        out_specs=tuple(pl.BlockSpec(memory_space=pltpu.VMEM) for _ in outs),
        scratch_shapes=list(scratch),
        compiler_params=pltpu.CompilerParams(vmem_limit_bytes=limit * 2**20),
        cost_estimate=pl.CostEstimate(flops=flops, bytes_accessed=size, transcendentals=0),
    )(*args)


def fetch(sources, targets, sems):
    copies = [
        pltpu.make_async_copy(source, target, sems.at[n])
        for n, (source, target) in enumerate(zip(sources, targets))
    ]
    for copy in copies:
        copy.start()
    return copies


def sds(shape, dtype=BF):
    return jax.ShapeDtypeStruct(shape, dtype)


def outgoing_body(span, slots, rf_ref, rows_hbm, out_ref, placing_ref, rows_ref, sems):
    (rows_copy,) = fetch([rows_hbm], [rows_ref], sems)
    count = rf_ref.shape[1]
    total = out_ref.shape[0]
    rf = rf_ref[...]
    target = jnp.where(rf >= 0, lax.div(rf, span), 1 << 20)
    slot = iota2((total, count), 0)
    owner = lax.div(slot, slots)
    rank = slot - owner * slots
    start = jnp.sum(jnp.where(target < owner, 1.0, 0.0), axis=1, keepdims=True)
    here = iota2((total, count), 1) - start.astype(jnp.int32)
    placing = jnp.where((target == owner) & (here == rank), 1.0, 0.0).astype(BF)
    placing_ref[...] = placing
    rows_copy.wait()
    out_ref[...] = mm(placing, rows_ref[...]).astype(BF)


def early_body(
    slots, owner_ref, placing_ref, cot_ref, wo_ref, pick_ref, pick_t_ref, placing_t_ref, dot_ref
):
    span, lanes = owner_ref.shape[0], 128
    total = pick_ref.shape[1]
    owner = owner_ref[...]
    device = iota2((span, lanes), 1)
    hot = jnp.where(owner == device, 1.0, 0.0)
    strict = jnp.where(iota2((span, span), 1) < iota2((span, span), 0), 1.0, 0.0).astype(BF)
    before = mm(strict, hot.astype(BF))
    slot = jnp.sum(hot * (before + (device * slots).astype(F32)), axis=1, keepdims=True)
    slot = jnp.where(owner >= 0, slot.astype(jnp.int32), -1)
    pick = jnp.where(iota2((span, total), 1) == slot, 1.0, 0.0)
    pick_ref[...] = pick.astype(BF)
    pick_t_ref[...] = pick.T.astype(BF)
    placing_t_ref[...] = placing_ref[...].T
    dot_ref[...] = mm(cot_ref[...], wo_ref[...], NT).astype(BF).T


def unit_frames(frames):
    frames32 = frames.astype(F32)
    inverse = lax.rsqrt(jnp.mean(frames32 * frames32, axis=1, keepdims=True) + EPS_NORM)
    return frames32, inverse, frames32 * inverse


def frames_body(pick_ref, in_ref, frames_ref, normed_ref):
    frames = mm(pick_ref[...], in_ref[...]).astype(BF)
    frames_ref[...] = frames
    normed_ref[...] = unit_frames(frames)[2].astype(BF)


def project_body(
    query_scale, normed_ref, wq_hbm, wk_hbm, wv_hbm,
    qt_ref, k_ref, kt_ref, v_ref, vt_ref, wk_ref, wv_ref, wq_ref, sems,
):
    copies = fetch([wq_hbm, wk_hbm, wv_hbm], [wq_ref, wk_ref, wv_ref], sems)
    normed = normed_ref[...]
    copies[0].wait()
    qt_ref[...] = (mm(normed, wq_ref[...]) * query_scale).astype(BF).T
    copies[1].wait()
    k = mm(normed, wk_ref[...]).astype(BF)
    k_ref[...] = k
    kt_ref[...] = k.T
    copies[2].wait()
    v = mm(normed, wv_ref[...]).astype(BF)
    v_ref[...] = v
    vt_ref[...] = v.T


TILE = 128
REACH = WIN + TILE


def softmax_parts(scores, slopes, first, begin, length):
    row = iota2((TILE, TILE), 0)
    col = iota2((TILE, TILE), 1)
    halo_bias = jnp.where(begin == 0, NEG, 0.0)
    count = REACH // TILE
    time = begin + first + iota2((1, TILE), 1)
    raised_cols, grad_cols, scales = [], [], []
    for h in range(2):
        at = slice(h * TILE, (h + 1) * TILE)
        parts = []
        for n in range(count):
            part = scores[n * TILE : (n + 1) * TILE, at]
            if n == 0:
                part = jnp.where(row > col, part, NEG)
            if n == count - 1:
                part = jnp.where(row <= col, part, NEG)
            elif first + n * TILE < WIN:
                part = part + halo_bias
            parts.append(part)
        peak = parts[0]
        for part in parts[1:]:
            peak = jnp.maximum(peak, part)
        peak = jnp.max(peak, axis=0, keepdims=True)
        moves = [slopes[n * TILE : (n + 1) * TILE, at] for n in range(count)]
        denom = centre = None
        low_parts = []
        for part, move in zip(parts, moves):
            part = jnp.exp2(part - peak)
            low_parts.append(part.astype(BF))
            moved = part * move
            denom = part if denom is None else denom + part
            centre = moved if centre is None else centre + moved
        denom = jnp.sum(denom, axis=0, keepdims=True)
        centre = jnp.sum(centre, axis=0, keepdims=True) / denom
        scales.append(jnp.where(time < length, 1.0 / denom, 0.0))
        raised_cols.append(jnp.concatenate(low_parts, axis=0))
        grad_cols.append(jnp.concatenate(
            [(part.astype(F32) * (move - centre)).astype(BF) for part, move in zip(low_parts, moves)], axis=0
        ))
    return (
        jnp.concatenate(raised_cols, axis=1), jnp.concatenate(grad_cols, axis=1), jnp.concatenate(scales, axis=1)
    )


def both_heads(value, axis, along):
    place = iota2(value.shape, axis)
    half = value.shape[axis] // 2
    zero = jnp.zeros((), value.dtype)
    return jnp.concatenate([jnp.where(place < half, value, zero), jnp.where(place < half, zero, value)], axis=along)


def scores_body(
    head_size, meta_ref, halo_ref, wk_ref, wv_ref, qt_ref, k_ref, v_ref, dot_ref,
    raised_ref, grads_ref, scale_ref, q_ref, do_ref, dkh_ref, dvh_ref, khalo_t_ref, vhalo_t_ref, back_ref,
    kx, vx,
):
    span, width = k_ref.shape
    begin, length = meta_ref[0], meta_ref[1]
    halo = halo_ref[...]
    kh = mm(halo, wk_ref[...]).astype(BF)
    kx[:WIN] = kh
    khalo_t_ref[...] = kh.T
    vh = mm(halo, wv_ref[...]).astype(BF)
    vx[:WIN] = vh
    vhalo_t_ref[...] = vh.T
    kx[WIN:] = k_ref[...]
    vx[WIN:] = v_ref[...]

    pair = 2 * head_size
    tiles = span // TILE
    upper = iota2((pair, TILE), 0) < head_size

    def one_pair(p, carry):
        cols = pl.ds(pl.multiple_of(p * pair, pair), pair)

        def multiply(a):
            here = slice(a * TILE, (a + 1) * TILE)
            keys = slice(a * TILE, a * TILE + REACH)
            scores = mm(kx[keys, cols], both_heads(qt_ref[cols, here], 0, 1))
            slopes = mm(vx[keys, cols], both_heads(dot_ref[cols, here], 0, 1))
            return scores, slopes

        halo_grads = []
        products = {0: multiply(0)}
        for a in range(tiles):
            if a + 1 < tiles:
                products[a + 1] = multiply(a + 1)
            raised, grads, scale = softmax_parts(*products.pop(a), a * TILE, begin, length)
            raised_ref[p * tiles + a] = raised
            grads_ref[p * tiles + a] = grads
            scale_ref[p * tiles + a] = scale
            here = slice(a * TILE, (a + 1) * TILE)
            far = WIN - a * TILE
            spread_scale = jnp.where(upper, scale[:, :TILE], scale[:, TILE:])
            queries = (qt_ref[cols, here].astype(F32) * spread_scale).T.astype(BF)
            slopes = (dot_ref[cols, here].astype(F32) * spread_scale).T.astype(BF)
            q_ref[here, cols] = queries
            do_ref[here, cols] = slopes
            halo_grads.append((
                mm(grads[:far], both_heads(queries, 1, 0)),
                mm(raised[:far], both_heads(slopes, 1, 0)),
            ))
        for which, scale, out in ((0, math.log(2.0), dkh_ref), (1, 1.0, dvh_ref)):
            for j in range(WIN // TILE):
                total = None
                for a in range(min(j + 1, tiles)):
                    piece = halo_grads[a][which][(j - a) * TILE : (j - a + 1) * TILE]
                    total = piece if total is None else total + piece
                out[j * TILE : (j + 1) * TILE, cols] = (total * scale).astype(BF)
        return carry

    lax.fori_loop(0, width // pair, one_pair, 0)
    back_ref[...] = (mm(dkh_ref[...], wk_ref[...], NT) + mm(dvh_ref[...], wv_ref[...], NT)).astype(BF)


def weights_body(
    scale, rows, head_size, meta_ref, normed_ref, halo_ref, cot_ref,
    q_ref, kt_ref, vt_ref, khalo_t_ref, vhalo_t_ref, do_ref, raised_ref, grads_ref, scale_ref, dkh_ref, dvh_ref,
    keep_ref, send_ref, ot, dqt, dk, dv,
    normed_t, halo_t, mixed_t, ktx, vtx,
):
    span, width = q_ref.shape
    ktx[:, :WIN] = khalo_t_ref[...]
    ktx[:, WIN:] = kt_ref[...]
    vtx[:, :WIN] = vhalo_t_ref[...]
    vtx[:, WIN:] = vt_ref[...]
    pair = 2 * head_size
    tiles = span // TILE
    upper = iota2((pair, TILE), 0) < head_size

    def one_pair(p, carry):
        cols = pl.ds(pl.multiple_of(p * pair, pair), pair)
        own_grads = []
        for a in range(tiles):
            here = slice(a * TILE, (a + 1) * TILE)
            keys = slice(a * TILE, a * TILE + REACH)
            at = p * tiles + a
            shrink = scale_ref[at]
            mixed = mm(vtx[cols, keys], raised_ref[at]) * shrink
            ot[cols, here] = jnp.where(upper, mixed[:, :TILE], mixed[:, TILE:]).astype(BF)
            moved = mm(ktx[cols, keys], grads_ref[at]) * (shrink * head_size ** (-0.5))
            dqt[cols, here] = jnp.where(upper, moved[:, :TILE], moved[:, TILE:]).astype(BF)
            near = slice(WIN - a * TILE, REACH)
            own_grads.append((
                mm(grads_ref[at, near], both_heads(q_ref[here, cols], 1, 0)),
                mm(raised_ref[at, near], both_heads(do_ref[here, cols], 1, 0)),
            ))
        for which, factor, out in ((0, math.log(2.0), dk), (1, 1.0, dv)):
            for j in range(tiles):
                total = None
                for a in range(j, tiles):
                    piece = own_grads[a][which][j * TILE : (j + 1) * TILE]
                    total = piece if total is None else total + piece
                out[j * TILE : (j + 1) * TILE, cols] = (total * factor).astype(BF)
        return carry

    lax.fori_loop(0, width // pair, one_pair, 0)

    chunks = width // (2 * rows)
    split = (chunks, 2, rows, span)
    normed_t[...] = normed_ref[...].T.reshape(split)
    halo_t[...] = halo_ref[...].T.reshape(split)
    mixed_t[...] = ot[...].reshape(split)
    mine = meta_ref[2]
    for side, out in ((1 - mine, send_ref), (mine, keep_ref)):
        own = normed_t[:, side].reshape(width // 2, span)
        far = halo_t[:, side].reshape(width // 2, span)
        mixed = mixed_t[:, side].reshape(width // 2, span)
        for n, total in enumerate((
            mm(own, dqt[...], NT),
            mm(own, dk[...]) + mm(far, dkh_ref[...]),
            mm(own, dv[...]) + mm(far, dvh_ref[...]),
            mm(mixed, cot_ref[...]),
        )):
            out[:, n * width : (n + 1) * width] = (total * scale).astype(BF)


def returning_body(
    frames_ref, dqt_ref, dk_ref, dv_ref, wq_ref, wk_ref, wv_ref, extra_ref, cot_ref, pick_t_ref, out_ref
):
    _, inverse, normed32 = unit_frames(frames_ref[...])
    slope = mm(dqt_ref[...].T, wq_ref[...], NT)
    slope = slope + mm(dk_ref[...], wk_ref[...], NT)
    slope = slope + mm(dv_ref[...], wv_ref[...], NT)
    slope = slope + extra_ref[...].astype(F32)
    centre = jnp.mean(slope * normed32, axis=1, keepdims=True)
    grad = inverse * (slope - normed32 * centre) + cot_ref[...].astype(F32)
    out_ref[...] = mm(pick_t_ref[...], grad.astype(BF)).astype(BF)


def out_body(frames_ref, ot_ref, wo_ref, out_ref):
    out_ref[...] = (mm(ot_ref[...].T, wo_ref[...]) + frames_ref[...].astype(F32)).astype(BF)


def arrived_body(placing_t_ref, in_ref, out_ref):
    out_ref[...] = mm(placing_t_ref[...], in_ref[...]).astype(BF)


def passed_along(shard, by):
    devices = lax.axis_size("seq")
    pairs = [(i, i + by) for i in range(devices) if 0 <= i + by < devices]
    return lax.ppermute(shard, "seq", pairs)


def spread_body(place_ref, *refs):
    parts = refs[0].shape[0]
    inputs, outs = refs[:-parts], refs[-parts:]
    for k, out in enumerate(outs):
        at = place_ref[0] ^ k
        total = inputs[0][at].astype(F32)
        for ref in inputs[1:]:
            total = total + ref[at].astype(F32)
        out[...] = total.astype(BF)


def spread(inputs, place, parts):
    columns = inputs[0].shape[-1]
    inputs = [shard.reshape(parts, -1, columns) for shard in inputs]
    piece = sds(inputs[0].shape[1:])
    return vmem_call(spread_body, [piece] * parts, [place.reshape(1)] + inputs, smem=(0,))


def swapped(pieces, axis, step):
    count = lax.axis_size(axis)
    return [pieces[0]] + [
        lax.ppermute(piece, axis, [(i, i ^ (k * step)) for i in range(count)])
        for k, piece in enumerate(pieces[1:], 1)
    ]


def shards(
    frame_rows, row_frame, frame_owner, lengths,
    query_weight, key_weight, value_weight, out_weight, cotangent,
):
    devices = lax.axis_size(AXES)
    row_count, width = frame_rows.shape
    span = frame_owner.shape[1]
    slots = row_count // devices
    slab = span * lax.axis_size("seq")
    head_size = width // H
    cube = 2 * span * width * width
    square = sds((span, width))
    begin = (lax.axis_index("seq") * span).astype(jnp.int32)
    rows = width // devices
    in_kernel = rows % 16 == 0
    core = (lax.axis_index("seq") & 1).astype(jnp.int32)
    meta = jnp.stack([begin, lengths[0], core if in_kernel else jnp.zeros((), jnp.int32)])
    cot = cotangent[0]

    def exchanged(shard):
        got = lax.all_to_all(
            shard.reshape(devices, slots, width), AXES, split_axis=0, concat_axis=0, tiled=True
        )
        return got.reshape(devices * slots, width)

    outgoing, placing = vmem_call(
        lambda *refs: outgoing_body(span, slots, *refs),
        [square, sds((devices * slots, row_count))],
        [row_frame.reshape(1, row_count), frame_rows],
        hbm=(1,),
        scratch=[pltpu.VMEM((row_count, width), BF), pltpu.SemaphoreType.DMA((1,))],
        flops=cube,
    )
    incoming = exchanged(outgoing)
    pick, pick_t, placing_t, dot = vmem_call(
        lambda *refs: early_body(slots, *refs),
        [square, square, square, sds((width, span))],
        [frame_owner.reshape(span, 1), placing, cot, out_weight],
        flops=2 * cube,
    )
    frames, normed = vmem_call(frames_body, [square, square], [pick, incoming], flops=cube)
    halo = passed_along(normed, 1)
    query_scale = head_size ** (-0.5) * math.log2(math.e)
    qt, k, kt, v, vt, wk, wv = vmem_call(
        lambda *refs: project_body(query_scale, *refs),
        [square] * 7,
        [normed, query_weight, key_weight, value_weight],
        hbm=(1, 2, 3),
        scratch=[pltpu.VMEM((width, width), BF), pltpu.SemaphoreType.DMA((3,))],
        flops=3 * cube,
    )
    units = H // 2 * (span // TILE)
    saved = sds((units, REACH, 2 * TILE))
    raised, grads, scales, q, do, dkh, dvh, khalo_t, vhalo_t, back = vmem_call(
        lambda *refs: scores_body(head_size, *refs),
        [saved, saved, sds((units, 1, 2 * TILE), F32)] + [square] * 7,
        [meta, halo, wk, wv, qt, k, v, dot],
        smem=(0,),
        scratch=[pltpu.VMEM((WIN + span, width), BF)] * 2,
        flops=12 * cube,
        limit=14,
    )
    extra = passed_along(back, -1)
    chunk = rows if in_kernel else width // 2
    split = pltpu.VMEM((width // (2 * chunk), 2, chunk, span), BF)
    half = sds((width // 2, 4 * width))
    keep, send, ot, dqt, dk, dv = vmem_call(
        lambda *refs: weights_body(slab ** (-0.5), chunk, head_size, *refs),
        [half, half] + [square] * 4,
        [meta, normed, halo, cot, q, kt, vt, khalo_t, vhalo_t, do, raised, grads, scales, dkh, dvh],
        smem=(0,),
        scratch=[split] * 3 + [pltpu.VMEM((width, WIN + span), BF)] * 2,
        flops=14 * cube,
        limit=14,
    )
    send, extra = lax.optimization_barrier((send, extra))
    if not in_kernel:
        sums = jnp.concatenate([keep, send], axis=0).reshape(-1, 2, rows, 4 * width)
        keep = lax.dynamic_index_in_dim(sums, core, 1, keepdims=False).reshape(half.shape)
        send = lax.dynamic_index_in_dim(sums, 1 - core, 1, keepdims=False).reshape(half.shape)
    seqs = lax.axis_size("seq")
    got = lax.ppermute(send, "seq", [(i, i ^ 1) for i in range(seqs)])
    returning, = vmem_call(
        returning_body,
        [square],
        [frames, dqt, dk, dv, query_weight, key_weight, value_weight, extra, cot, pick_t],
        flops=4 * cube,
    )
    got, returning = lax.optimization_barrier((got, returning))
    pieces = spread([keep, got], lax.axis_index("stream"), lax.axis_size("stream"))
    pieces = swapped(pieces, "stream", 1)
    *pieces, returning = lax.optimization_barrier((*pieces, returning))
    arrived = exchanged(returning)
    out_frames, = vmem_call(out_body, [square], [frames, ot, out_weight], flops=cube)
    frame_grads, = vmem_call(arrived_body, [square], [placing_t, arrived], flops=cube)
    pieces = swapped(spread(pieces, lax.axis_index("seq") >> 1, seqs // 2), "seq", 2)
    weight_grads = pieces[0].astype(F32)
    for piece in pieces[1:]:
        weight_grads = weight_grads + piece.astype(F32)
    return (out_frames[None], frame_grads, weight_grads)


def solution(mesh):
    return jax.shard_map(
        shards,
        mesh=mesh,
        in_specs=(
            P(AXES, None), P(AXES), P("stream", "seq"), P("stream"),
            P(), P(), P(), P(), P("stream", "seq", None),
        ),
        out_specs=(P("stream", "seq", None), P(AXES, None), P(AXES, None)),
        check_vma=False,
    )
```

```python
import math

import jax
import jax.numpy as jnp
from jax import lax
from jax.experimental import pallas as pl
from jax.experimental.pallas import tpu as pltpu
from jax.sharding import PartitionSpec as P

H = 8
WIN = 512
NEG = -1e30
EPS_NORM = 1e-06
AXES = ("stream", "seq")
BF = jnp.bfloat16
F32 = jnp.float32

NN = (((1,), (0,)), ((), ()))
NT = (((1,), (1,)), ((), ()))


def mm(a, b, dims=NN):
    return lax.dot_general(a, b, dims, preferred_element_type=F32)


def iota2(shape, dim):
    return lax.broadcasted_iota(jnp.int32, shape, dim)


def vmem_call(body, outs, args, smem=(), hbm=(), scratch=(), flops=0, limit=12):
    spaces = [pltpu.SMEM if i in smem else pltpu.HBM if i in hbm else pltpu.VMEM for i in range(len(args))]
    size = sum(math.prod(a.shape) * a.dtype.itemsize for a in list(args) + list(outs))
    return pl.pallas_call(
        body,
        out_shape=tuple(outs),
        in_specs=[pl.BlockSpec(memory_space=space) for space in spaces],
        out_specs=tuple(pl.BlockSpec(memory_space=pltpu.VMEM) for _ in outs),
        scratch_shapes=list(scratch),
        compiler_params=pltpu.CompilerParams(vmem_limit_bytes=limit * 2**20),
        cost_estimate=pl.CostEstimate(flops=flops, bytes_accessed=size, transcendentals=0),
    )(*args)


def fetch(sources, targets, sems):
    copies = [
        pltpu.make_async_copy(source, target, sems.at[n])
        for n, (source, target) in enumerate(zip(sources, targets))
    ]
    for copy in copies:
        copy.start()
    return copies


def sds(shape, dtype=BF):
    return jax.ShapeDtypeStruct(shape, dtype)


def outgoing_body(span, slots, rf_ref, rows_hbm, out_ref, placing_ref, rows_ref, sems):
    (rows_copy,) = fetch([rows_hbm], [rows_ref], sems)
    count = rf_ref.shape[1]
    total = out_ref.shape[0]
    rf = rf_ref[...]
    target = jnp.where(rf >= 0, lax.div(rf, span), 1 << 20)
    slot = iota2((total, count), 0)
    owner = lax.div(slot, slots)
    rank = slot - owner * slots
    start = jnp.sum(jnp.where(target < owner, 1.0, 0.0), axis=1, keepdims=True)
    here = iota2((total, count), 1) - start.astype(jnp.int32)
    placing = jnp.where((target == owner) & (here == rank), 1.0, 0.0).astype(BF)
    placing_ref[...] = placing
    rows_copy.wait()
    out_ref[...] = mm(placing, rows_ref[...]).astype(BF)


def early_body(
    slots, owner_ref, placing_ref, cot_ref, wo_ref, pick_ref, pick_t_ref, placing_t_ref, dot_ref
):
    span, lanes = owner_ref.shape[0], 128
    total = pick_ref.shape[1]
    owner = owner_ref[...]
    device = iota2((span, lanes), 1)
    hot = jnp.where(owner == device, 1.0, 0.0)
    strict = jnp.where(iota2((span, span), 1) < iota2((span, span), 0), 1.0, 0.0).astype(BF)
    before = mm(strict, hot.astype(BF))
    slot = jnp.sum(hot * (before + (device * slots).astype(F32)), axis=1, keepdims=True)
    slot = jnp.where(owner >= 0, slot.astype(jnp.int32), -1)
    pick = jnp.where(iota2((span, total), 1) == slot, 1.0, 0.0)
    pick_ref[...] = pick.astype(BF)
    pick_t_ref[...] = pick.T.astype(BF)
    placing_t_ref[...] = placing_ref[...].T
    dot_ref[...] = mm(cot_ref[...], wo_ref[...], NT).astype(BF).T


def unit_frames(frames):
    frames32 = frames.astype(F32)
    inverse = lax.rsqrt(jnp.mean(frames32 * frames32, axis=1, keepdims=True) + EPS_NORM)
    return frames32, inverse, frames32 * inverse


def frames_body(pick_ref, in_ref, frames_ref, normed_ref):
    frames = mm(pick_ref[...], in_ref[...]).astype(BF)
    frames_ref[...] = frames
    normed_ref[...] = unit_frames(frames)[2].astype(BF)


def project_body(
    query_scale, normed_ref, wq_hbm, wk_hbm, wv_hbm,
    qt_ref, k_ref, kt_ref, v_ref, vt_ref, wk_ref, wv_ref, wq_ref, sems,
):
    copies = fetch([wq_hbm, wk_hbm, wv_hbm], [wq_ref, wk_ref, wv_ref], sems)
    normed = normed_ref[...]
    copies[0].wait()
    qt_ref[...] = (mm(normed, wq_ref[...]) * query_scale).astype(BF).T
    copies[1].wait()
    k = mm(normed, wk_ref[...]).astype(BF)
    k_ref[...] = k
    kt_ref[...] = k.T
    copies[2].wait()
    v = mm(normed, wv_ref[...]).astype(BF)
    v_ref[...] = v
    vt_ref[...] = v.T


TILE = 128
REACH = WIN + TILE


def softmax_parts(scores, slopes, first, begin, length):
    row = iota2((TILE, TILE), 0)
    col = iota2((TILE, TILE), 1)
    halo_bias = jnp.where(begin == 0, NEG, 0.0)
    count = REACH // TILE
    time = begin + first + iota2((1, TILE), 1)
    raised_cols, grad_cols, scales = [], [], []
    for h in range(2):
        at = slice(h * TILE, (h + 1) * TILE)
        parts = []
        for n in range(count):
            part = scores[n * TILE : (n + 1) * TILE, at]
            if n == 0:
                part = jnp.where(row > col, part, NEG)
            if n == count - 1:
                part = jnp.where(row <= col, part, NEG)
            elif first + n * TILE < WIN:
                part = part + halo_bias
            parts.append(part)
        peak = parts[0]
        for part in parts[1:]:
            peak = jnp.maximum(peak, part)
        peak = jnp.max(peak, axis=0, keepdims=True)
        moves = [slopes[n * TILE : (n + 1) * TILE, at] for n in range(count)]
        denom = centre = None
        low_parts = []
        for part, move in zip(parts, moves):
            part = jnp.exp2(part - peak)
            low_parts.append(part.astype(BF))
            moved = part * move
            denom = part if denom is None else denom + part
            centre = moved if centre is None else centre + moved
        denom = jnp.sum(denom, axis=0, keepdims=True)
        centre = jnp.sum(centre, axis=0, keepdims=True) / denom
        scales.append(jnp.where(time < length, 1.0 / denom, 0.0))
        raised_cols.append(jnp.concatenate(low_parts, axis=0))
        grad_cols.append(jnp.concatenate(
            [(part.astype(F32) * (move - centre)).astype(BF) for part, move in zip(low_parts, moves)], axis=0
        ))
    return (
        jnp.concatenate(raised_cols, axis=1), jnp.concatenate(grad_cols, axis=1), jnp.concatenate(scales, axis=1)
    )


def both_heads(value, axis, along):
    place = iota2(value.shape, axis)
    half = value.shape[axis] // 2
    zero = jnp.zeros((), value.dtype)
    return jnp.concatenate([jnp.where(place < half, value, zero), jnp.where(place < half, zero, value)], axis=along)


def scores_body(
    head_size, meta_ref, halo_ref, wk_ref, wv_ref, qt_ref, k_ref, v_ref, dot_ref,
    raised_ref, grads_ref, scale_ref, q_ref, do_ref, dkh_ref, dvh_ref, khalo_t_ref, vhalo_t_ref, back_ref,
    kx, vx,
):
    span, width = k_ref.shape
    begin, length = meta_ref[0], meta_ref[1]
    halo = halo_ref[...]
    kh = mm(halo, wk_ref[...]).astype(BF)
    kx[:WIN] = kh
    khalo_t_ref[...] = kh.T
    vh = mm(halo, wv_ref[...]).astype(BF)
    vx[:WIN] = vh
    vhalo_t_ref[...] = vh.T
    kx[WIN:] = k_ref[...]
    vx[WIN:] = v_ref[...]

    pair = 2 * head_size
    tiles = span // TILE
    upper = iota2((pair, TILE), 0) < head_size

    def one_pair(p, carry):
        cols = pl.ds(pl.multiple_of(p * pair, pair), pair)

        def multiply(a):
            here = slice(a * TILE, (a + 1) * TILE)
            keys = slice(a * TILE, a * TILE + REACH)
            scores = mm(kx[keys, cols], both_heads(qt_ref[cols, here], 0, 1))
            slopes = mm(vx[keys, cols], both_heads(dot_ref[cols, here], 0, 1))
            return scores, slopes

        halo_grads = []
        products = {0: multiply(0)}
        for a in range(tiles):
            if a + 1 < tiles:
                products[a + 1] = multiply(a + 1)
            raised, grads, scale = softmax_parts(*products.pop(a), a * TILE, begin, length)
            raised_ref[p * tiles + a] = raised
            grads_ref[p * tiles + a] = grads
            scale_ref[p * tiles + a] = scale
            here = slice(a * TILE, (a + 1) * TILE)
            far = WIN - a * TILE
            spread_scale = jnp.where(upper, scale[:, :TILE], scale[:, TILE:])
            queries = (qt_ref[cols, here].astype(F32) * spread_scale).T.astype(BF)
            slopes = (dot_ref[cols, here].astype(F32) * spread_scale).T.astype(BF)
            q_ref[here, cols] = queries
            do_ref[here, cols] = slopes
            halo_grads.append((
                mm(grads[:far], both_heads(queries, 1, 0)),
                mm(raised[:far], both_heads(slopes, 1, 0)),
            ))
        for which, scale, out in ((0, math.log(2.0), dkh_ref), (1, 1.0, dvh_ref)):
            for j in range(WIN // TILE):
                total = None
                for a in range(min(j + 1, tiles)):
                    piece = halo_grads[a][which][(j - a) * TILE : (j - a + 1) * TILE]
                    total = piece if total is None else total + piece
                out[j * TILE : (j + 1) * TILE, cols] = (total * scale).astype(BF)
        return carry

    lax.fori_loop(0, width // pair, one_pair, 0)
    back_ref[...] = (mm(dkh_ref[...], wk_ref[...], NT) + mm(dvh_ref[...], wv_ref[...], NT)).astype(BF)


def weights_body(
    scale, rows, head_size, meta_ref, normed_ref, halo_ref, frames_ref, cot_ref,
    wq_hbm, wk_hbm, wv_hbm, wo_hbm,
    q_ref, kt_ref, vt_ref, khalo_t_ref, vhalo_t_ref, do_ref, raised_ref, grads_ref, scale_ref, dkh_ref, dvh_ref,
    keep_ref, send_ref, out_ref, slope_ref,
    normed_t, halo_t, mixed_t, ktx, vtx, ot, dqt, dk, dv, wq, wk, wv, wo, sems,
):
    span, width = q_ref.shape
    copies = fetch([wq_hbm, wk_hbm, wv_hbm, wo_hbm], [wq, wk, wv, wo], sems)
    ktx[:, :WIN] = khalo_t_ref[...]
    ktx[:, WIN:] = kt_ref[...]
    vtx[:, :WIN] = vhalo_t_ref[...]
    vtx[:, WIN:] = vt_ref[...]
    pair = 2 * head_size
    tiles = span // TILE
    upper = iota2((pair, TILE), 0) < head_size

    def one_pair(p, carry):
        cols = pl.ds(pl.multiple_of(p * pair, pair), pair)
        own_grads = []
        for a in range(tiles):
            here = slice(a * TILE, (a + 1) * TILE)
            keys = slice(a * TILE, a * TILE + REACH)
            at = p * tiles + a
            shrink = scale_ref[at]
            mixed = mm(vtx[cols, keys], raised_ref[at]) * shrink
            ot[cols, here] = jnp.where(upper, mixed[:, :TILE], mixed[:, TILE:]).astype(BF)
            moved = mm(ktx[cols, keys], grads_ref[at]) * (shrink * head_size ** (-0.5))
            dqt[cols, here] = jnp.where(upper, moved[:, :TILE], moved[:, TILE:]).astype(BF)
            near = slice(WIN - a * TILE, REACH)
            own_grads.append((
                mm(grads_ref[at, near], both_heads(q_ref[here, cols], 1, 0)),
                mm(raised_ref[at, near], both_heads(do_ref[here, cols], 1, 0)),
            ))
        for which, factor, out in ((0, math.log(2.0), dk), (1, 1.0, dv)):
            for j in range(tiles):
                total = None
                for a in range(j, tiles):
                    piece = own_grads[a][which][j * TILE : (j + 1) * TILE]
                    total = piece if total is None else total + piece
                out[j * TILE : (j + 1) * TILE, cols] = (total * factor).astype(BF)
        return carry

    lax.fori_loop(0, width // pair, one_pair, 0)

    chunks = width // (2 * rows)
    split = (chunks, 2, rows, span)
    normed_t[...] = normed_ref[...].T.reshape(split)
    halo_t[...] = halo_ref[...].T.reshape(split)
    mixed_t[...] = ot[...].reshape(split)
    mine = meta_ref[2]
    for side, out in ((1 - mine, send_ref), (mine, keep_ref)):
        own = normed_t[:, side].reshape(width // 2, span)
        far = halo_t[:, side].reshape(width // 2, span)
        mixed = mixed_t[:, side].reshape(width // 2, span)
        for n, total in enumerate((
            mm(own, dqt[...], NT),
            mm(own, dk[...]) + mm(far, dkh_ref[...]),
            mm(own, dv[...]) + mm(far, dvh_ref[...]),
            mm(mixed, cot_ref[...]),
        )):
            out[:, n * width : (n + 1) * width] = (total * scale).astype(BF)
    for copy in copies:
        copy.wait()
    slope = mm(dqt[...].T, wq[...], NT)
    slope = slope + mm(dk[...], wk[...], NT)
    slope_ref[...] = slope + mm(dv[...], wv[...], NT)
    out = mm(ot[...].T, wo[...]) + frames_ref[...].astype(F32)
    out_ref[...] = out.astype(BF)


def returning_body(frames_ref, slope_ref, extra_ref, cot_ref, pick_t_ref, out_ref):
    _, inverse, normed32 = unit_frames(frames_ref[...])
    slope = slope_ref[...] + extra_ref[...].astype(F32)
    centre = jnp.mean(slope * normed32, axis=1, keepdims=True)
    grad = inverse * (slope - normed32 * centre) + cot_ref[...].astype(F32)
    out_ref[...] = mm(pick_t_ref[...], grad.astype(BF)).astype(BF)


def arrived_body(placing_t_ref, in_ref, out_ref):
    out_ref[...] = mm(placing_t_ref[...], in_ref[...]).astype(BF)


def passed_along(shard, by):
    devices = lax.axis_size("seq")
    pairs = [(i, i + by) for i in range(devices) if 0 <= i + by < devices]
    return lax.ppermute(shard, "seq", pairs)


def spread_body(place_ref, *refs):
    parts = refs[0].shape[0]
    inputs, outs = refs[:-parts], refs[-parts:]
    for k, out in enumerate(outs):
        at = place_ref[0] ^ k
        total = inputs[0][at].astype(F32)
        for ref in inputs[1:]:
            total = total + ref[at].astype(F32)
        out[...] = total.astype(BF)


def spread(inputs, place, parts):
    columns = inputs[0].shape[-1]
    inputs = [shard.reshape(parts, -1, columns) for shard in inputs]
    piece = sds(inputs[0].shape[1:])
    return vmem_call(spread_body, [piece] * parts, [place.reshape(1)] + inputs, smem=(0,))


def swapped(pieces, axis, step):
    count = lax.axis_size(axis)
    return [pieces[0]] + [
        lax.ppermute(piece, axis, [(i, i ^ (k * step)) for i in range(count)])
        for k, piece in enumerate(pieces[1:], 1)
    ]


def shards(
    frame_rows, row_frame, frame_owner, lengths,
    query_weight, key_weight, value_weight, out_weight, cotangent,
):
    devices = lax.axis_size(AXES)
    row_count, width = frame_rows.shape
    span = frame_owner.shape[1]
    slots = row_count // devices
    slab = span * lax.axis_size("seq")
    head_size = width // H
    cube = 2 * span * width * width
    square = sds((span, width))
    begin = (lax.axis_index("seq") * span).astype(jnp.int32)
    rows = width // devices
    in_kernel = rows % 16 == 0
    core = (lax.axis_index("seq") & 1).astype(jnp.int32)
    meta = jnp.stack([begin, lengths[0], core if in_kernel else jnp.zeros((), jnp.int32)])
    cot = cotangent[0]

    def exchanged(shard):
        got = lax.all_to_all(
            shard.reshape(devices, slots, width), AXES, split_axis=0, concat_axis=0, tiled=True
        )
        return got.reshape(devices * slots, width)

    outgoing, placing = vmem_call(
        lambda *refs: outgoing_body(span, slots, *refs),
        [square, sds((devices * slots, row_count))],
        [row_frame.reshape(1, row_count), frame_rows],
        hbm=(1,),
        scratch=[pltpu.VMEM((row_count, width), BF), pltpu.SemaphoreType.DMA((1,))],
        flops=cube,
    )
    incoming = exchanged(outgoing)
    pick, pick_t, placing_t, dot = vmem_call(
        lambda *refs: early_body(slots, *refs),
        [square, square, square, sds((width, span))],
        [frame_owner.reshape(span, 1), placing, cot, out_weight],
        flops=2 * cube,
    )
    frames, normed = vmem_call(frames_body, [square, square], [pick, incoming], flops=cube)
    halo = passed_along(normed, 1)
    query_scale = head_size ** (-0.5) * math.log2(math.e)
    qt, k, kt, v, vt, wk, wv = vmem_call(
        lambda *refs: project_body(query_scale, *refs),
        [square] * 7,
        [normed, query_weight, key_weight, value_weight],
        hbm=(1, 2, 3),
        scratch=[pltpu.VMEM((width, width), BF), pltpu.SemaphoreType.DMA((3,))],
        flops=3 * cube,
    )
    units = H // 2 * (span // TILE)
    saved = sds((units, REACH, 2 * TILE))
    raised, grads, scales, q, do, dkh, dvh, khalo_t, vhalo_t, back = vmem_call(
        lambda *refs: scores_body(head_size, *refs),
        [saved, saved, sds((units, 1, 2 * TILE), F32)] + [square] * 7,
        [meta, halo, wk, wv, qt, k, v, dot],
        smem=(0,),
        scratch=[pltpu.VMEM((WIN + span, width), BF)] * 2,
        flops=12 * cube,
        limit=24,
    )
    extra = passed_along(back, -1)
    chunk = rows if in_kernel else width // 2
    split = pltpu.VMEM((width // (2 * chunk), 2, chunk, span), BF)
    half = sds((width // 2, 4 * width))
    whole = pltpu.VMEM((width, width), BF)
    keep, send, out_frames, slope = vmem_call(
        lambda *refs: weights_body(slab ** (-0.5), chunk, head_size, *refs),
        [half, half, square, sds((span, width), F32)],
        [meta, normed, halo, frames, cot, query_weight, key_weight, value_weight, out_weight,
         q, kt, vt, khalo_t, vhalo_t, do, raised, grads, scales, dkh, dvh],
        smem=(0,),
        hbm=(5, 6, 7, 8),
        scratch=[split] * 3 + [pltpu.VMEM((width, WIN + span), BF)] * 2 + [whole] * 8
        + [pltpu.SemaphoreType.DMA((4,))],
        flops=18 * cube,
        limit=26,
    )
    send, extra = lax.optimization_barrier((send, extra))
    if not in_kernel:
        sums = jnp.concatenate([keep, send], axis=0).reshape(-1, 2, rows, 4 * width)
        keep = lax.dynamic_index_in_dim(sums, core, 1, keepdims=False).reshape(half.shape)
        send = lax.dynamic_index_in_dim(sums, 1 - core, 1, keepdims=False).reshape(half.shape)
    seqs = lax.axis_size("seq")
    got = lax.ppermute(send, "seq", [(i, i ^ 1) for i in range(seqs)])
    seqs = lax.axis_size("seq")
    got = lax.ppermute(send, "seq", [(i, i ^ 1) for i in range(seqs)])
    pieces = spread([keep, got], lax.axis_index("stream"), lax.axis_size("stream"))
    *pieces, extra = lax.optimization_barrier((*pieces, extra))
    pieces = swapped(pieces, "stream", 1)
    returning, = vmem_call(
        returning_body, [square], [frames, slope, extra, cot, pick_t], flops=cube
    )
    arrived = exchanged(returning)
    frame_grads, = vmem_call(arrived_body, [square], [placing_t, arrived], flops=cube)
    pieces = swapped(spread(pieces, lax.axis_index("seq") >> 1, seqs // 2), "seq", 2)
    weight_grads = pieces[0].astype(F32)
    for piece in pieces[1:]:
        weight_grads = weight_grads + piece.astype(F32)
    return (out_frames[None], frame_grads, weight_grads)


def solution(mesh):
    return jax.shard_map(
        shards,
        mesh=mesh,
        in_specs=(
            P(AXES, None), P(AXES), P("stream", "seq"), P("stream"),
            P(), P(), P(), P(), P("stream", "seq", None),
        ),
        out_specs=(P("stream", "seq", None), P(AXES, None), P(AXES, None)),
        check_vma=False,
    )
```

```python
import math

import jax
import jax.numpy as jnp
from jax import lax
from jax.experimental import pallas as pl
from jax.experimental.pallas import tpu as pltpu
from jax.sharding import PartitionSpec as P

H = 8
WIN = 512
NEG = -1e30
EPS_NORM = 1e-06
AXES = ("stream", "seq")
BF = jnp.bfloat16
F32 = jnp.float32

NN = (((1,), (0,)), ((), ()))
NT = (((1,), (1,)), ((), ()))


def mm(a, b, dims=NN):
    return lax.dot_general(a, b, dims, preferred_element_type=F32)


def iota2(shape, dim):
    return lax.broadcasted_iota(jnp.int32, shape, dim)


def vmem_call(body, outs, args, smem=(), hbm=(), scratch=(), flops=0, limit=12):
    spaces = [pltpu.SMEM if i in smem else pltpu.HBM if i in hbm else pltpu.VMEM for i in range(len(args))]
    size = sum(math.prod(a.shape) * a.dtype.itemsize for a in list(args) + list(outs))
    return pl.pallas_call(
        body,
        out_shape=tuple(outs),
        in_specs=[pl.BlockSpec(memory_space=space) for space in spaces],
        out_specs=tuple(pl.BlockSpec(memory_space=pltpu.VMEM) for _ in outs),
        scratch_shapes=list(scratch),
        compiler_params=pltpu.CompilerParams(vmem_limit_bytes=limit * 2**20),
        cost_estimate=pl.CostEstimate(flops=flops, bytes_accessed=size, transcendentals=0),
    )(*args)


def fetch(sources, targets, sems):
    copies = [
        pltpu.make_async_copy(source, target, sems.at[n])
        for n, (source, target) in enumerate(zip(sources, targets))
    ]
    for copy in copies:
        copy.start()
    return copies


def sds(shape, dtype=BF):
    return jax.ShapeDtypeStruct(shape, dtype)


def outgoing_body(span, slots, rf_ref, rows_hbm, out_ref, placing_ref, rows_ref, sems):
    (rows_copy,) = fetch([rows_hbm], [rows_ref], sems)
    count = rf_ref.shape[1]
    total = out_ref.shape[0]
    rf = rf_ref[...]
    target = jnp.where(rf >= 0, lax.div(rf, span), 1 << 20)
    slot = iota2((total, count), 0)
    owner = lax.div(slot, slots)
    rank = slot - owner * slots
    start = jnp.sum(jnp.where(target < owner, 1.0, 0.0), axis=1, keepdims=True)
    here = iota2((total, count), 1) - start.astype(jnp.int32)
    placing = jnp.where((target == owner) & (here == rank), 1.0, 0.0).astype(BF)
    placing_ref[...] = placing
    rows_copy.wait()
    out_ref[...] = mm(placing, rows_ref[...]).astype(BF)


def early_body(
    slots, owner_ref, placing_ref, cot_ref, wo_ref, pick_ref, pick_t_ref, placing_t_ref, dot_ref
):
    span, lanes = owner_ref.shape[0], 128
    total = pick_ref.shape[1]
    owner = owner_ref[...]
    device = iota2((span, lanes), 1)
    hot = jnp.where(owner == device, 1.0, 0.0)
    strict = jnp.where(iota2((span, span), 1) < iota2((span, span), 0), 1.0, 0.0).astype(BF)
    before = mm(strict, hot.astype(BF))
    slot = jnp.sum(hot * (before + (device * slots).astype(F32)), axis=1, keepdims=True)
    slot = jnp.where(owner >= 0, slot.astype(jnp.int32), -1)
    pick = jnp.where(iota2((span, total), 1) == slot, 1.0, 0.0)
    pick_ref[...] = pick.astype(BF)
    pick_t_ref[...] = pick.T.astype(BF)
    placing_t_ref[...] = placing_ref[...].T
    dot_ref[...] = mm(cot_ref[...], wo_ref[...], NT).astype(BF).T


def unit_frames(frames):
    frames32 = frames.astype(F32)
    inverse = lax.rsqrt(jnp.mean(frames32 * frames32, axis=1, keepdims=True) + EPS_NORM)
    return frames32, inverse, frames32 * inverse


def frames_body(pick_ref, in_ref, frames_ref, normed_ref):
    frames = mm(pick_ref[...], in_ref[...]).astype(BF)
    frames_ref[...] = frames
    normed_ref[...] = unit_frames(frames)[2].astype(BF)


def project_body(
    query_scale, normed_ref, wq_hbm, wk_hbm, wv_hbm,
    qt_ref, k_ref, kt_ref, v_ref, vt_ref, wk_ref, wv_ref, wq_ref, sems,
):
    copies = fetch([wq_hbm, wk_hbm, wv_hbm], [wq_ref, wk_ref, wv_ref], sems)
    normed = normed_ref[...]
    copies[0].wait()
    qt_ref[...] = (mm(normed, wq_ref[...]) * query_scale).astype(BF).T
    copies[1].wait()
    k = mm(normed, wk_ref[...]).astype(BF)
    k_ref[...] = k
    kt_ref[...] = k.T
    copies[2].wait()
    v = mm(normed, wv_ref[...]).astype(BF)
    v_ref[...] = v
    vt_ref[...] = v.T


TILE = 128
REACH = WIN + TILE


def softmax_parts(scores, slopes, first, begin, length):
    row = iota2((TILE, TILE), 0)
    col = iota2((TILE, TILE), 1)
    halo_bias = jnp.where(begin == 0, NEG, 0.0)
    count = REACH // TILE
    time = begin + first + iota2((1, TILE), 1)
    raised_cols, grad_cols, scales = [], [], []
    for h in range(2):
        at = slice(h * TILE, (h + 1) * TILE)
        parts = []
        for n in range(count):
            part = scores[n * TILE : (n + 1) * TILE, at]
            if n == 0:
                part = jnp.where(row > col, part, NEG)
            if n == count - 1:
                part = jnp.where(row <= col, part, NEG)
            elif first + n * TILE < WIN:
                part = part + halo_bias
            parts.append(part)
        peak = parts[0]
        for part in parts[1:]:
            peak = jnp.maximum(peak, part)
        peak = jnp.max(peak, axis=0, keepdims=True)
        moves = [slopes[n * TILE : (n + 1) * TILE, at] for n in range(count)]
        denom = centre = None
        low_parts = []
        for part, move in zip(parts, moves):
            part = jnp.exp2(part - peak)
            low_parts.append(part.astype(BF))
            moved = part * move
            denom = part if denom is None else denom + part
            centre = moved if centre is None else centre + moved
        denom = jnp.sum(denom, axis=0, keepdims=True)
        centre = jnp.sum(centre, axis=0, keepdims=True) / denom
        scales.append(jnp.where(time < length, 1.0 / denom, 0.0))
        raised_cols.append(jnp.concatenate(low_parts, axis=0))
        grad_cols.append(jnp.concatenate(
            [(part.astype(F32) * (move - centre)).astype(BF) for part, move in zip(low_parts, moves)], axis=0
        ))
    return (
        jnp.concatenate(raised_cols, axis=1), jnp.concatenate(grad_cols, axis=1), jnp.concatenate(scales, axis=1)
    )


def both_heads(value, axis, along):
    place = iota2(value.shape, axis)
    half = value.shape[axis] // 2
    zero = jnp.zeros((), value.dtype)
    return jnp.concatenate([jnp.where(place < half, value, zero), jnp.where(place < half, zero, value)], axis=along)


def load_halves(first, halo_k, halo_v, k_ref, v_ref, kx, vx, khalo_t, vhalo_t):
    cols = slice(first, first + kx.shape[1])
    kx[:WIN] = halo_k
    vx[:WIN] = halo_v
    khalo_t[...] = halo_k.T
    vhalo_t[...] = halo_v.T
    kx[WIN:] = k_ref[:, cols]
    vx[WIN:] = v_ref[:, cols]


def pair_units(first, p, head_size, begin, length, kx, vx, qt_ref, dot_ref, visit):
    pair = 2 * head_size
    upper = iota2((pair, TILE), 0) < head_size
    cols = pl.ds(pl.multiple_of(p * pair, pair), pair)
    feats = pl.ds(pl.multiple_of(first + p * pair, pair), pair)
    tiles = qt_ref.shape[1] // TILE

    def multiply(a):
        here = slice(a * TILE, (a + 1) * TILE)
        keys = slice(a * TILE, a * TILE + REACH)
        scores = mm(kx[keys, cols], both_heads(qt_ref[feats, here], 0, 1))
        slopes = mm(vx[keys, cols], both_heads(dot_ref[feats, here], 0, 1))
        return scores, slopes

    products = {0: multiply(0)}
    for a in range(tiles):
        if a + 1 < tiles:
            products[a + 1] = multiply(a + 1)
        raised, grads, scale = softmax_parts(*products.pop(a), a * TILE, begin, length)
        here = slice(a * TILE, (a + 1) * TILE)
        spread_scale = jnp.where(upper, scale[:, :TILE], scale[:, TILE:])
        queries = (qt_ref[feats, here].astype(F32) * spread_scale).T.astype(BF)
        slopes = (dot_ref[feats, here].astype(F32) * spread_scale).T.astype(BF)
        visit(a, cols, raised, grads, scale, queries, slopes)


def store_sums(parts, offset, low, high, out, cols, scale):
    for j in range(low, high):
        total = None
        for a, part in enumerate(parts):
            at = (j - offset(a)) * TILE
            if 0 <= at < part.shape[0]:
                piece = part[at : at + TILE]
                total = piece if total is None else total + piece
        out[(j - low) * TILE : (j - low + 1) * TILE, cols] = (total * scale).astype(BF)


LN2 = math.log(2.0)


def transposed_products(a, cols, keys_t, raised, grads, shrink, head_size, ktx, vtx, ot, dqt):
    pair = 2 * head_size
    upper = iota2((pair, TILE), 0) < head_size
    here = slice(a * TILE, (a + 1) * TILE)
    mixed = mm(vtx[cols, keys_t], raised) * shrink
    ot[cols, here] = jnp.where(upper, mixed[:, :TILE], mixed[:, TILE:]).astype(BF)
    moved = mm(ktx[cols, keys_t], grads) * (shrink * head_size ** (-0.5))
    dqt[cols, here] = jnp.where(upper, moved[:, :TILE], moved[:, TILE:]).astype(BF)


def side_sums(scale, rows, mine, keep_ref, send_ref, normed_t, halo_t, dqt, dk, dv, dkh, dvh, mixed_t=None, cot=None):
    half = normed_t.shape[0] * rows
    span = normed_t.shape[3]
    for side, out in ((1 - mine, send_ref), (mine, keep_ref)):
        own = normed_t[:, side].reshape(half, span)
        far = halo_t[:, side].reshape(half, span)
        totals = [mm(own, dqt, NT), mm(own, dk) + mm(far, dkh), mm(own, dv) + mm(far, dvh)]
        if mixed_t is not None:
            totals.append(mm(mixed_t[:, side].reshape(half, span), cot))
        at = 0
        for total in totals:
            out[:, at : at + total.shape[1]] = (total * scale).astype(BF)
            at += total.shape[1]


def first_body(
    scale, rows, head_size, meta_ref, halo_ref, wk_ref, wv_ref, qt_ref, k_ref, kt_ref, v_ref, vt_ref,
    dot_hbm, normed_hbm,
    keep_ref, send_ref, mixed_ref, own_ref, far_ref, halo_kv_ref,
    kx, vx, ktx, vtx, dot, normed, normed_t, halo_t, sems,
):
    copies = fetch([dot_hbm, normed_hbm], [dot, normed], sems)
    half = kx.shape[1]
    span = k_ref.shape[0]
    begin, length, mine = meta_ref[0], meta_ref[1], meta_ref[2]
    halo = halo_ref[...]
    kh = mm(halo, wk_ref[...]).astype(BF)
    vh = mm(halo, wv_ref[...]).astype(BF)
    halo_kv_ref[:, :half] = kh[:, half:]
    halo_kv_ref[:, half:] = vh[:, half:]
    load_halves(0, kh[:, :half], vh[:, :half], k_ref, v_ref, kx, vx, ktx.at[:, :WIN], vtx.at[:, :WIN])
    ktx[:, WIN:] = kt_ref[:half]
    vtx[:, WIN:] = vt_ref[:half]
    copies[0].wait()
    pair = 2 * head_size
    tiles = span // TILE

    def one_pair(p, carry):
        grads_k, grads_v = [], []

        def visit(a, cols, raised, grads, shrink, queries, slopes):
            keys_t = slice(a * TILE, a * TILE + REACH)
            transposed_products(
                a, cols, keys_t, raised, grads, shrink, head_size, ktx, vtx,
                mixed_ref.at[:half], mixed_ref.at[half:],
            )
            grads_k.append(mm(grads, both_heads(queries, 1, 0)))
            grads_v.append(mm(raised, both_heads(slopes, 1, 0)))

        pair_units(0, p, head_size, begin, length, kx, vx, qt_ref, dot, visit)
        for parts, factor, start in ((grads_k, LN2, 0), (grads_v, 1.0, half)):
            cols = pl.ds(pl.multiple_of(start + p * pair, pair), pair)
            store_sums(parts, lambda a: a, 0, WIN // TILE, far_ref, cols, factor)
            store_sums(parts, lambda a: a, WIN // TILE, WIN // TILE + tiles, own_ref, cols, factor)
        return carry

    lax.fori_loop(0, half // pair, one_pair, 0)
    copies[1].wait()
    split = normed_t.shape
    normed_t[...] = normed[...].T.reshape(split)
    halo_t[...] = halo.T.reshape(split)
    side_sums(
        scale, rows, mine, keep_ref, send_ref, normed_t, halo_t, mixed_ref[half:],
        own_ref[:, :half], own_ref[:, half:], far_ref[:, :half], far_ref[:, half:],
    )


def second_body(
    head_size, meta_ref, halo_kv_ref, far_one_ref, wk_ref, wv_ref, qt_ref, k_ref, v_ref, dot_hbm,
    raised_ref, grads_ref, scale_ref, q_ref, do_ref, far_ref, khalo_t_ref, vhalo_t_ref, back_ref,
    kx, vx, dot, sems,
):
    copies = fetch([dot_hbm], [dot], sems)
    half = kx.shape[1]
    begin, length = meta_ref[0], meta_ref[1]
    load_halves(
        half, halo_kv_ref[:, :half], halo_kv_ref[:, half:], k_ref, v_ref, kx, vx, khalo_t_ref, vhalo_t_ref
    )
    copies[0].wait()
    pair = 2 * head_size
    tiles = k_ref.shape[0] // TILE

    def one_pair(p, carry):
        grads_k, grads_v = [], []

        def visit(a, cols, raised, grads, scale, queries, slopes):
            raised_ref[p * tiles + a] = raised
            grads_ref[p * tiles + a] = grads
            scale_ref[p * tiles + a] = scale
            here = slice(a * TILE, (a + 1) * TILE)
            q_ref[here, cols] = queries
            do_ref[here, cols] = slopes
            far = WIN - a * TILE
            grads_k.append(mm(grads[:far], both_heads(queries, 1, 0)))
            grads_v.append(mm(raised[:far], both_heads(slopes, 1, 0)))

        pair_units(half, p, head_size, begin, length, kx, vx, qt_ref, dot, visit)
        for parts, factor, start in ((grads_k, LN2, 0), (grads_v, 1.0, half)):
            cols = pl.ds(pl.multiple_of(start + p * pair, pair), pair)
            store_sums(parts, lambda a: a, 0, WIN // TILE, far_ref, cols, factor)
        return carry

    lax.fori_loop(0, half // pair, one_pair, 0)
    back = mm(far_one_ref[:, :half], wk_ref[:, :half], NT) + mm(far_one_ref[:, half:], wv_ref[:, :half], NT)
    back = back + mm(far_ref[:, :half], wk_ref[:, half:], NT)
    back_ref[...] = (back + mm(far_ref[:, half:], wv_ref[:, half:], NT)).astype(BF)


def third_body(
    scale, rows, head_size, meta_ref, normed_hbm, halo_hbm, frames_ref, cot_hbm,
    wq_hbm, wk_hbm, wv_hbm, wo_hbm, mixed_one_hbm, own_one_hbm,
    q_ref, kt_ref, vt_ref, khalo_t_ref, vhalo_t_ref, do_ref, raised_ref, grads_ref, scale_ref, far_ref,
    keep_ref, send_ref, out_ref, slope_ref,
    normed_t, halo_t, mixed_t, ktx, vtx, mixed, dqt, own,
    normed, halo, cot, wq, wk, wv, wo, own_one, sems,
):
    span, half = q_ref.shape
    copies = fetch(
        [normed_hbm, halo_hbm, cot_hbm, wq_hbm, wk_hbm, wv_hbm, wo_hbm, mixed_one_hbm, own_one_hbm],
        [normed, halo, cot, wq, wk, wv, wo, mixed.at[: 2 * half], own_one], sems,
    )
    ktx[:, :WIN] = khalo_t_ref[...]
    ktx[:, WIN:] = kt_ref[half:]
    vtx[:, :WIN] = vhalo_t_ref[...]
    vtx[:, WIN:] = vt_ref[half:]
    pair = 2 * head_size
    tiles = span // TILE
    late = mixed.at[2 * half :]

    def one_pair(p, carry):
        cols = pl.ds(pl.multiple_of(p * pair, pair), pair)
        grads_k, grads_v = [], []
        for a in range(tiles):
            here = slice(a * TILE, (a + 1) * TILE)
            at = p * tiles + a
            transposed_products(
                a, cols, slice(a * TILE, a * TILE + REACH), raised_ref[at], grads_ref[at], scale_ref[at],
                head_size, ktx, vtx, late, dqt,
            )
            near = slice(WIN - a * TILE, REACH)
            grads_k.append(mm(grads_ref[at, near], both_heads(q_ref[here, cols], 1, 0)))
            grads_v.append(mm(raised_ref[at, near], both_heads(do_ref[here, cols], 1, 0)))
        for parts, factor, start in ((grads_k, LN2, 0), (grads_v, 1.0, half)):
            cols = pl.ds(pl.multiple_of(start + p * pair, pair), pair)
            store_sums(parts, lambda a: 0, 0, tiles, own, cols, factor)
        return carry

    lax.fori_loop(0, half // pair, one_pair, 0)
    for copy in copies:
        copy.wait()
    split = normed_t.shape
    normed_t[...] = normed[...].T.reshape(split)
    halo_t[...] = halo[...].T.reshape(split)
    attended_t = jnp.concatenate([mixed[:half], mixed[2 * half :]], axis=0)
    mixed_t[...] = attended_t.reshape(split)
    side_sums(
        scale, rows, meta_ref[2], keep_ref, send_ref, normed_t, halo_t, dqt[...],
        own[:, :half], own[:, half:], far_ref[:, :half], far_ref[:, half:], mixed_t, cot[...],
    )
    query_grad_t = jnp.concatenate([mixed[half : 2 * half], dqt[...]], axis=0)
    slope = mm(query_grad_t.T, wq[...], NT)
    for grads, low in ((own_one, 0), (own, half)):
        slope = slope + mm(grads[:, :half], wk[:, low : low + half], NT)
        slope = slope + mm(grads[:, half:], wv[:, low : low + half], NT)
    slope_ref[...] = slope
    out = mm(attended_t.T, wo[...]) + frames_ref[...].astype(F32)
    out_ref[...] = out.astype(BF)


def returning_body(
    frames_ref, slope_ref, extra_ref, cot_hbm, pick_t_hbm, out_ref, cot_ref, pick_t_ref, sems
):
    copies = fetch([cot_hbm, pick_t_hbm], [cot_ref, pick_t_ref], sems)
    _, inverse, normed32 = unit_frames(frames_ref[...])
    slope = slope_ref[...] + extra_ref[...].astype(F32)
    centre = jnp.mean(slope * normed32, axis=1, keepdims=True)
    copies[0].wait()
    grad = inverse * (slope - normed32 * centre) + cot_ref[...].astype(F32)
    copies[1].wait()
    out_ref[...] = mm(pick_t_ref[...], grad.astype(BF)).astype(BF)


def arrived_body(placing_t_ref, in_ref, out_ref):
    out_ref[...] = mm(placing_t_ref[...], in_ref[...]).astype(BF)


def passed_along(shard, by):
    devices = lax.axis_size("seq")
    pairs = [(i, i + by) for i in range(devices) if 0 <= i + by < devices]
    return lax.ppermute(shard, "seq", pairs)


def spread_body(place_ref, *refs):
    parts = refs[0].shape[0]
    inputs, outs = refs[:-parts], refs[-parts:]
    for k, out in enumerate(outs):
        at = place_ref[0] ^ k
        total = inputs[0][at].astype(F32)
        for ref in inputs[1:]:
            total = total + ref[at].astype(F32)
        out[...] = total.astype(BF)


def spread(inputs, place, parts):
    columns = inputs[0].shape[-1]
    inputs = [shard.reshape(parts, -1, columns) for shard in inputs]
    piece = sds(inputs[0].shape[1:])
    return vmem_call(spread_body, [piece] * parts, [place.reshape(1)] + inputs, smem=(0,))


def spread_late_body(count, place_ref, *refs):
    one, two, outs = refs[:count], refs[count : 2 * count], refs[2 * count :]
    half = one[0].shape[2] // 3
    for k, out in enumerate(outs):
        at = place_ref[0] ^ k
        totals = []
        for group in (one, two):
            total = group[0][at].astype(F32)
            for ref in group[1:]:
                total = total + ref[at].astype(F32)
            totals.append(total.astype(BF))
        for n in range(3):
            out[:, 2 * n * half : (2 * n + 1) * half] = totals[0][:, n * half : (n + 1) * half]
            out[:, (2 * n + 1) * half : (2 * n + 2) * half] = totals[1][:, n * half : (n + 1) * half]
        out[:, 6 * half :] = totals[1][:, 3 * half :]


def spread_late(one, two, place, parts):
    rows = one[0].shape[0] // parts
    columns = one[0].shape[1] + two[0].shape[1]
    inputs = [shard.reshape(parts, rows, -1) for shard in one + two]
    return vmem_call(
        lambda *refs: spread_late_body(len(one), *refs),
        [sds((rows, columns))] * parts,
        [place.reshape(1)] + inputs,
        smem=(0,),
    )


def swapped(pieces, axis, step):
    count = lax.axis_size(axis)
    return [pieces[0]] + [
        lax.ppermute(piece, axis, [(i, i ^ (k * step)) for i in range(count)])
        for k, piece in enumerate(pieces[1:], 1)
    ]


def shards(
    frame_rows, row_frame, frame_owner, lengths,
    query_weight, key_weight, value_weight, out_weight, cotangent,
):
    devices = lax.axis_size(AXES)
    row_count, width = frame_rows.shape
    span = frame_owner.shape[1]
    slots = row_count // devices
    slab = span * lax.axis_size("seq")
    head_size = width // H
    cube = 2 * span * width * width
    square = sds((span, width))
    begin = (lax.axis_index("seq") * span).astype(jnp.int32)
    rows = width // devices
    in_kernel = rows % 16 == 0
    core = (lax.axis_index("seq") & 1).astype(jnp.int32)
    meta = jnp.stack([begin, lengths[0], core if in_kernel else jnp.zeros((), jnp.int32)])
    cot = cotangent[0]

    def exchanged(shard):
        got = lax.all_to_all(
            shard.reshape(devices, slots, width), AXES, split_axis=0, concat_axis=0, tiled=True
        )
        return got.reshape(devices * slots, width)

    outgoing, placing = vmem_call(
        lambda *refs: outgoing_body(span, slots, *refs),
        [square, sds((devices * slots, row_count))],
        [row_frame.reshape(1, row_count), frame_rows],
        hbm=(1,),
        scratch=[pltpu.VMEM((row_count, width), BF), pltpu.SemaphoreType.DMA((1,))],
        flops=cube,
    )
    incoming = exchanged(outgoing)
    pick, pick_t, placing_t, dot = vmem_call(
        lambda *refs: early_body(slots, *refs),
        [square, square, square, sds((width, span))],
        [frame_owner.reshape(span, 1), placing, cot, out_weight],
        flops=2 * cube,
    )
    frames, normed = vmem_call(frames_body, [square, square], [pick, incoming], flops=cube)
    halo = passed_along(normed, 1)
    query_scale = head_size ** (-0.5) * math.log2(math.e)
    qt, k, kt, v, vt, wk, wv = vmem_call(
        lambda *refs: project_body(query_scale, *refs),
        [square] * 7,
        [normed, query_weight, key_weight, value_weight],
        hbm=(1, 2, 3),
        scratch=[pltpu.VMEM((width, width), BF), pltpu.SemaphoreType.DMA((3,))],
        flops=3 * cube,
    )
    seqs, streams = lax.axis_size("seq"), lax.axis_size("stream")
    stream, chip = lax.axis_index("stream"), lax.axis_index("seq") >> 1
    scale = slab ** (-0.5)
    chunk = rows if in_kernel else width // 2
    heads_half = width // 2
    split = pltpu.VMEM((width // (2 * chunk), 2, chunk, span), BF)
    whole = pltpu.VMEM((width, width), BF)
    ext = pltpu.VMEM((WIN + span, heads_half), BF)
    ext_t = pltpu.VMEM((heads_half, WIN + span), BF)

    def by_core(keep, send):
        if in_kernel:
            return keep, send
        sums = jnp.concatenate([keep, send], axis=0).reshape(-1, 2, rows, keep.shape[1])
        return tuple(
            lax.dynamic_index_in_dim(sums, side, 1, keepdims=False).reshape(keep.shape) for side in (core, 1 - core)
        )

    def core_swap(send):
        return lax.ppermute(send, "seq", [(i, i ^ 1) for i in range(seqs)])

    sums = [sds((width // 2, 3 * heads_half))] * 2
    keep, send, mixed_one, own_one, far_one, halo_kv = vmem_call(
        lambda *refs: first_body(scale, chunk, head_size, *refs),
        sums + [square] * 4,
        [meta, halo, wk, wv, qt, k, kt, v, vt, dot, normed],
        smem=(0,),
        hbm=(9, 10),
        scratch=[ext, ext, ext_t, ext_t, whole, whole, split, split, pltpu.SemaphoreType.DMA((2,))],
        flops=14 * cube,
        limit=24,
    )
    keep, send = by_core(keep, send)
    got = core_swap(send)
    units = H // 4 * (span // TILE)
    saved = sds((units, REACH, 2 * TILE))
    tall = sds((span, heads_half))
    wide = sds((heads_half, span))
    raised, grads, scales, q, do, far_two, khalo_t, vhalo_t, back = vmem_call(
        lambda *refs: second_body(head_size, *refs),
        [saved, saved, sds((units, 1, 2 * TILE), F32), tall, tall, square, wide, wide, square],
        [meta, halo_kv, far_one, wk, wv, qt, k, v, dot],
        smem=(0,),
        hbm=(8,),
        scratch=[ext, ext, whole, pltpu.SemaphoreType.DMA((1,))],
        flops=7 * cube,
        limit=24,
    )
    extra = passed_along(back, -1)
    pieces_one = swapped(spread([keep, got], stream, streams), "stream", 1)
    sums = [sds((width // 2, 3 * heads_half + width))] * 2
    keep, send, out_frames, slope = vmem_call(
        lambda *refs: third_body(scale, chunk, head_size, *refs),
        sums + [square, sds((span, width), F32)],
        [meta, normed, halo, frames, cot, query_weight, key_weight, value_weight, out_weight, mixed_one, own_one,
         q, kt, vt, khalo_t, vhalo_t, do, raised, grads, scales, far_two],
        smem=(0,),
        hbm=(1, 2, 4, 5, 6, 7, 8, 9, 10),
        scratch=[split] * 3 + [ext_t, ext_t, pltpu.VMEM((3 * heads_half, span), BF), pltpu.VMEM((heads_half, span), BF)]
        + [whole] * 9 + [pltpu.SemaphoreType.DMA((9,))],
        flops=14 * cube,
        limit=24,
    )
    send, extra, *pieces_one = lax.optimization_barrier((send, extra, *pieces_one))
    keep, send = by_core(keep, send)
    got = core_swap(send)
    returning, = vmem_call(
        returning_body,
        [square],
        [frames, slope, extra, cot, pick_t],
        hbm=(3, 4),
        scratch=[whole, whole, pltpu.SemaphoreType.DMA((2,))],
        flops=cube,
    )
    got, _ = lax.optimization_barrier((got, returning))
    pieces = swapped(spread([keep, got], stream, streams), "stream", 1)
    arrived = exchanged(returning)
    frame_grads, = vmem_call(arrived_body, [square], [placing_t, arrived], flops=cube)
    pieces = swapped(spread_late(pieces_one, pieces, chip, seqs // 2), "seq", 2)
    weight_grads = pieces[0].astype(F32)
    for piece in pieces[1:]:
        weight_grads = weight_grads + piece.astype(F32)
    return (out_frames[None], frame_grads, weight_grads)


def solution(mesh):
    return jax.shard_map(
        shards,
        mesh=mesh,
        in_specs=(
            P(AXES, None), P(AXES), P("stream", "seq"), P("stream"),
            P(), P(), P(), P(), P("stream", "seq", None),
        ),
        out_specs=(P("stream", "seq", None), P(AXES, None), P(AXES, None)),
        check_vma=False,
    )
```

```python
import math

import jax
import jax.numpy as jnp
from jax import lax
from jax.experimental import pallas as pl
from jax.experimental.pallas import tpu as pltpu
from jax.sharding import PartitionSpec as P

H = 8
WIN = 512
NEG = -1e30
EPS_NORM = 1e-06
AXES = ("stream", "seq")
BF = jnp.bfloat16
F32 = jnp.float32

NN = (((1,), (0,)), ((), ()))
NT = (((1,), (1,)), ((), ()))


def mm(a, b, dims=NN):
    return lax.dot_general(a, b, dims, preferred_element_type=F32)


def iota2(shape, dim):
    return lax.broadcasted_iota(jnp.int32, shape, dim)


def vmem_call(body, outs, args, smem=(), hbm=(), scratch=(), carry=(), flops=0, limit=12):
    used, inner, args = len(args), body, list(args) + list(carry)

    def body(*refs):
        inner(*refs[:used], *refs[len(args) :])

    spaces = [pltpu.SMEM if i in smem else pltpu.HBM if i in hbm else pltpu.VMEM for i in range(len(args))]
    size = sum(math.prod(a.shape) * a.dtype.itemsize for a in list(args) + list(outs))
    return pl.pallas_call(
        body,
        out_shape=tuple(outs),
        in_specs=[pl.BlockSpec(memory_space=space) for space in spaces],
        out_specs=tuple(pl.BlockSpec(memory_space=pltpu.VMEM) for _ in outs),
        scratch_shapes=list(scratch),
        compiler_params=pltpu.CompilerParams(vmem_limit_bytes=limit * 2**20),
        cost_estimate=pl.CostEstimate(flops=flops, bytes_accessed=size, transcendentals=0),
    )(*args)


def fetch(sources, targets, sems):
    copies = [
        pltpu.make_async_copy(source, target, sems.at[n])
        for n, (source, target) in enumerate(zip(sources, targets))
    ]
    for copy in copies:
        copy.start()
    return copies


def sds(shape, dtype=BF):
    return jax.ShapeDtypeStruct(shape, dtype)


def outgoing_body(span, slots, rf_ref, rows_hbm, out_ref, placing_ref, rows_ref, sems):
    (rows_copy,) = fetch([rows_hbm], [rows_ref], sems)
    count = rf_ref.shape[1]
    total = out_ref.shape[0]
    rf = rf_ref[...]
    target = jnp.where(rf >= 0, lax.div(rf, span), 1 << 20)
    slot = iota2((total, count), 0)
    owner = lax.div(slot, slots)
    rank = slot - owner * slots
    start = jnp.sum(jnp.where(target < owner, 1.0, 0.0), axis=1, keepdims=True)
    here = iota2((total, count), 1) - start.astype(jnp.int32)
    placing = jnp.where((target == owner) & (here == rank), 1.0, 0.0).astype(BF)
    placing_ref[...] = placing
    rows_copy.wait()
    out_ref[...] = mm(placing, rows_ref[...]).astype(BF)


def early_body(
    slots, owner_ref, placing_ref, cot_ref, wo_ref, pick_ref, pick_t_ref, placing_t_ref, dot_ref
):
    span, lanes = owner_ref.shape[0], 128
    total = pick_ref.shape[1]
    owner = owner_ref[...]
    device = iota2((span, lanes), 1)
    hot = jnp.where(owner == device, 1.0, 0.0)
    strict = jnp.where(iota2((span, span), 1) < iota2((span, span), 0), 1.0, 0.0).astype(BF)
    before = mm(strict, hot.astype(BF))
    slot = jnp.sum(hot * (before + (device * slots).astype(F32)), axis=1, keepdims=True)
    slot = jnp.where(owner >= 0, slot.astype(jnp.int32), -1)
    pick = jnp.where(iota2((span, total), 1) == slot, 1.0, 0.0)
    pick_ref[...] = pick.astype(BF)
    pick_t_ref[...] = pick.T.astype(BF)
    placing_t_ref[...] = placing_ref[...].T
    dot_ref[...] = mm(cot_ref[...], wo_ref[...], NT).astype(BF).T


def unit_frames(frames):
    frames32 = frames.astype(F32)
    inverse = lax.rsqrt(jnp.mean(frames32 * frames32, axis=1, keepdims=True) + EPS_NORM)
    return frames32, inverse, frames32 * inverse


def frames_body(pick_ref, in_ref, frames_ref, normed_ref):
    frames = mm(pick_ref[...], in_ref[...]).astype(BF)
    frames_ref[...] = frames
    normed_ref[...] = unit_frames(frames)[2].astype(BF)


def project_body(
    query_scale, normed_ref, wq_hbm, wk_hbm, wv_hbm,
    qt_ref, k_ref, kt_ref, v_ref, vt_ref, wk_ref, wv_ref, wq_ref, sems,
):
    copies = fetch([wq_hbm, wk_hbm, wv_hbm], [wq_ref, wk_ref, wv_ref], sems)
    normed = normed_ref[...]
    copies[0].wait()
    qt_ref[...] = (mm(normed, wq_ref[...]) * query_scale).astype(BF).T
    copies[1].wait()
    k = mm(normed, wk_ref[...]).astype(BF)
    k_ref[...] = k
    kt_ref[...] = k.T
    copies[2].wait()
    v = mm(normed, wv_ref[...]).astype(BF)
    v_ref[...] = v
    vt_ref[...] = v.T


TILE = 128
REACH = WIN + TILE


def softmax_parts(scores, slopes, first, begin, length):
    row = iota2((TILE, TILE), 0)
    col = iota2((TILE, TILE), 1)
    halo_bias = jnp.where(begin == 0, NEG, 0.0)
    count = REACH // TILE
    time = begin + first + iota2((1, TILE), 1)
    raised_cols, grad_cols, scales = [], [], []
    for h in range(2):
        at = slice(h * TILE, (h + 1) * TILE)
        parts = []
        for n in range(count):
            part = scores[n * TILE : (n + 1) * TILE, at]
            if n == 0:
                part = jnp.where(row > col, part, NEG)
            if n == count - 1:
                part = jnp.where(row <= col, part, NEG)
            elif first + n * TILE < WIN:
                part = part + halo_bias
            parts.append(part)
        peak = parts[0]
        for part in parts[1:]:
            peak = jnp.maximum(peak, part)
        peak = jnp.max(peak, axis=0, keepdims=True)
        moves = [slopes[n * TILE : (n + 1) * TILE, at] for n in range(count)]
        denom = centre = None
        low_parts = []
        for part, move in zip(parts, moves):
            part = jnp.exp2(part - peak)
            low_parts.append(part.astype(BF))
            moved = part * move
            denom = part if denom is None else denom + part
            centre = moved if centre is None else centre + moved
        denom = jnp.sum(denom, axis=0, keepdims=True)
        centre = jnp.sum(centre, axis=0, keepdims=True) / denom
        scales.append(jnp.where(time < length, 1.0 / denom, 0.0))
        raised_cols.append(jnp.concatenate(low_parts, axis=0))
        grad_cols.append(jnp.concatenate(
            [(part.astype(F32) * (move - centre)).astype(BF) for part, move in zip(low_parts, moves)], axis=0
        ))
    return (
        jnp.concatenate(raised_cols, axis=1), jnp.concatenate(grad_cols, axis=1), jnp.concatenate(scales, axis=1)
    )


def both_heads(value, axis, along):
    place = iota2(value.shape, axis)
    half = value.shape[axis] // 2
    zero = jnp.zeros((), value.dtype)
    return jnp.concatenate([jnp.where(place < half, value, zero), jnp.where(place < half, zero, value)], axis=along)


def scores_body(
    head_size, meta_ref, halo_ref, wk_ref, wv_ref, qt_ref, k_ref, v_ref, dot_ref,
    raised_ref, grads_ref, scale_ref, q_ref, do_ref, dkh_ref, dvh_ref, khalo_t_ref, vhalo_t_ref, back_ref,
    kx, vx,
):
    span, width = k_ref.shape
    begin, length = meta_ref[0], meta_ref[1]
    halo = halo_ref[...]
    kh = mm(halo, wk_ref[...]).astype(BF)
    kx[:WIN] = kh
    khalo_t_ref[...] = kh.T
    vh = mm(halo, wv_ref[...]).astype(BF)
    vx[:WIN] = vh
    vhalo_t_ref[...] = vh.T
    kx[WIN:] = k_ref[...]
    vx[WIN:] = v_ref[...]

    pair = 2 * head_size
    tiles = span // TILE
    upper = iota2((pair, TILE), 0) < head_size

    def one_pair(p, carry):
        cols = pl.ds(pl.multiple_of(p * pair, pair), pair)

        def multiply(a):
            here = slice(a * TILE, (a + 1) * TILE)
            keys = slice(a * TILE, a * TILE + REACH)
            scores = mm(kx[keys, cols], both_heads(qt_ref[cols, here], 0, 1))
            slopes = mm(vx[keys, cols], both_heads(dot_ref[cols, here], 0, 1))
            return scores, slopes

        halo_grads = []
        products = {0: multiply(0)}
        for a in range(tiles):
            if a + 1 < tiles:
                products[a + 1] = multiply(a + 1)
            raised, grads, scale = softmax_parts(*products.pop(a), a * TILE, begin, length)
            raised_ref[p * tiles + a] = raised
            grads_ref[p * tiles + a] = grads
            scale_ref[p * tiles + a] = scale
            here = slice(a * TILE, (a + 1) * TILE)
            far = WIN - a * TILE
            spread_scale = jnp.where(upper, scale[:, :TILE], scale[:, TILE:])
            queries = (qt_ref[cols, here].astype(F32) * spread_scale).T.astype(BF)
            slopes = (dot_ref[cols, here].astype(F32) * spread_scale).T.astype(BF)
            q_ref[here, cols] = queries
            do_ref[here, cols] = slopes
            halo_grads.append((
                mm(grads[:far], both_heads(queries, 1, 0)),
                mm(raised[:far], both_heads(slopes, 1, 0)),
            ))
        for which, scale, out in ((0, math.log(2.0), dkh_ref), (1, 1.0, dvh_ref)):
            for j in range(WIN // TILE):
                total = None
                for a in range(min(j + 1, tiles)):
                    piece = halo_grads[a][which][(j - a) * TILE : (j - a + 1) * TILE]
                    total = piece if total is None else total + piece
                out[j * TILE : (j + 1) * TILE, cols] = (total * scale).astype(BF)
        return carry

    lax.fori_loop(0, width // pair, one_pair, 0)
    back_ref[...] = (mm(dkh_ref[...], wk_ref[...], NT) + mm(dvh_ref[...], wv_ref[...], NT)).astype(BF)


def weights_body(
    scale, rows, head_size, meta_ref, normed_ref, halo_ref, frames_ref, cot_ref,
    wq_hbm, wk_hbm, wv_hbm, wo_hbm,
    q_ref, kt_ref, vt_ref, khalo_t_ref, vhalo_t_ref, do_ref, raised_ref, grads_ref, scale_ref, dkh_ref, dvh_ref,
    keep_ref, send_ref, out_ref, slope_ref,
    normed_t, halo_t, mixed_t, ktx, vtx, ot, dqt, dk, dv, wq, wk, wv, wo, sems,
):
    span, width = q_ref.shape
    copies = fetch([wq_hbm, wk_hbm, wv_hbm, wo_hbm], [wq, wk, wv, wo], sems)
    ktx[:, :WIN] = khalo_t_ref[...]
    ktx[:, WIN:] = kt_ref[...]
    vtx[:, :WIN] = vhalo_t_ref[...]
    vtx[:, WIN:] = vt_ref[...]
    pair = 2 * head_size
    tiles = span // TILE
    upper = iota2((pair, TILE), 0) < head_size

    def one_pair(p, carry):
        cols = pl.ds(pl.multiple_of(p * pair, pair), pair)
        own_grads = []
        for a in range(tiles):
            here = slice(a * TILE, (a + 1) * TILE)
            keys = slice(a * TILE, a * TILE + REACH)
            at = p * tiles + a
            shrink = scale_ref[at]
            mixed = mm(vtx[cols, keys], raised_ref[at]) * shrink
            ot[cols, here] = jnp.where(upper, mixed[:, :TILE], mixed[:, TILE:]).astype(BF)
            moved = mm(ktx[cols, keys], grads_ref[at]) * (shrink * head_size ** (-0.5))
            dqt[cols, here] = jnp.where(upper, moved[:, :TILE], moved[:, TILE:]).astype(BF)
            near = slice(WIN - a * TILE, REACH)
            own_grads.append((
                mm(grads_ref[at, near], both_heads(q_ref[here, cols], 1, 0)),
                mm(raised_ref[at, near], both_heads(do_ref[here, cols], 1, 0)),
            ))
        for which, factor, out in ((0, math.log(2.0), dk), (1, 1.0, dv)):
            for j in range(tiles):
                total = None
                for a in range(j, tiles):
                    piece = own_grads[a][which][j * TILE : (j + 1) * TILE]
                    total = piece if total is None else total + piece
                out[j * TILE : (j + 1) * TILE, cols] = (total * factor).astype(BF)
        return carry

    lax.fori_loop(0, width // pair, one_pair, 0)

    chunks = width // (2 * rows)
    split = (chunks, 2, rows, span)
    normed_t[...] = normed_ref[...].T.reshape(split)
    halo_t[...] = halo_ref[...].T.reshape(split)
    mixed_t[...] = ot[...].reshape(split)
    mine = meta_ref[2]
    for side, out in ((1 - mine, send_ref), (mine, keep_ref)):
        own = normed_t[:, side].reshape(width // 2, span)
        far = halo_t[:, side].reshape(width // 2, span)
        mixed = mixed_t[:, side].reshape(width // 2, span)
        for n, total in enumerate((
            mm(own, dqt[...], NT),
            mm(own, dk[...]) + mm(far, dkh_ref[...]),
            mm(own, dv[...]) + mm(far, dvh_ref[...]),
            mm(mixed, cot_ref[...]),
        )):
            out[:, n * width : (n + 1) * width] = (total * scale).astype(BF)
    for copy in copies:
        copy.wait()
    slope = mm(dqt[...].T, wq[...], NT)
    slope = slope + mm(dk[...], wk[...], NT)
    slope_ref[...] = slope + mm(dv[...], wv[...], NT)
    out = mm(ot[...].T, wo[...]) + frames_ref[...].astype(F32)
    out_ref[...] = out.astype(BF)


def returning_body(frames_ref, slope_ref, extra_ref, cot_ref, pick_t_ref, out_ref):
    _, inverse, normed32 = unit_frames(frames_ref[...])
    slope = slope_ref[...] + extra_ref[...].astype(F32)
    centre = jnp.mean(slope * normed32, axis=1, keepdims=True)
    grad = inverse * (slope - normed32 * centre) + cot_ref[...].astype(F32)
    out_ref[...] = mm(pick_t_ref[...], grad.astype(BF)).astype(BF)


def arrived_body(placing_t_ref, in_ref, out_ref):
    out_ref[...] = mm(placing_t_ref[...], in_ref[...]).astype(BF)


def passed_along(shard, by):
    devices = lax.axis_size("seq")
    pairs = [(i, i + by) for i in range(devices) if 0 <= i + by < devices]
    return lax.ppermute(shard, "seq", pairs)


def spread_body(place_ref, *refs):
    parts = refs[0].shape[0]
    inputs, outs = refs[:-parts], refs[-parts:]
    for k, out in enumerate(outs):
        at = place_ref[0] ^ k
        total = inputs[0][at].astype(F32)
        for ref in inputs[1:]:
            total = total + ref[at].astype(F32)
        out[...] = total.astype(BF)


def spread(inputs, place, parts, carry=()):
    columns = inputs[0].shape[-1]
    inputs = [shard.reshape(parts, -1, columns) for shard in inputs]
    piece = sds(inputs[0].shape[1:])
    return vmem_call(spread_body, [piece] * parts, [place.reshape(1)] + inputs, smem=(0,), carry=carry)


def swapped(pieces, axis, step):
    count = lax.axis_size(axis)
    return [pieces[0]] + [
        lax.ppermute(piece, axis, [(i, i ^ (k * step)) for i in range(count)])
        for k, piece in enumerate(pieces[1:], 1)
    ]


def shards(
    frame_rows, row_frame, frame_owner, lengths,
    query_weight, key_weight, value_weight, out_weight, cotangent,
):
    devices = lax.axis_size(AXES)
    row_count, width = frame_rows.shape
    span = frame_owner.shape[1]
    slots = row_count // devices
    slab = span * lax.axis_size("seq")
    head_size = width // H
    cube = 2 * span * width * width
    square = sds((span, width))
    begin = (lax.axis_index("seq") * span).astype(jnp.int32)
    rows = width // devices
    in_kernel = rows % 16 == 0
    core = (lax.axis_index("seq") & 1).astype(jnp.int32)
    meta = jnp.stack([begin, lengths[0], core if in_kernel else jnp.zeros((), jnp.int32)])
    cot = cotangent[0]

    def exchanged(shard):
        got = lax.all_to_all(
            shard.reshape(devices, slots, width), AXES, split_axis=0, concat_axis=0, tiled=True
        )
        return got.reshape(devices * slots, width)

    outgoing, placing = vmem_call(
        lambda *refs: outgoing_body(span, slots, *refs),
        [square, sds((devices * slots, row_count))],
        [row_frame.reshape(1, row_count), frame_rows],
        hbm=(1,),
        scratch=[pltpu.VMEM((row_count, width), BF), pltpu.SemaphoreType.DMA((1,))],
        flops=cube,
    )
    incoming = exchanged(outgoing)
    pick, pick_t, placing_t, dot = vmem_call(
        lambda *refs: early_body(slots, *refs),
        [square, square, square, sds((width, span))],
        [frame_owner.reshape(span, 1), placing, cot, out_weight],
        flops=2 * cube,
    )
    frames, normed = vmem_call(
        frames_body, [square, square], [pick, incoming], carry=[pick_t, placing_t, dot], flops=cube
    )
    halo = passed_along(normed, 1)
    query_scale = head_size ** (-0.5) * math.log2(math.e)
    qt, k, kt, v, vt, wk, wv = vmem_call(
        lambda *refs: project_body(query_scale, *refs),
        [square] * 7,
        [normed, query_weight, key_weight, value_weight],
        hbm=(1, 2, 3),
        scratch=[pltpu.VMEM((width, width), BF), pltpu.SemaphoreType.DMA((3,))],
        carry=[pick_t, placing_t, dot, frames],
        flops=3 * cube,
    )
    units = H // 2 * (span // TILE)
    saved = sds((units, REACH, 2 * TILE))
    raised, grads, scales, q, do, dkh, dvh, khalo_t, vhalo_t, back = vmem_call(
        lambda *refs: scores_body(head_size, *refs),
        [saved, saved, sds((units, 1, 2 * TILE), F32)] + [square] * 7,
        [meta, halo, wk, wv, qt, k, v, dot],
        smem=(0,),
        scratch=[pltpu.VMEM((WIN + span, width), BF)] * 2,
        carry=[normed, kt, vt, frames, pick_t, placing_t],
        flops=12 * cube,
        limit=24,
    )
    extra = passed_along(back, -1)
    chunk = rows if in_kernel else width // 2
    split = pltpu.VMEM((width // (2 * chunk), 2, chunk, span), BF)
    half = sds((width // 2, 4 * width))
    whole = pltpu.VMEM((width, width), BF)
    keep, send, out_frames, slope = vmem_call(
        lambda *refs: weights_body(slab ** (-0.5), chunk, head_size, *refs),
        [half, half, square, sds((span, width), F32)],
        [meta, normed, halo, frames, cot, query_weight, key_weight, value_weight, out_weight,
         q, kt, vt, khalo_t, vhalo_t, do, raised, grads, scales, dkh, dvh],
        smem=(0,),
        hbm=(5, 6, 7, 8),
        scratch=[split] * 3 + [pltpu.VMEM((width, WIN + span), BF)] * 2 + [whole] * 8
        + [pltpu.SemaphoreType.DMA((4,))],
        carry=[pick_t, placing_t],
        flops=18 * cube,
        limit=26,
    )
    send, extra = lax.optimization_barrier((send, extra))
    if not in_kernel:
        sums = jnp.concatenate([keep, send], axis=0).reshape(-1, 2, rows, 4 * width)
        keep = lax.dynamic_index_in_dim(sums, core, 1, keepdims=False).reshape(half.shape)
        send = lax.dynamic_index_in_dim(sums, 1 - core, 1, keepdims=False).reshape(half.shape)
    seqs = lax.axis_size("seq")
    got = lax.ppermute(send, "seq", [(i, i ^ 1) for i in range(seqs)])
    seqs = lax.axis_size("seq")
    got = lax.ppermute(send, "seq", [(i, i ^ 1) for i in range(seqs)])
    returning, = vmem_call(
        returning_body, [square], [frames, slope, extra, cot, pick_t], carry=[placing_t, keep], flops=cube
    )
    got, _ = lax.optimization_barrier((got, returning))
    pieces = spread([keep, got], lax.axis_index("stream"), lax.axis_size("stream"), [placing_t])
    pieces = swapped(pieces, "stream", 1)
    arrived = exchanged(returning)
    frame_grads, = vmem_call(arrived_body, [square], [placing_t, arrived], flops=cube)
    pieces = swapped(spread(pieces, lax.axis_index("seq") >> 1, seqs // 2), "seq", 2)
    weight_grads = pieces[0].astype(F32)
    for piece in pieces[1:]:
        weight_grads = weight_grads + piece.astype(F32)
    return (out_frames[None], frame_grads, weight_grads)


def solution(mesh):
    return jax.shard_map(
        shards,
        mesh=mesh,
        in_specs=(
            P(AXES, None), P(AXES), P("stream", "seq"), P("stream"),
            P(), P(), P(), P(), P("stream", "seq", None),
        ),
        out_specs=(P("stream", "seq", None), P(AXES, None), P(AXES, None)),
        check_vma=False,
    )
```

```python
import math

import jax
import jax.numpy as jnp
from jax import lax
from jax.experimental import pallas as pl
from jax.experimental.pallas import tpu as pltpu
from jax.sharding import PartitionSpec as P

H = 8
WIN = 512
NEG = -1e30
EPS_NORM = 1e-06
AXES = ("stream", "seq")
BF = jnp.bfloat16
F32 = jnp.float32

NN = (((1,), (0,)), ((), ()))
NT = (((1,), (1,)), ((), ()))


def mm(a, b, dims=NN):
    return lax.dot_general(a, b, dims, preferred_element_type=F32)


def iota2(shape, dim):
    return lax.broadcasted_iota(jnp.int32, shape, dim)


def vmem_call(body, outs, args, smem=(), hbm=(), scratch=(), flops=0, limit=12):
    spaces = [pltpu.SMEM if i in smem else pltpu.HBM if i in hbm else pltpu.VMEM for i in range(len(args))]
    size = sum(math.prod(a.shape) * a.dtype.itemsize for a in list(args) + list(outs))
    return pl.pallas_call(
        body,
        out_shape=tuple(outs),
        in_specs=[pl.BlockSpec(memory_space=space) for space in spaces],
        out_specs=tuple(pl.BlockSpec(memory_space=pltpu.VMEM) for _ in outs),
        scratch_shapes=list(scratch),
        compiler_params=pltpu.CompilerParams(vmem_limit_bytes=limit * 2**20),
        cost_estimate=pl.CostEstimate(flops=flops, bytes_accessed=size, transcendentals=0),
    )(*args)


def fetch(sources, targets, sems):
    copies = [
        pltpu.make_async_copy(source, target, sems.at[n])
        for n, (source, target) in enumerate(zip(sources, targets))
    ]
    for copy in copies:
        copy.start()
    return copies


def sds(shape, dtype=BF):
    return jax.ShapeDtypeStruct(shape, dtype)


def placing_of(span, slots, rf, total):
    count = rf.shape[1]
    target = jnp.where(rf >= 0, lax.div(rf, span), 1 << 20)
    slot = iota2((total, count), 0)
    owner = lax.div(slot, slots)
    rank = slot - owner * slots
    start = jnp.sum(jnp.where(target < owner, 1.0, 0.0), axis=1, keepdims=True)
    here = iota2((total, count), 1) - start.astype(jnp.int32)
    return jnp.where((target == owner) & (here == rank), 1.0, 0.0)


def outgoing_body(span, slots, rf_ref, rows_hbm, out_ref, rows_ref, sems):
    (rows_copy,) = fetch([rows_hbm], [rows_ref], sems)
    placing = placing_of(span, slots, rf_ref[...], out_ref.shape[0]).astype(BF)
    rows_copy.wait()
    out_ref[...] = mm(placing, rows_ref[...]).astype(BF)


def placing_t_body(span, slots, rf_ref, out_ref):
    out_ref[...] = placing_of(span, slots, rf_ref[...], out_ref.shape[1]).T.astype(BF)


def early_body(slots, owner_ref, pick_ref, pick_t_ref):
    span, lanes = owner_ref.shape[0], 128
    total = pick_ref.shape[1]
    owner = owner_ref[...]
    device = iota2((span, lanes), 1)
    hot = jnp.where(owner == device, 1.0, 0.0)
    strict = jnp.where(iota2((span, span), 1) < iota2((span, span), 0), 1.0, 0.0).astype(BF)
    before = mm(strict, hot.astype(BF))
    slot = jnp.sum(hot * (before + (device * slots).astype(F32)), axis=1, keepdims=True)
    slot = jnp.where(owner >= 0, slot.astype(jnp.int32), -1)
    pick = jnp.where(iota2((span, total), 1) == slot, 1.0, 0.0)
    pick_ref[...] = pick.astype(BF)
    pick_t_ref[...] = pick.T.astype(BF)


def unit_frames(frames):
    frames32 = frames.astype(F32)
    inverse = lax.rsqrt(jnp.mean(frames32 * frames32, axis=1, keepdims=True) + EPS_NORM)
    return frames32, inverse, frames32 * inverse


def frames_body(pick_ref, in_ref, frames_ref, normed_ref):
    frames = mm(pick_ref[...], in_ref[...]).astype(BF)
    frames_ref[...] = frames
    normed_ref[...] = unit_frames(frames)[2].astype(BF)


def project_body(
    query_scale, normed_ref, wq_hbm, wk_hbm, wv_hbm,
    qt_ref, k_ref, kt_ref, v_ref, vt_ref, wk_ref, wv_ref, wq_ref, sems,
):
    copies = fetch([wq_hbm, wk_hbm, wv_hbm], [wq_ref, wk_ref, wv_ref], sems)
    normed = normed_ref[...]
    copies[0].wait()
    qt_ref[...] = (mm(normed, wq_ref[...]) * query_scale).astype(BF).T
    copies[1].wait()
    k = mm(normed, wk_ref[...]).astype(BF)
    k_ref[...] = k
    kt_ref[...] = k.T
    copies[2].wait()
    v = mm(normed, wv_ref[...]).astype(BF)
    v_ref[...] = v
    vt_ref[...] = v.T


TILE = 128
REACH = WIN + TILE


def softmax_parts(scores, slopes, first, begin, length):
    row = iota2((TILE, TILE), 0)
    col = iota2((TILE, TILE), 1)
    halo_bias = jnp.where(begin == 0, NEG, 0.0)
    count = REACH // TILE
    time = begin + first + iota2((1, TILE), 1)
    raised_cols, grad_cols, scales = [], [], []
    for h in range(2):
        at = slice(h * TILE, (h + 1) * TILE)
        parts = []
        for n in range(count):
            part = scores[n * TILE : (n + 1) * TILE, at]
            if n == 0:
                part = jnp.where(row > col, part, NEG)
            if n == count - 1:
                part = jnp.where(row <= col, part, NEG)
            elif first + n * TILE < WIN:
                part = part + halo_bias
            parts.append(part)
        peak = parts[0]
        for part in parts[1:]:
            peak = jnp.maximum(peak, part)
        peak = jnp.max(peak, axis=0, keepdims=True)
        moves = [slopes[n * TILE : (n + 1) * TILE, at] for n in range(count)]
        denom = centre = None
        low_parts = []
        for part, move in zip(parts, moves):
            part = jnp.exp2(part - peak)
            low_parts.append(part.astype(BF))
            moved = part * move
            denom = part if denom is None else denom + part
            centre = moved if centre is None else centre + moved
        denom = jnp.sum(denom, axis=0, keepdims=True)
        centre = jnp.sum(centre, axis=0, keepdims=True) / denom
        scales.append(jnp.where(time < length, 1.0 / denom, 0.0))
        raised_cols.append(jnp.concatenate(low_parts, axis=0))
        grad_cols.append(jnp.concatenate(
            [(part.astype(F32) * (move - centre)).astype(BF) for part, move in zip(low_parts, moves)], axis=0
        ))
    return (
        jnp.concatenate(raised_cols, axis=1), jnp.concatenate(grad_cols, axis=1), jnp.concatenate(scales, axis=1)
    )


def both_heads(value, axis, along):
    place = iota2(value.shape, axis)
    half = value.shape[axis] // 2
    zero = jnp.zeros((), value.dtype)
    return jnp.concatenate([jnp.where(place < half, value, zero), jnp.where(place < half, zero, value)], axis=along)


def scores_body(
    head_size, meta_ref, halo_ref, wk_ref, wv_ref, qt_ref, k_ref, v_ref, cot_hbm, wo_hbm,
    raised_ref, grads_ref, scale_ref, q_ref, do_ref, dkh_ref, dvh_ref, khalo_t_ref, vhalo_t_ref, back_ref,
    kx, vx, dot_ref, cot_ref, wo_ref, sems,
):
    copies = fetch([cot_hbm, wo_hbm], [cot_ref, wo_ref], sems)
    span, width = k_ref.shape
    begin, length = meta_ref[0], meta_ref[1]
    halo = halo_ref[...]
    kh = mm(halo, wk_ref[...]).astype(BF)
    kx[:WIN] = kh
    khalo_t_ref[...] = kh.T
    vh = mm(halo, wv_ref[...]).astype(BF)
    vx[:WIN] = vh
    vhalo_t_ref[...] = vh.T
    kx[WIN:] = k_ref[...]
    vx[WIN:] = v_ref[...]

    pair = 2 * head_size
    tiles = span // TILE
    upper = iota2((pair, TILE), 0) < head_size

    def one_pair(p, carry):
        cols = pl.ds(pl.multiple_of(p * pair, pair), pair)

        def multiply(a):
            here = slice(a * TILE, (a + 1) * TILE)
            keys = slice(a * TILE, a * TILE + REACH)
            scores = mm(kx[keys, cols], both_heads(qt_ref[cols, here], 0, 1))
            slopes = mm(vx[keys, cols], both_heads(dot_ref[cols, here], 0, 1))
            return scores, slopes

        halo_grads = []
        products = {0: multiply(0)}
        for a in range(tiles):
            if a + 1 < tiles:
                products[a + 1] = multiply(a + 1)
            raised, grads, scale = softmax_parts(*products.pop(a), a * TILE, begin, length)
            raised_ref[p * tiles + a] = raised
            grads_ref[p * tiles + a] = grads
            scale_ref[p * tiles + a] = scale
            here = slice(a * TILE, (a + 1) * TILE)
            far = WIN - a * TILE
            spread_scale = jnp.where(upper, scale[:, :TILE], scale[:, TILE:])
            queries = (qt_ref[cols, here].astype(F32) * spread_scale).T.astype(BF)
            slopes = (dot_ref[cols, here].astype(F32) * spread_scale).T.astype(BF)
            q_ref[here, cols] = queries
            do_ref[here, cols] = slopes
            halo_grads.append((
                mm(grads[:far], both_heads(queries, 1, 0)),
                mm(raised[:far], both_heads(slopes, 1, 0)),
            ))
        for which, scale, out in ((0, math.log(2.0), dkh_ref), (1, 1.0, dvh_ref)):
            for j in range(WIN // TILE):
                total = None
                for a in range(min(j + 1, tiles)):
                    piece = halo_grads[a][which][(j - a) * TILE : (j - a + 1) * TILE]
                    total = piece if total is None else total + piece
                out[j * TILE : (j + 1) * TILE, cols] = (total * scale).astype(BF)
        return carry

    for copy in copies:
        copy.wait()
    dot_ref[...] = mm(cot_ref[...], wo_ref[...], NT).astype(BF).T
    lax.fori_loop(0, width // pair, one_pair, 0)
    back_ref[...] = (mm(dkh_ref[...], wk_ref[...], NT) + mm(dvh_ref[...], wv_ref[...], NT)).astype(BF)


def weights_body(
    scale, rows, head_size, meta_ref, normed_hbm, halo_hbm, frames_ref, cot_hbm,
    wq_hbm, wk_hbm, wv_hbm, wo_hbm,
    q_ref, kt_ref, vt_ref, khalo_t_ref, vhalo_t_ref, do_ref, raised_ref, grads_ref, scale_ref, dkh_ref, dvh_ref,
    keep_ref, send_ref, out_ref, slope_ref,
    normed_t, halo_t, mixed_t, ktx, vtx, ot, dqt, dk, dv,
    wq, wk, wv, wo, normed_ref, halo_ref, cot_ref, sems,
):
    span, width = q_ref.shape
    copies = fetch(
        [wq_hbm, wk_hbm, wv_hbm, wo_hbm, normed_hbm, halo_hbm, cot_hbm],
        [wq, wk, wv, wo, normed_ref, halo_ref, cot_ref], sems,
    )
    ktx[:, :WIN] = khalo_t_ref[...]
    ktx[:, WIN:] = kt_ref[...]
    vtx[:, :WIN] = vhalo_t_ref[...]
    vtx[:, WIN:] = vt_ref[...]
    pair = 2 * head_size
    tiles = span // TILE
    upper = iota2((pair, TILE), 0) < head_size

    def one_pair(p, carry):
        cols = pl.ds(pl.multiple_of(p * pair, pair), pair)
        own_grads = []
        for a in range(tiles):
            here = slice(a * TILE, (a + 1) * TILE)
            keys = slice(a * TILE, a * TILE + REACH)
            at = p * tiles + a
            shrink = scale_ref[at]
            mixed = mm(vtx[cols, keys], raised_ref[at]) * shrink
            ot[cols, here] = jnp.where(upper, mixed[:, :TILE], mixed[:, TILE:]).astype(BF)
            moved = mm(ktx[cols, keys], grads_ref[at]) * (shrink * head_size ** (-0.5))
            dqt[cols, here] = jnp.where(upper, moved[:, :TILE], moved[:, TILE:]).astype(BF)
            near = slice(WIN - a * TILE, REACH)
            own_grads.append((
                mm(grads_ref[at, near], both_heads(q_ref[here, cols], 1, 0)),
                mm(raised_ref[at, near], both_heads(do_ref[here, cols], 1, 0)),
            ))
        for which, factor, out in ((0, math.log(2.0), dk), (1, 1.0, dv)):
            for j in range(tiles):
                total = None
                for a in range(j, tiles):
                    piece = own_grads[a][which][j * TILE : (j + 1) * TILE]
                    total = piece if total is None else total + piece
                out[j * TILE : (j + 1) * TILE, cols] = (total * factor).astype(BF)
        return carry

    lax.fori_loop(0, width // pair, one_pair, 0)

    for copy in copies:
        copy.wait()
    chunks = width // (2 * rows)
    split = (chunks, 2, rows, span)
    normed_t[...] = normed_ref[...].T.reshape(split)
    halo_t[...] = halo_ref[...].T.reshape(split)
    mixed_t[...] = ot[...].reshape(split)
    mine = meta_ref[2]
    for side, out in ((1 - mine, send_ref), (mine, keep_ref)):
        own = normed_t[:, side].reshape(width // 2, span)
        far = halo_t[:, side].reshape(width // 2, span)
        mixed = mixed_t[:, side].reshape(width // 2, span)
        for n, total in enumerate((
            mm(own, dqt[...], NT),
            mm(own, dk[...]) + mm(far, dkh_ref[...]),
            mm(own, dv[...]) + mm(far, dvh_ref[...]),
            mm(mixed, cot_ref[...]),
        )):
            out[:, n * width : (n + 1) * width] = (total * scale).astype(BF)
    slope = mm(dqt[...].T, wq[...], NT)
    slope = slope + mm(dk[...], wk[...], NT)
    slope_ref[...] = slope + mm(dv[...], wv[...], NT)
    out = mm(ot[...].T, wo[...]) + frames_ref[...].astype(F32)
    out_ref[...] = out.astype(BF)


def returning_body(
    frames_ref, slope_ref, extra_ref, cot_hbm, pick_t_hbm, out_ref, cot_ref, pick_t_ref, sems
):
    copies = fetch([cot_hbm, pick_t_hbm], [cot_ref, pick_t_ref], sems)
    _, inverse, normed32 = unit_frames(frames_ref[...])
    slope = slope_ref[...] + extra_ref[...].astype(F32)
    centre = jnp.mean(slope * normed32, axis=1, keepdims=True)
    copies[0].wait()
    grad = inverse * (slope - normed32 * centre) + cot_ref[...].astype(F32)
    copies[1].wait()
    out_ref[...] = mm(pick_t_ref[...], grad.astype(BF)).astype(BF)


def arrived_body(placing_t_ref, in_ref, out_ref):
    out_ref[...] = mm(placing_t_ref[...], in_ref[...]).astype(BF)


def passed_along(shard, by):
    devices = lax.axis_size("seq")
    pairs = [(i, i + by) for i in range(devices) if 0 <= i + by < devices]
    return lax.ppermute(shard, "seq", pairs)


def spread_body(place_ref, *refs):
    parts = refs[0].shape[0]
    inputs, outs = refs[:-parts], refs[-parts:]
    for k, out in enumerate(outs):
        at = place_ref[0] ^ k
        total = inputs[0][at].astype(F32)
        for ref in inputs[1:]:
            total = total + ref[at].astype(F32)
        out[...] = total.astype(BF)


def spread(inputs, place, parts):
    columns = inputs[0].shape[-1]
    inputs = [shard.reshape(parts, -1, columns) for shard in inputs]
    piece = sds(inputs[0].shape[1:])
    return vmem_call(spread_body, [piece] * parts, [place.reshape(1)] + inputs, smem=(0,))


def swapped(pieces, axis, step):
    count = lax.axis_size(axis)
    return [pieces[0]] + [
        lax.ppermute(piece, axis, [(i, i ^ (k * step)) for i in range(count)])
        for k, piece in enumerate(pieces[1:], 1)
    ]


def shards(
    frame_rows, row_frame, frame_owner, lengths,
    query_weight, key_weight, value_weight, out_weight, cotangent,
):
    devices = lax.axis_size(AXES)
    row_count, width = frame_rows.shape
    span = frame_owner.shape[1]
    slots = row_count // devices
    slab = span * lax.axis_size("seq")
    head_size = width // H
    cube = 2 * span * width * width
    square = sds((span, width))
    begin = (lax.axis_index("seq") * span).astype(jnp.int32)
    rows = width // devices
    in_kernel = rows % 16 == 0
    core = (lax.axis_index("seq") & 1).astype(jnp.int32)
    meta = jnp.stack([begin, lengths[0], core if in_kernel else jnp.zeros((), jnp.int32)])
    cot = cotangent[0]

    def exchanged(shard):
        got = lax.all_to_all(
            shard.reshape(devices, slots, width), AXES, split_axis=0, concat_axis=0, tiled=True
        )
        return got.reshape(devices * slots, width)

    outgoing, = vmem_call(
        lambda *refs: outgoing_body(span, slots, *refs),
        [square],
        [row_frame.reshape(1, row_count), frame_rows],
        hbm=(1,),
        scratch=[pltpu.VMEM((row_count, width), BF), pltpu.SemaphoreType.DMA((1,))],
        flops=cube,
    )
    incoming = exchanged(outgoing)
    pick, pick_t = vmem_call(
        lambda *refs: early_body(slots, *refs),
        [square, square],
        [frame_owner.reshape(span, 1)],
        flops=cube,
    )
    frames, normed = vmem_call(frames_body, [square, square], [pick, incoming], flops=cube)
    halo = passed_along(normed, 1)
    query_scale = head_size ** (-0.5) * math.log2(math.e)
    qt, k, kt, v, vt, wk, wv = vmem_call(
        lambda *refs: project_body(query_scale, *refs),
        [square] * 7,
        [normed, query_weight, key_weight, value_weight],
        hbm=(1, 2, 3),
        scratch=[pltpu.VMEM((width, width), BF), pltpu.SemaphoreType.DMA((3,))],
        flops=3 * cube,
    )
    units = H // 2 * (span // TILE)
    saved = sds((units, REACH, 2 * TILE))
    raised, grads, scales, q, do, dkh, dvh, khalo_t, vhalo_t, back = vmem_call(
        lambda *refs: scores_body(head_size, *refs),
        [saved, saved, sds((units, 1, 2 * TILE), F32)] + [square] * 7,
        [meta, halo, wk, wv, qt, k, v, cot, out_weight],
        smem=(0,),
        hbm=(7, 8),
        scratch=[pltpu.VMEM((WIN + span, width), BF)] * 2
        + [pltpu.VMEM((width, span), BF)] * 3 + [pltpu.SemaphoreType.DMA((2,))],
        flops=12 * cube,
        limit=24,
    )
    extra = passed_along(back, -1)
    chunk = rows if in_kernel else width // 2
    split = pltpu.VMEM((width // (2 * chunk), 2, chunk, span), BF)
    half = sds((width // 2, 4 * width))
    whole = pltpu.VMEM((width, width), BF)
    keep, send, out_frames, slope = vmem_call(
        lambda *refs: weights_body(slab ** (-0.5), chunk, head_size, *refs),
        [half, half, square, sds((span, width), F32)],
        [meta, normed, halo, frames, cot, query_weight, key_weight, value_weight, out_weight,
         q, kt, vt, khalo_t, vhalo_t, do, raised, grads, scales, dkh, dvh],
        smem=(0,),
        hbm=(1, 2, 4, 5, 6, 7, 8),
        scratch=[split] * 3 + [pltpu.VMEM((width, WIN + span), BF)] * 2 + [whole] * 11
        + [pltpu.SemaphoreType.DMA((7,))],
        flops=18 * cube,
        limit=26,
    )
    send, extra = lax.optimization_barrier((send, extra))
    if not in_kernel:
        sums = jnp.concatenate([keep, send], axis=0).reshape(-1, 2, rows, 4 * width)
        keep = lax.dynamic_index_in_dim(sums, core, 1, keepdims=False).reshape(half.shape)
        send = lax.dynamic_index_in_dim(sums, 1 - core, 1, keepdims=False).reshape(half.shape)
    seqs = lax.axis_size("seq")
    got = lax.ppermute(send, "seq", [(i, i ^ 1) for i in range(seqs)])
    seqs = lax.axis_size("seq")
    got = lax.ppermute(send, "seq", [(i, i ^ 1) for i in range(seqs)])
    returning, = vmem_call(
        returning_body,
        [square],
        [frames, slope, extra, cot, pick_t],
        hbm=(3, 4),
        scratch=[whole, whole, pltpu.SemaphoreType.DMA((2,))],
        flops=cube,
    )
    pieces = spread([keep, got], lax.axis_index("stream"), lax.axis_size("stream"))
    pieces = swapped(pieces, "stream", 1)
    late_rows, returning = lax.optimization_barrier((row_frame.reshape(1, row_count), returning))
    arrived = exchanged(returning)
    placing_t, = vmem_call(
        lambda *refs: placing_t_body(span, slots, *refs),
        [sds((row_count, devices * slots))],
        [late_rows],
    )
    frame_grads, = vmem_call(arrived_body, [square], [placing_t, arrived], flops=cube)
    pieces = swapped(spread(pieces, lax.axis_index("seq") >> 1, seqs // 2), "seq", 2)
    weight_grads = pieces[0].astype(F32)
    for piece in pieces[1:]:
        weight_grads = weight_grads + piece.astype(F32)
    return (out_frames[None], frame_grads, weight_grads)


def solution(mesh):
    return jax.shard_map(
        shards,
        mesh=mesh,
        in_specs=(
            P(AXES, None), P(AXES), P("stream", "seq"), P("stream"),
            P(), P(), P(), P(), P("stream", "seq", None),
        ),
        out_specs=(P("stream", "seq", None), P(AXES, None), P(AXES, None)),
        check_vma=False,
    )
```

```python
import math

import jax
import jax.numpy as jnp
from jax import lax
from jax.experimental import pallas as pl
from jax.experimental.pallas import tpu as pltpu
from jax.sharding import PartitionSpec as P

H = 8
WIN = 512
NEG = -1e30
EPS_NORM = 1e-06
AXES = ("stream", "seq")
BF = jnp.bfloat16
F32 = jnp.float32

NN = (((1,), (0,)), ((), ()))
NT = (((1,), (1,)), ((), ()))


def mm(a, b, dims=NN):
    return lax.dot_general(a, b, dims, preferred_element_type=F32)


def iota2(shape, dim):
    return lax.broadcasted_iota(jnp.int32, shape, dim)


def vmem_call(body, outs, args, smem=(), hbm=(), scratch=(), flops=0, limit=12):
    spaces = [pltpu.SMEM if i in smem else pltpu.HBM if i in hbm else pltpu.VMEM for i in range(len(args))]
    size = sum(math.prod(a.shape) * a.dtype.itemsize for a in list(args) + list(outs))
    return pl.pallas_call(
        body,
        out_shape=tuple(outs),
        in_specs=[pl.BlockSpec(memory_space=space) for space in spaces],
        out_specs=tuple(pl.BlockSpec(memory_space=pltpu.VMEM) for _ in outs),
        scratch_shapes=list(scratch),
        compiler_params=pltpu.CompilerParams(vmem_limit_bytes=limit * 2**20),
        cost_estimate=pl.CostEstimate(flops=flops, bytes_accessed=size, transcendentals=0),
    )(*args)


def fetch(sources, targets, sems):
    copies = [
        pltpu.make_async_copy(source, target, sems.at[n])
        for n, (source, target) in enumerate(zip(sources, targets))
    ]
    for copy in copies:
        copy.start()
    return copies


def sds(shape, dtype=BF):
    return jax.ShapeDtypeStruct(shape, dtype)


def placing_of(span, slots, rf, total):
    count = rf.shape[1]
    target = jnp.where(rf >= 0, lax.div(rf, span), 1 << 20)
    slot = iota2((total, count), 0)
    owner = lax.div(slot, slots)
    rank = slot - owner * slots
    start = jnp.sum(jnp.where(target < owner, 1.0, 0.0), axis=1, keepdims=True)
    here = iota2((total, count), 1) - start.astype(jnp.int32)
    return jnp.where((target == owner) & (here == rank), 1.0, 0.0)


def outgoing_body(span, slots, rf_ref, rows_hbm, out_ref, rows_ref, sems):
    (rows_copy,) = fetch([rows_hbm], [rows_ref], sems)
    placing = placing_of(span, slots, rf_ref[...], out_ref.shape[0]).astype(BF)
    rows_copy.wait()
    out_ref[...] = mm(placing, rows_ref[...]).astype(BF)


def placing_t_body(span, slots, rf_ref, out_ref):
    out_ref[...] = placing_of(span, slots, rf_ref[...], out_ref.shape[1]).T.astype(BF)


def early_body(slots, owner_ref, pick_ref, pick_t_ref):
    span, lanes = owner_ref.shape[0], 128
    total = pick_ref.shape[1]
    owner = owner_ref[...]
    device = iota2((span, lanes), 1)
    hot = jnp.where(owner == device, 1.0, 0.0)
    strict = jnp.where(iota2((span, span), 1) < iota2((span, span), 0), 1.0, 0.0).astype(BF)
    before = mm(strict, hot.astype(BF))
    slot = jnp.sum(hot * (before + (device * slots).astype(F32)), axis=1, keepdims=True)
    slot = jnp.where(owner >= 0, slot.astype(jnp.int32), -1)
    pick = jnp.where(iota2((span, total), 1) == slot, 1.0, 0.0)
    pick_ref[...] = pick.astype(BF)
    pick_t_ref[...] = pick.T.astype(BF)


def unit_frames(frames):
    frames32 = frames.astype(F32)
    inverse = lax.rsqrt(jnp.mean(frames32 * frames32, axis=1, keepdims=True) + EPS_NORM)
    return frames32, inverse, frames32 * inverse


def frames_body(pick_ref, in_ref, frames_ref, normed_ref):
    frames = mm(pick_ref[...], in_ref[...]).astype(BF)
    frames_ref[...] = frames
    normed_ref[...] = unit_frames(frames)[2].astype(BF)


def project_body(
    query_scale, normed_ref, wq_hbm, wk_hbm, wv_hbm,
    qt_ref, k_ref, kt_ref, v_ref, vt_ref, wk_ref, wv_ref, wq_ref, sems,
):
    copies = fetch([wq_hbm, wk_hbm, wv_hbm], [wq_ref, wk_ref, wv_ref], sems)
    normed = normed_ref[...]
    copies[0].wait()
    qt_ref[...] = (mm(normed, wq_ref[...]) * query_scale).astype(BF).T
    copies[1].wait()
    k = mm(normed, wk_ref[...]).astype(BF)
    k_ref[...] = k
    kt_ref[...] = k.T
    copies[2].wait()
    v = mm(normed, wv_ref[...]).astype(BF)
    v_ref[...] = v
    vt_ref[...] = v.T


TILE = 128
REACH = WIN + TILE


def raised_scores(scores, first, begin):
    row = iota2((TILE, TILE), 0)
    col = iota2((TILE, TILE), 1)
    halo_bias = jnp.where(begin == 0, NEG, 0.0)
    count = REACH // TILE
    raised_cols = []
    for h in range(2):
        at = slice(h * TILE, (h + 1) * TILE)
        parts = []
        for n in range(count):
            part = scores[n * TILE : (n + 1) * TILE, at]
            if n == 0:
                part = jnp.where(row > col, part, NEG)
            if n == count - 1:
                part = jnp.where(row <= col, part, NEG)
            elif first + n * TILE < WIN:
                part = part + halo_bias
            parts.append(part)
        peak = parts[0]
        for part in parts[1:]:
            peak = jnp.maximum(peak, part)
        peak = jnp.max(peak, axis=0, keepdims=True)
        raised_cols.append(jnp.concatenate([jnp.exp2((part - peak).astype(BF)) for part in parts], axis=0))
    return jnp.concatenate(raised_cols, axis=1)


def both_heads(value, axis, along):
    place = iota2(value.shape, axis)
    half = value.shape[axis] // 2
    zero = jnp.zeros((), value.dtype)
    return jnp.concatenate([jnp.where(place < half, value, zero), jnp.where(place < half, zero, value)], axis=along)


def scores_body(
    head_size, meta_ref, halo_ref, wk_ref, wv_ref, qt_ref, k_ref, v_ref, vt_ref, cot_hbm, wo_hbm,
    raised_ref, grads_ref, scale_ref, q_ref, do_ref, dkh_ref, dvh_ref, khalo_t_ref, halo_t_ref, ot_ref, back_ref,
    kx, vx, vtx, dot_ref, cot_ref, wo_ref, sems,
):
    copies = fetch([cot_hbm, wo_hbm], [cot_ref, wo_ref], sems)
    span, width = k_ref.shape
    begin, length = meta_ref[0], meta_ref[1]
    halo = halo_ref[...]
    kh = mm(halo, wk_ref[...]).astype(BF)
    kx[:WIN] = kh
    khalo_t_ref[...] = kh.T
    vh = mm(halo, wv_ref[...]).astype(BF)
    vx[:WIN] = vh
    vtx[:, :WIN] = vh.T
    vtx[:, WIN:] = vt_ref[...]
    halo_t_ref[...] = halo.T
    kx[WIN:] = k_ref[...]
    vx[WIN:] = v_ref[...]

    pair = 2 * head_size
    tiles = span // TILE
    upper = iota2((pair, TILE), 0) < head_size
    ones = jnp.ones((16, REACH), BF)

    def one_pair(p, carry):
        cols = pl.ds(pl.multiple_of(p * pair, pair), pair)

        def multiply(a):
            here = slice(a * TILE, (a + 1) * TILE)
            keys = slice(a * TILE, a * TILE + REACH)
            scores = mm(kx[keys, cols], both_heads(qt_ref[cols, here], 0, 1))
            slopes = mm(vx[keys, cols], both_heads(dot_ref[cols, here], 0, 1))
            return scores, slopes

        halo_grads = []

        def raise_and_mix(a, scores):
            here = slice(a * TILE, (a + 1) * TILE)
            keys = slice(a * TILE, a * TILE + REACH)
            raised = raised_scores(scores, a * TILE, begin)
            raised_ref[p * tiles + a] = raised
            mixed = mm(jnp.concatenate([vtx[cols, keys], ones], axis=0), raised)
            time = begin + a * TILE + iota2((1, 2 * TILE), 1) % TILE
            scale = jnp.where(time < length, 1.0 / mixed[pair : pair + 1], 0.0)
            scale_ref[p * tiles + a] = scale
            spread_scale = jnp.where(upper, scale[:, :TILE], scale[:, TILE:])
            mixed = jnp.where(upper, mixed[:pair, :TILE], mixed[:pair, TILE:]) * spread_scale
            ot_ref[cols, here] = mixed.astype(BF)
            return raised, mixed, spread_scale

        def finish(a, slopes, raised, mixed, spread_scale):
            here = slice(a * TILE, (a + 1) * TILE)
            out_grad = dot_ref[cols, here].astype(F32)
            product = mixed * out_grad
            grad_cols = []
            for h in range(2):
                at = slice(h * TILE, (h + 1) * TILE)
                centre = jnp.sum(product[h * head_size : (h + 1) * head_size], axis=0, keepdims=True)
                grad_cols.append(raised[:, at] * (slopes[:, at] - centre).astype(BF))
            grads = jnp.concatenate(grad_cols, axis=1)
            grads_ref[p * tiles + a] = grads
            far = WIN - a * TILE
            queries = (qt_ref[cols, here].astype(F32) * spread_scale).T.astype(BF)
            out_grad = (out_grad * spread_scale).T.astype(BF)
            q_ref[here, cols] = queries
            do_ref[here, cols] = out_grad
            halo_grads.append((
                mm(grads[:far], both_heads(queries, 1, 0)),
                mm(raised[:far], both_heads(out_grad, 1, 0)),
            ))

        scores, slopes = multiply(0)
        waiting = None
        for a in range(tiles):
            ahead = multiply(a + 1) if a + 1 < tiles else None
            mixed = raise_and_mix(a, scores)
            if waiting is not None:
                finish(*waiting)
            waiting = (a, slopes, *mixed)
            if ahead is not None:
                scores, slopes = ahead
        finish(*waiting)
        for which, scale, out in ((0, math.log(2.0), dkh_ref), (1, 1.0, dvh_ref)):
            for j in range(WIN // TILE):
                total = None
                for a in range(min(j + 1, tiles)):
                    piece = halo_grads[a][which][(j - a) * TILE : (j - a + 1) * TILE]
                    total = piece if total is None else total + piece
                out[j * TILE : (j + 1) * TILE, cols] = (total * scale).astype(BF)
        return carry

    for copy in copies:
        copy.wait()
    dot_ref[...] = mm(cot_ref[...], wo_ref[...], NT).astype(BF).T
    lax.fori_loop(0, width // pair, one_pair, 0)
    back_ref[...] = (mm(dkh_ref[...], wk_ref[...], NT) + mm(dvh_ref[...], wv_ref[...], NT)).astype(BF)


def weights_body(
    scale, rows, head_size, meta_ref, normed_hbm, halo_t_ref, frames_ref, cot_hbm,
    wq_hbm, wk_hbm, wv_hbm, wo_hbm,
    q_ref, kt_ref, khalo_t_ref, ot, do_ref, raised_ref, grads_ref, scale_ref, dkh_ref, dvh_ref,
    keep_ref, send_ref, out_ref, slope_ref,
    normed_t, halo_t, mixed_t, ktx, dqt, dk, dv,
    wq, wk, wv, wo, normed_ref, cot_ref, sems,
):
    span, width = q_ref.shape
    copies = fetch(
        [wq_hbm, wk_hbm, wv_hbm, wo_hbm, normed_hbm, cot_hbm],
        [wq, wk, wv, wo, normed_ref, cot_ref], sems,
    )
    ktx[:, :WIN] = khalo_t_ref[...]
    ktx[:, WIN:] = kt_ref[...]
    pair = 2 * head_size
    tiles = span // TILE
    upper = iota2((pair, TILE), 0) < head_size

    def one_pair(p, carry):
        cols = pl.ds(pl.multiple_of(p * pair, pair), pair)
        own_grads = []
        for a in range(tiles):
            here = slice(a * TILE, (a + 1) * TILE)
            keys = slice(a * TILE, a * TILE + REACH)
            at = p * tiles + a
            shrink = scale_ref[at]
            moved = mm(ktx[cols, keys], grads_ref[at]) * (shrink * head_size ** (-0.5))
            dqt[cols, here] = jnp.where(upper, moved[:, :TILE], moved[:, TILE:]).astype(BF)
            near = slice(WIN - a * TILE, REACH)
            own_grads.append((
                mm(grads_ref[at, near], both_heads(q_ref[here, cols], 1, 0)),
                mm(raised_ref[at, near], both_heads(do_ref[here, cols], 1, 0)),
            ))
        for which, factor, out in ((0, math.log(2.0), dk), (1, 1.0, dv)):
            for j in range(tiles):
                total = None
                for a in range(j, tiles):
                    piece = own_grads[a][which][j * TILE : (j + 1) * TILE]
                    total = piece if total is None else total + piece
                out[j * TILE : (j + 1) * TILE, cols] = (total * factor).astype(BF)
        return carry

    lax.fori_loop(0, width // pair, one_pair, 0)

    for copy in copies:
        copy.wait()
    chunks = width // (2 * rows)
    split = (chunks, 2, rows, span)
    normed_t[...] = normed_ref[...].T.reshape(split)
    halo_t[...] = halo_t_ref[...].reshape(split)
    mixed_t[...] = ot[...].reshape(split)
    mine = meta_ref[2]
    for side, out in ((1 - mine, send_ref), (mine, keep_ref)):
        own = normed_t[:, side].reshape(width // 2, span)
        far = halo_t[:, side].reshape(width // 2, span)
        mixed = mixed_t[:, side].reshape(width // 2, span)
        for n, total in enumerate((
            mm(own, dqt[...], NT),
            mm(own, dk[...]) + mm(far, dkh_ref[...]),
            mm(own, dv[...]) + mm(far, dvh_ref[...]),
            mm(mixed, cot_ref[...]),
        )):
            out[:, n * width : (n + 1) * width] = (total * scale).astype(BF)
    slope = mm(dqt[...].T, wq[...], NT)
    slope = slope + mm(dk[...], wk[...], NT)
    slope_ref[...] = slope + mm(dv[...], wv[...], NT)
    out = mm(ot[...].T, wo[...]) + frames_ref[...].astype(F32)
    out_ref[...] = out.astype(BF)


def returning_body(
    frames_ref, slope_ref, extra_ref, cot_hbm, pick_t_hbm, out_ref, cot_ref, pick_t_ref, sems
):
    copies = fetch([cot_hbm, pick_t_hbm], [cot_ref, pick_t_ref], sems)
    _, inverse, normed32 = unit_frames(frames_ref[...])
    slope = slope_ref[...] + extra_ref[...].astype(F32)
    centre = jnp.mean(slope * normed32, axis=1, keepdims=True)
    copies[0].wait()
    grad = inverse * (slope - normed32 * centre) + cot_ref[...].astype(F32)
    copies[1].wait()
    out_ref[...] = mm(pick_t_ref[...], grad.astype(BF)).astype(BF)


def arrived_body(placing_t_ref, in_ref, out_ref):
    out_ref[...] = mm(placing_t_ref[...], in_ref[...]).astype(BF)


def passed_along(shard, by):
    devices = lax.axis_size("seq")
    pairs = [(i, i + by) for i in range(devices) if 0 <= i + by < devices]
    return lax.ppermute(shard, "seq", pairs)


def spread_body(place_ref, *refs):
    parts = refs[0].shape[0]
    inputs, outs = refs[:-parts], refs[-parts:]
    for k, out in enumerate(outs):
        at = place_ref[0] ^ k
        total = inputs[0][at].astype(F32)
        for ref in inputs[1:]:
            total = total + ref[at].astype(F32)
        out[...] = total.astype(BF)


def spread(inputs, place, parts):
    columns = inputs[0].shape[-1]
    inputs = [shard.reshape(parts, -1, columns) for shard in inputs]
    piece = sds(inputs[0].shape[1:])
    return vmem_call(spread_body, [piece] * parts, [place.reshape(1)] + inputs, smem=(0,))


def swapped(pieces, axis, step):
    count = lax.axis_size(axis)
    return [pieces[0]] + [
        lax.ppermute(piece, axis, [(i, i ^ (k * step)) for i in range(count)])
        for k, piece in enumerate(pieces[1:], 1)
    ]


def shards(
    frame_rows, row_frame, frame_owner, lengths,
    query_weight, key_weight, value_weight, out_weight, cotangent,
):
    devices = lax.axis_size(AXES)
    row_count, width = frame_rows.shape
    span = frame_owner.shape[1]
    slots = row_count // devices
    slab = span * lax.axis_size("seq")
    head_size = width // H
    cube = 2 * span * width * width
    square = sds((span, width))
    begin = (lax.axis_index("seq") * span).astype(jnp.int32)
    rows = width // devices
    in_kernel = rows % 16 == 0
    core = (lax.axis_index("seq") & 1).astype(jnp.int32)
    meta = jnp.stack([begin, lengths[0], core if in_kernel else jnp.zeros((), jnp.int32)])
    cot = cotangent[0]

    def exchanged(shard):
        got = lax.all_to_all(
            shard.reshape(devices, slots, width), AXES, split_axis=0, concat_axis=0, tiled=True
        )
        return got.reshape(devices * slots, width)

    outgoing, = vmem_call(
        lambda *refs: outgoing_body(span, slots, *refs),
        [square],
        [row_frame.reshape(1, row_count), frame_rows],
        hbm=(1,),
        scratch=[pltpu.VMEM((row_count, width), BF), pltpu.SemaphoreType.DMA((1,))],
        flops=cube,
    )
    incoming = exchanged(outgoing)
    pick, pick_t = vmem_call(
        lambda *refs: early_body(slots, *refs),
        [square, square],
        [frame_owner.reshape(span, 1)],
        flops=cube,
    )
    frames, normed = vmem_call(frames_body, [square, square], [pick, incoming], flops=cube)
    halo = passed_along(normed, 1)
    query_scale = head_size ** (-0.5) * math.log2(math.e)
    qt, k, kt, v, vt, wk, wv = vmem_call(
        lambda *refs: project_body(query_scale, *refs),
        [square] * 7,
        [normed, query_weight, key_weight, value_weight],
        hbm=(1, 2, 3),
        scratch=[pltpu.VMEM((width, width), BF), pltpu.SemaphoreType.DMA((3,))],
        flops=3 * cube,
    )
    units = H // 2 * (span // TILE)
    saved = sds((units, REACH, 2 * TILE))
    raised, grads, scales, q, do, dkh, dvh, khalo_t, halo_t, ot, back = vmem_call(
        lambda *refs: scores_body(head_size, *refs),
        [saved, saved, sds((units, 1, 2 * TILE), F32)] + [square] * 8,
        [meta, halo, wk, wv, qt, k, v, vt, cot, out_weight],
        smem=(0,),
        hbm=(8, 9),
        scratch=[pltpu.VMEM((WIN + span, width), BF)] * 2 + [pltpu.VMEM((width, WIN + span), BF)]
        + [pltpu.VMEM((width, span), BF)] * 3 + [pltpu.SemaphoreType.DMA((2,))],
        flops=12 * cube,
        limit=24,
    )
    extra = passed_along(back, -1)
    chunk = rows if in_kernel else width // 2
    split = pltpu.VMEM((width // (2 * chunk), 2, chunk, span), BF)
    half = sds((width // 2, 4 * width))
    whole = pltpu.VMEM((width, width), BF)
    keep, send, out_frames, slope = vmem_call(
        lambda *refs: weights_body(slab ** (-0.5), chunk, head_size, *refs),
        [half, half, square, sds((span, width), F32)],
        [meta, normed, halo_t, frames, cot, query_weight, key_weight, value_weight, out_weight,
         q, kt, khalo_t, ot, do, raised, grads, scales, dkh, dvh],
        smem=(0,),
        hbm=(1, 4, 5, 6, 7, 8),
        scratch=[split] * 3 + [pltpu.VMEM((width, WIN + span), BF)] + [whole] * 9
        + [pltpu.SemaphoreType.DMA((6,))],
        flops=18 * cube,
        limit=26,
    )
    send, extra = lax.optimization_barrier((send, extra))
    if not in_kernel:
        sums = jnp.concatenate([keep, send], axis=0).reshape(-1, 2, rows, 4 * width)
        keep = lax.dynamic_index_in_dim(sums, core, 1, keepdims=False).reshape(half.shape)
        send = lax.dynamic_index_in_dim(sums, 1 - core, 1, keepdims=False).reshape(half.shape)
    seqs = lax.axis_size("seq")
    got = lax.ppermute(send, "seq", [(i, i ^ 1) for i in range(seqs)])
    seqs = lax.axis_size("seq")
    got = lax.ppermute(send, "seq", [(i, i ^ 1) for i in range(seqs)])
    returning, = vmem_call(
        returning_body,
        [square],
        [frames, slope, extra, cot, pick_t],
        hbm=(3, 4),
        scratch=[whole, whole, pltpu.SemaphoreType.DMA((2,))],
        flops=cube,
    )
    pieces = spread([keep, got], lax.axis_index("stream"), lax.axis_size("stream"))
    pieces = swapped(pieces, "stream", 1)
    late_rows, returning = lax.optimization_barrier((row_frame.reshape(1, row_count), returning))
    arrived = exchanged(returning)
    placing_t, = vmem_call(
        lambda *refs: placing_t_body(span, slots, *refs),
        [sds((row_count, devices * slots))],
        [late_rows],
    )
    frame_grads, = vmem_call(arrived_body, [square], [placing_t, arrived], flops=cube)
    pieces = swapped(spread(pieces, lax.axis_index("seq") >> 1, seqs // 2), "seq", 2)
    weight_grads = pieces[0].astype(F32)
    for piece in pieces[1:]:
        weight_grads = weight_grads + piece.astype(F32)
    return (out_frames[None], frame_grads, weight_grads)


def solution(mesh):
    return jax.shard_map(
        shards,
        mesh=mesh,
        in_specs=(
            P(AXES, None), P(AXES), P("stream", "seq"), P("stream"),
            P(), P(), P(), P(), P("stream", "seq", None),
        ),
        out_specs=(P("stream", "seq", None), P(AXES, None), P(AXES, None)),
        check_vma=False,
    )
```

```python
import math

import jax
import jax.numpy as jnp
from jax import lax
from jax.experimental import pallas as pl
from jax.experimental.pallas import tpu as pltpu
from jax.sharding import PartitionSpec as P

H = 8
WIN = 512
NEG = -1e30
EPS_NORM = 1e-06
AXES = ("stream", "seq")
BF = jnp.bfloat16
F32 = jnp.float32

NN = (((1,), (0,)), ((), ()))
NT = (((1,), (1,)), ((), ()))


def mm(a, b, dims=NN):
    return lax.dot_general(a, b, dims, preferred_element_type=F32)


def iota2(shape, dim):
    return lax.broadcasted_iota(jnp.int32, shape, dim)


def vmem_call(body, outs, args, smem=(), hbm=(), scratch=(), carry=(), flops=0, limit=12):
    used, inner, args = len(args), body, list(args) + list(carry)

    def body(*refs):
        inner(*refs[:used], *refs[len(args) :])

    spaces = [pltpu.SMEM if i in smem else pltpu.HBM if i in hbm else pltpu.VMEM for i in range(len(args))]
    size = sum(math.prod(a.shape) * a.dtype.itemsize for a in list(args) + list(outs))
    return pl.pallas_call(
        body,
        out_shape=tuple(outs),
        in_specs=[pl.BlockSpec(memory_space=space) for space in spaces],
        out_specs=tuple(pl.BlockSpec(memory_space=pltpu.VMEM) for _ in outs),
        scratch_shapes=list(scratch),
        compiler_params=pltpu.CompilerParams(vmem_limit_bytes=limit * 2**20),
        cost_estimate=pl.CostEstimate(flops=flops, bytes_accessed=size, transcendentals=0),
    )(*args)


def fetch(sources, targets, sems):
    copies = [
        pltpu.make_async_copy(source, target, sems.at[n])
        for n, (source, target) in enumerate(zip(sources, targets))
    ]
    for copy in copies:
        copy.start()
    return copies


def sds(shape, dtype=BF):
    return jax.ShapeDtypeStruct(shape, dtype)


def placing_of(span, slots, rf, total):
    count = rf.shape[1]
    target = jnp.where(rf >= 0, lax.div(rf, span), 1 << 20)
    slot = iota2((total, count), 0)
    owner = lax.div(slot, slots)
    rank = slot - owner * slots
    start = jnp.sum(jnp.where(target < owner, 1.0, 0.0), axis=1, keepdims=True)
    here = iota2((total, count), 1) - start.astype(jnp.int32)
    return jnp.where((target == owner) & (here == rank), 1.0, 0.0)


def outgoing_body(span, slots, rf_ref, rows_hbm, out_ref, rows_ref, sems):
    (rows_copy,) = fetch([rows_hbm], [rows_ref], sems)
    placing = placing_of(span, slots, rf_ref[...], out_ref.shape[0]).astype(BF)
    rows_copy.wait()
    out_ref[...] = mm(placing, rows_ref[...]).astype(BF)


def placing_t_body(span, slots, rf_ref, out_ref):
    out_ref[...] = placing_of(span, slots, rf_ref[...], out_ref.shape[1]).T.astype(BF)


def early_body(slots, owner_ref, pick_ref, pick_t_ref):
    span, lanes = owner_ref.shape[0], 128
    total = pick_ref.shape[1]
    owner = owner_ref[...]
    device = iota2((span, lanes), 1)
    hot = jnp.where(owner == device, 1.0, 0.0)
    strict = jnp.where(iota2((span, span), 1) < iota2((span, span), 0), 1.0, 0.0).astype(BF)
    before = mm(strict, hot.astype(BF))
    slot = jnp.sum(hot * (before + (device * slots).astype(F32)), axis=1, keepdims=True)
    slot = jnp.where(owner >= 0, slot.astype(jnp.int32), -1)
    pick = jnp.where(iota2((span, total), 1) == slot, 1.0, 0.0)
    pick_ref[...] = pick.astype(BF)
    pick_t_ref[...] = pick.T.astype(BF)


def unit_frames(frames):
    frames32 = frames.astype(F32)
    inverse = lax.rsqrt(jnp.mean(frames32 * frames32, axis=1, keepdims=True) + EPS_NORM)
    return frames32, inverse, frames32 * inverse


def frames_body(pick_ref, in_ref, frames_ref, normed_ref):
    frames = mm(pick_ref[...], in_ref[...]).astype(BF)
    frames_ref[...] = frames
    normed_ref[...] = unit_frames(frames)[2].astype(BF)


def project_body(
    query_scale, normed_ref, wq_hbm, wk_hbm, wv_hbm,
    qt_ref, k_ref, kt_ref, v_ref, vt_ref, wk_ref, wv_ref, normed_t_ref, wq_ref, sems,
):
    copies = fetch([wq_hbm, wk_hbm, wv_hbm], [wq_ref, wk_ref, wv_ref], sems)
    normed = normed_ref[...]
    normed_t_ref[...] = normed.T
    copies[0].wait()
    qt_ref[...] = (mm(normed, wq_ref[...]) * query_scale).astype(BF).T
    copies[1].wait()
    k = mm(normed, wk_ref[...]).astype(BF)
    k_ref[...] = k
    kt_ref[...] = k.T
    copies[2].wait()
    v = mm(normed, wv_ref[...]).astype(BF)
    v_ref[...] = v
    vt_ref[...] = v.T


TILE = 128
REACH = WIN + TILE


def raised_scores(scores, first, begin):
    row = iota2((TILE, TILE), 0)
    col = iota2((TILE, TILE), 1)
    halo_bias = jnp.where(begin == 0, NEG, 0.0)
    count = REACH // TILE
    raised_cols = []
    for h in range(2):
        at = slice(h * TILE, (h + 1) * TILE)
        parts = []
        for n in range(count):
            part = scores[n * TILE : (n + 1) * TILE, at]
            if n == 0:
                part = jnp.where(row > col, part, NEG)
            if n == count - 1:
                part = jnp.where(row <= col, part, NEG)
            elif first + n * TILE < WIN:
                part = part + halo_bias
            parts.append(part)
        peak = parts[0]
        for part in parts[1:]:
            peak = jnp.maximum(peak, part)
        peak = jnp.max(peak, axis=0, keepdims=True)
        raised_cols.append(jnp.concatenate([jnp.exp2((part - peak).astype(BF)) for part in parts], axis=0))
    return jnp.concatenate(raised_cols, axis=1)


def both_heads(value, axis, along):
    place = iota2(value.shape, axis)
    half = value.shape[axis] // 2
    zero = jnp.zeros((), value.dtype)
    return jnp.concatenate([jnp.where(place < half, value, zero), jnp.where(place < half, zero, value)], axis=along)


def scores_body(
    head_size, meta_ref, halo_ref, wk_ref, wv_ref, qt_ref, k_ref, v_ref, vt_ref, cot_hbm, wo_hbm,
    raised_ref, grads_ref, scale_ref, q_ref, do_ref, dkh_ref, dvh_ref, khalo_t_ref, halo_t_ref, ot_ref, back_ref,
    kx, vx, vtx, dot_ref, cot_ref, wo_ref, sems,
):
    copies = fetch([cot_hbm, wo_hbm], [cot_ref, wo_ref], sems)
    span, width = k_ref.shape
    begin, length = meta_ref[0], meta_ref[1]
    halo = halo_ref[...]
    kh = mm(halo, wk_ref[...]).astype(BF)
    kx[:WIN] = kh
    khalo_t_ref[...] = kh.T
    vh = mm(halo, wv_ref[...]).astype(BF)
    vx[:WIN] = vh
    vtx[:, :WIN] = vh.T
    vtx[:, WIN:] = vt_ref[...]
    halo_t_ref[...] = halo.T
    kx[WIN:] = k_ref[...]
    vx[WIN:] = v_ref[...]

    pair = 2 * head_size
    tiles = span // TILE
    upper = iota2((pair, TILE), 0) < head_size
    ones = jnp.ones((16, REACH), BF)

    def one_pair(p, carry):
        cols = pl.ds(pl.multiple_of(p * pair, pair), pair)

        def multiply(a):
            here = slice(a * TILE, (a + 1) * TILE)
            keys = slice(a * TILE, a * TILE + REACH)
            scores = mm(kx[keys, cols], both_heads(qt_ref[cols, here], 0, 1))
            slopes = mm(vx[keys, cols], both_heads(dot_ref[cols, here], 0, 1))
            return scores, slopes

        halo_grads = []

        def raise_and_mix(a, scores):
            here = slice(a * TILE, (a + 1) * TILE)
            keys = slice(a * TILE, a * TILE + REACH)
            raised = raised_scores(scores, a * TILE, begin)
            raised_ref[p * tiles + a] = raised
            mixed = mm(jnp.concatenate([vtx[cols, keys], ones], axis=0), raised)
            time = begin + a * TILE + iota2((1, 2 * TILE), 1) % TILE
            scale = jnp.where(time < length, 1.0 / mixed[pair : pair + 1], 0.0)
            scale_ref[p * tiles + a] = scale
            spread_scale = jnp.where(upper, scale[:, :TILE], scale[:, TILE:])
            mixed = jnp.where(upper, mixed[:pair, :TILE], mixed[:pair, TILE:]) * spread_scale
            ot_ref[cols, here] = mixed.astype(BF)
            return raised, mixed, spread_scale

        def finish(a, slopes, raised, mixed, spread_scale):
            here = slice(a * TILE, (a + 1) * TILE)
            out_grad = dot_ref[cols, here].astype(F32)
            product = mixed * out_grad
            grad_cols = []
            for h in range(2):
                at = slice(h * TILE, (h + 1) * TILE)
                centre = jnp.sum(product[h * head_size : (h + 1) * head_size], axis=0, keepdims=True)
                grad_cols.append(raised[:, at] * (slopes[:, at] - centre).astype(BF))
            grads = jnp.concatenate(grad_cols, axis=1)
            grads_ref[p * tiles + a] = grads
            far = WIN - a * TILE
            queries = (qt_ref[cols, here].astype(F32) * spread_scale).T.astype(BF)
            out_grad = (out_grad * spread_scale).T.astype(BF)
            q_ref[here, cols] = queries
            do_ref[here, cols] = out_grad
            halo_grads.append((
                mm(grads[:far], both_heads(queries, 1, 0)),
                mm(raised[:far], both_heads(out_grad, 1, 0)),
            ))

        scores, slopes = multiply(0)
        waiting = None
        for a in range(tiles):
            ahead = multiply(a + 1) if a + 1 < tiles else None
            mixed = raise_and_mix(a, scores)
            if waiting is not None:
                finish(*waiting)
            waiting = (a, slopes, *mixed)
            if ahead is not None:
                scores, slopes = ahead
        finish(*waiting)
        for which, scale, out in ((0, math.log(2.0), dkh_ref), (1, 1.0, dvh_ref)):
            for j in range(WIN // TILE):
                total = None
                for a in range(min(j + 1, tiles)):
                    piece = halo_grads[a][which][(j - a) * TILE : (j - a + 1) * TILE]
                    total = piece if total is None else total + piece
                out[j * TILE : (j + 1) * TILE, cols] = (total * scale).astype(BF)
        return carry

    for copy in copies:
        copy.wait()
    dot_ref[...] = mm(cot_ref[...], wo_ref[...], NT).astype(BF).T
    lax.fori_loop(0, width // pair, one_pair, 0)
    back_ref[...] = (mm(dkh_ref[...], wk_ref[...], NT) + mm(dvh_ref[...], wv_ref[...], NT)).astype(BF)


def weights_body(
    scale, rows, head_size, meta_ref, normed_turned_ref, halo_t_ref, frames_ref, cot_hbm,
    wq_hbm, wk_hbm, wv_hbm, wo_hbm,
    q_ref, kt_ref, khalo_t_ref, ot, do_ref, raised_ref, grads_ref, scale_ref, dkh_ref, dvh_ref,
    keep_ref, send_ref, out_ref, slope_ref,
    normed_t, halo_t, mixed_t, ktx, dqt, dk, dv,
    wq, wk, wv, wo, cot_ref, sems,
):
    span, width = q_ref.shape
    copies = fetch(
        [wq_hbm, wk_hbm, wv_hbm, wo_hbm, cot_hbm], [wq, wk, wv, wo, cot_ref], sems
    )
    ktx[:, :WIN] = khalo_t_ref[...]
    ktx[:, WIN:] = kt_ref[...]
    pair = 2 * head_size
    tiles = span // TILE
    upper = iota2((pair, TILE), 0) < head_size

    def one_pair(p, carry):
        cols = pl.ds(pl.multiple_of(p * pair, pair), pair)
        own_grads = []
        for a in range(tiles):
            here = slice(a * TILE, (a + 1) * TILE)
            keys = slice(a * TILE, a * TILE + REACH)
            at = p * tiles + a
            shrink = scale_ref[at]
            moved = mm(ktx[cols, keys], grads_ref[at]) * (shrink * head_size ** (-0.5))
            dqt[cols, here] = jnp.where(upper, moved[:, :TILE], moved[:, TILE:]).astype(BF)
            near = slice(WIN - a * TILE, REACH)
            own_grads.append((
                mm(grads_ref[at, near], both_heads(q_ref[here, cols], 1, 0)),
                mm(raised_ref[at, near], both_heads(do_ref[here, cols], 1, 0)),
            ))
        for which, factor, out in ((0, math.log(2.0), dk), (1, 1.0, dv)):
            for j in range(tiles):
                total = None
                for a in range(j, tiles):
                    piece = own_grads[a][which][j * TILE : (j + 1) * TILE]
                    total = piece if total is None else total + piece
                out[j * TILE : (j + 1) * TILE, cols] = (total * factor).astype(BF)
        return carry

    lax.fori_loop(0, width // pair, one_pair, 0)

    for copy in copies:
        copy.wait()
    chunks = width // (2 * rows)
    split = (chunks, 2, rows, span)
    normed_t[...] = normed_turned_ref[...].reshape(split)
    halo_t[...] = halo_t_ref[...].reshape(split)
    mixed_t[...] = ot[...].reshape(split)
    mine = meta_ref[2]
    for side, out in ((1 - mine, send_ref), (mine, keep_ref)):
        own = normed_t[:, side].reshape(width // 2, span)
        far = halo_t[:, side].reshape(width // 2, span)
        mixed = mixed_t[:, side].reshape(width // 2, span)
        for n, total in enumerate((
            mm(own, dqt[...], NT),
            mm(own, dk[...]) + mm(far, dkh_ref[...]),
            mm(own, dv[...]) + mm(far, dvh_ref[...]),
            mm(mixed, cot_ref[...]),
        )):
            out[:, n * width : (n + 1) * width] = (total * scale).astype(BF)
    slope = mm(dqt[...].T, wq[...], NT)
    slope = slope + mm(dk[...], wk[...], NT)
    slope_ref[...] = slope + mm(dv[...], wv[...], NT)
    out = mm(ot[...].T, wo[...]) + frames_ref[...].astype(F32)
    out_ref[...] = out.astype(BF)


def returning_body(
    frames_ref, slope_ref, extra_ref, cot_hbm, pick_t_hbm, out_ref, cot_ref, pick_t_ref, sems
):
    copies = fetch([cot_hbm, pick_t_hbm], [cot_ref, pick_t_ref], sems)
    _, inverse, normed32 = unit_frames(frames_ref[...])
    slope = slope_ref[...] + extra_ref[...].astype(F32)
    centre = jnp.mean(slope * normed32, axis=1, keepdims=True)
    copies[0].wait()
    grad = inverse * (slope - normed32 * centre) + cot_ref[...].astype(F32)
    copies[1].wait()
    out_ref[...] = mm(pick_t_ref[...], grad.astype(BF)).astype(BF)


def arrived_body(placing_t_ref, in_ref, out_ref):
    out_ref[...] = mm(placing_t_ref[...], in_ref[...]).astype(BF)


def passed_along(shard, by):
    devices = lax.axis_size("seq")
    pairs = [(i, i + by) for i in range(devices) if 0 <= i + by < devices]
    return lax.ppermute(shard, "seq", pairs)


def spread_body(place_ref, *refs):
    parts = refs[0].shape[0]
    inputs, outs = refs[:-parts], refs[-parts:]
    for k, out in enumerate(outs):
        at = place_ref[0] ^ k
        total = inputs[0][at].astype(F32)
        for ref in inputs[1:]:
            total = total + ref[at].astype(F32)
        out[...] = total.astype(BF)


def spread(inputs, place, parts, carry=()):
    columns = inputs[0].shape[-1]
    inputs = [shard.reshape(parts, -1, columns) for shard in inputs]
    piece = sds(inputs[0].shape[1:])
    return vmem_call(spread_body, [piece] * parts, [place.reshape(1)] + inputs, smem=(0,), carry=carry)


def swapped(pieces, axis, step):
    count = lax.axis_size(axis)
    return [pieces[0]] + [
        lax.ppermute(piece, axis, [(i, i ^ (k * step)) for i in range(count)])
        for k, piece in enumerate(pieces[1:], 1)
    ]


def shards(
    frame_rows, row_frame, frame_owner, lengths,
    query_weight, key_weight, value_weight, out_weight, cotangent,
):
    devices = lax.axis_size(AXES)
    row_count, width = frame_rows.shape
    span = frame_owner.shape[1]
    slots = row_count // devices
    slab = span * lax.axis_size("seq")
    head_size = width // H
    cube = 2 * span * width * width
    square = sds((span, width))
    begin = (lax.axis_index("seq") * span).astype(jnp.int32)
    rows = width // devices
    in_kernel = rows % 16 == 0
    core = (lax.axis_index("seq") & 1).astype(jnp.int32)
    meta = jnp.stack([begin, lengths[0], core if in_kernel else jnp.zeros((), jnp.int32)])
    cot = cotangent[0]

    def exchanged(shard):
        got = lax.all_to_all(
            shard.reshape(devices, slots, width), AXES, split_axis=0, concat_axis=0, tiled=True
        )
        return got.reshape(devices * slots, width)

    outgoing, = vmem_call(
        lambda *refs: outgoing_body(span, slots, *refs),
        [square],
        [row_frame.reshape(1, row_count), frame_rows],
        hbm=(1,),
        scratch=[pltpu.VMEM((row_count, width), BF), pltpu.SemaphoreType.DMA((1,))],
        flops=cube,
    )
    incoming = exchanged(outgoing)
    pick, pick_t = vmem_call(
        lambda *refs: early_body(slots, *refs),
        [square, square],
        [frame_owner.reshape(span, 1)],
        flops=cube,
    )
    frames, normed = vmem_call(frames_body, [square, square], [pick, incoming], flops=cube)
    halo = passed_along(normed, 1)
    query_scale = head_size ** (-0.5) * math.log2(math.e)
    qt, k, kt, v, vt, wk, wv, normed_turned = vmem_call(
        lambda *refs: project_body(query_scale, *refs),
        [square] * 8,
        [normed, query_weight, key_weight, value_weight],
        hbm=(1, 2, 3),
        scratch=[pltpu.VMEM((width, width), BF), pltpu.SemaphoreType.DMA((3,))],
        flops=3 * cube,
    )
    units = H // 2 * (span // TILE)
    saved = sds((units, REACH, 2 * TILE))
    raised, grads, scales, q, do, dkh, dvh, khalo_t, halo_t, ot, back = vmem_call(
        lambda *refs: scores_body(head_size, *refs),
        [saved, saved, sds((units, 1, 2 * TILE), F32)] + [square] * 8,
        [meta, halo, wk, wv, qt, k, v, vt, cot, out_weight],
        smem=(0,),
        hbm=(8, 9),
        scratch=[pltpu.VMEM((WIN + span, width), BF)] * 2 + [pltpu.VMEM((width, WIN + span), BF)]
        + [pltpu.VMEM((width, span), BF)] * 3 + [pltpu.SemaphoreType.DMA((2,))],
        flops=12 * cube,
        limit=24,
    )
    extra = passed_along(back, -1)
    chunk = rows if in_kernel else width // 2
    split = pltpu.VMEM((width // (2 * chunk), 2, chunk, span), BF)
    half = sds((width // 2, 4 * width))
    whole = pltpu.VMEM((width, width), BF)
    keep, send, out_frames, slope = vmem_call(
        lambda *refs: weights_body(slab ** (-0.5), chunk, head_size, *refs),
        [half, half, square, sds((span, width), F32)],
        [meta, normed_turned, halo_t, frames, cot, query_weight, key_weight, value_weight, out_weight,
         q, kt, khalo_t, ot, do, raised, grads, scales, dkh, dvh],
        smem=(0,),
        hbm=(4, 5, 6, 7, 8),
        scratch=[split] * 3 + [pltpu.VMEM((width, WIN + span), BF)] + [whole] * 8
        + [pltpu.SemaphoreType.DMA((5,))],
        flops=18 * cube,
        limit=26,
    )
    send, extra = lax.optimization_barrier((send, extra))
    if not in_kernel:
        sums = jnp.concatenate([keep, send], axis=0).reshape(-1, 2, rows, 4 * width)
        keep = lax.dynamic_index_in_dim(sums, core, 1, keepdims=False).reshape(half.shape)
        send = lax.dynamic_index_in_dim(sums, 1 - core, 1, keepdims=False).reshape(half.shape)
    seqs = lax.axis_size("seq")
    got = lax.ppermute(send, "seq", [(i, i ^ 1) for i in range(seqs)])
    seqs = lax.axis_size("seq")
    got = lax.ppermute(send, "seq", [(i, i ^ 1) for i in range(seqs)])
    returning, = vmem_call(
        returning_body,
        [square],
        [frames, slope, extra, cot, pick_t],
        hbm=(3, 4),
        scratch=[whole, whole, pltpu.SemaphoreType.DMA((2,))],
        flops=cube,
    )
    pieces = spread([keep, got], lax.axis_index("stream"), lax.axis_size("stream"), [returning])
    pieces = swapped(pieces, "stream", 1)
    late_rows, returning = lax.optimization_barrier((row_frame.reshape(1, row_count), returning))
    arrived = exchanged(returning)
    placing_t, = vmem_call(
        lambda *refs: placing_t_body(span, slots, *refs),
        [sds((row_count, devices * slots))],
        [late_rows],
        flops=40 * cube,
    )
    frame_grads, = vmem_call(arrived_body, [square], [placing_t, arrived], flops=cube)
    pieces = swapped(spread(pieces, lax.axis_index("seq") >> 1, seqs // 2), "seq", 2)
    weight_grads = pieces[0].astype(F32)
    for piece in pieces[1:]:
        weight_grads = weight_grads + piece.astype(F32)
    return (out_frames[None], frame_grads, weight_grads)


def solution(mesh):
    return jax.shard_map(
        shards,
        mesh=mesh,
        in_specs=(
            P(AXES, None), P(AXES), P("stream", "seq"), P("stream"),
            P(), P(), P(), P(), P("stream", "seq", None),
        ),
        out_specs=(P("stream", "seq", None), P(AXES, None), P(AXES, None)),
        check_vma=False,
    )
```

```python
import math

import jax
import jax.numpy as jnp
from jax import lax
from jax.experimental import pallas as pl
from jax.experimental.pallas import tpu as pltpu
from jax.sharding import PartitionSpec as P

H = 8
WIN = 512
NEG = -1e30
EPS_NORM = 1e-06
AXES = ("stream", "seq")
BF = jnp.bfloat16
F32 = jnp.float32

NN = (((1,), (0,)), ((), ()))
NT = (((1,), (1,)), ((), ()))


def mm(a, b, dims=NN):
    return lax.dot_general(a, b, dims, preferred_element_type=F32)


def iota2(shape, dim):
    return lax.broadcasted_iota(jnp.int32, shape, dim)


def vmem_call(body, outs, args, smem=(), hbm=(), scratch=(), carry=(), flops=0, limit=12):
    used, inner, args = len(args), body, list(args) + list(carry)

    def body(*refs):
        inner(*refs[:used], *refs[len(args) :])

    spaces = [pltpu.SMEM if i in smem else pltpu.HBM if i in hbm else pltpu.VMEM for i in range(len(args))]
    size = sum(math.prod(a.shape) * a.dtype.itemsize for a in list(args) + list(outs))
    return pl.pallas_call(
        body,
        out_shape=tuple(outs),
        in_specs=[pl.BlockSpec(memory_space=space) for space in spaces],
        out_specs=tuple(pl.BlockSpec(memory_space=pltpu.VMEM) for _ in outs),
        scratch_shapes=list(scratch),
        compiler_params=pltpu.CompilerParams(vmem_limit_bytes=limit * 2**20),
        cost_estimate=pl.CostEstimate(flops=flops, bytes_accessed=size, transcendentals=0),
    )(*args)


def fetch(sources, targets, sems):
    copies = [
        pltpu.make_async_copy(source, target, sems.at[n])
        for n, (source, target) in enumerate(zip(sources, targets))
    ]
    for copy in copies:
        copy.start()
    return copies


def sds(shape, dtype=BF):
    return jax.ShapeDtypeStruct(shape, dtype)


def placing_of(span, slots, rf, total):
    count = rf.shape[1]
    target = jnp.where(rf >= 0, lax.div(rf, span), 1 << 20)
    slot = iota2((total, count), 0)
    owner = lax.div(slot, slots)
    rank = slot - owner * slots
    start = jnp.sum(jnp.where(target < owner, 1.0, 0.0), axis=1, keepdims=True)
    here = iota2((total, count), 1) - start.astype(jnp.int32)
    return jnp.where((target == owner) & (here == rank), 1.0, 0.0)


def outgoing_body(span, slots, rf_ref, rows_hbm, out_ref, rows_ref, sems):
    (rows_copy,) = fetch([rows_hbm], [rows_ref], sems)
    placing = placing_of(span, slots, rf_ref[...], out_ref.shape[0]).astype(BF)
    rows_copy.wait()
    out_ref[...] = mm(placing, rows_ref[...]).astype(BF)


def placing_t_body(span, slots, rf_ref, out_ref):
    out_ref[...] = placing_of(span, slots, rf_ref[...], out_ref.shape[1]).T.astype(BF)


def early_body(slots, owner_ref, pick_ref, pick_t_ref):
    span, lanes = owner_ref.shape[0], 128
    total = pick_ref.shape[1]
    owner = owner_ref[...]
    device = iota2((span, lanes), 1)
    hot = jnp.where(owner == device, 1.0, 0.0)
    strict = jnp.where(iota2((span, span), 1) < iota2((span, span), 0), 1.0, 0.0).astype(BF)
    before = mm(strict, hot.astype(BF))
    slot = jnp.sum(hot * (before + (device * slots).astype(F32)), axis=1, keepdims=True)
    slot = jnp.where(owner >= 0, slot.astype(jnp.int32), -1)
    pick = jnp.where(iota2((span, total), 1) == slot, 1.0, 0.0)
    pick_ref[...] = pick.astype(BF)
    pick_t_ref[...] = pick.T.astype(BF)


def unit_frames(frames):
    frames32 = frames.astype(F32)
    inverse = lax.rsqrt(jnp.mean(frames32 * frames32, axis=1, keepdims=True) + EPS_NORM)
    return frames32, inverse, frames32 * inverse


def frames_body(pick_ref, in_ref, frames_ref, normed_ref):
    frames = mm(pick_ref[...], in_ref[...]).astype(BF)
    frames_ref[...] = frames
    normed_ref[...] = unit_frames(frames)[2].astype(BF)


def project_body(
    query_scale, normed_ref, wq_hbm, wk_hbm, wv_hbm,
    qt_ref, k_ref, kt_ref, v_ref, vt_ref, wk_ref, wv_ref, normed_t_ref, wq_ref, sems,
):
    copies = fetch([wq_hbm, wk_hbm, wv_hbm], [wq_ref, wk_ref, wv_ref], sems)
    normed = normed_ref[...]
    normed_t_ref[...] = normed.T
    copies[0].wait()
    qt_ref[...] = (mm(normed, wq_ref[...]) * query_scale).astype(BF).T
    copies[1].wait()
    k = mm(normed, wk_ref[...]).astype(BF)
    k_ref[...] = k
    kt_ref[...] = k.T
    copies[2].wait()
    v = mm(normed, wv_ref[...]).astype(BF)
    v_ref[...] = v
    vt_ref[...] = v.T


TILE = 128
REACH = WIN + TILE


def raised_scores(scores, first, begin):
    row = iota2((TILE, TILE), 0)
    col = iota2((TILE, TILE), 1)
    halo_bias = jnp.where(begin == 0, NEG, 0.0)
    count = REACH // TILE
    raised_cols = []
    for h in range(2):
        at = slice(h * TILE, (h + 1) * TILE)
        parts = []
        for n in range(count):
            part = scores[n * TILE : (n + 1) * TILE, at]
            if n == 0:
                part = jnp.where(row > col, part, NEG)
            if n == count - 1:
                part = jnp.where(row <= col, part, NEG)
            elif first + n * TILE < WIN:
                part = part + halo_bias
            parts.append(part)
        peak = parts[0]
        for part in parts[1:]:
            peak = jnp.maximum(peak, part)
        peak = jnp.max(peak, axis=0, keepdims=True)
        raised_cols.append(jnp.concatenate([jnp.exp2((part - peak).astype(BF)) for part in parts], axis=0))
    return jnp.concatenate(raised_cols, axis=1)


def both_heads(value, axis, along):
    place = iota2(value.shape, axis)
    half = value.shape[axis] // 2
    zero = jnp.zeros((), value.dtype)
    return jnp.concatenate([jnp.where(place < half, value, zero), jnp.where(place < half, zero, value)], axis=along)


def scores_body(
    head_size, meta_ref, halo_ref, wk_ref, wv_ref, qt_ref, k_ref, v_ref, vt_ref, cot_hbm, wo_hbm,
    raised_ref, grads_ref, scale_ref, q_ref, do_ref, dkh_ref, dvh_ref, khalo_t_ref, halo_t_ref, ot_ref, back_ref,
    kx, vx, vtx, dot_ref, cot_ref, wo_ref, sems,
):
    copies = fetch([cot_hbm, wo_hbm], [cot_ref, wo_ref], sems)
    span, width = k_ref.shape
    begin, length = meta_ref[0], meta_ref[1]
    halo = halo_ref[...]
    kh = mm(halo, wk_ref[...]).astype(BF)
    kx[:WIN] = kh
    khalo_t_ref[...] = kh.T
    vh = mm(halo, wv_ref[...]).astype(BF)
    vx[:WIN] = vh
    vtx[:, :WIN] = vh.T
    vtx[:, WIN:] = vt_ref[...]
    halo_t_ref[...] = halo.T
    kx[WIN:] = k_ref[...]
    vx[WIN:] = v_ref[...]

    pair = 2 * head_size
    tiles = span // TILE
    upper = iota2((pair, TILE), 0) < head_size
    ones = jnp.ones((16, REACH), BF)

    def one_pair(p, carry):
        cols = pl.ds(pl.multiple_of(p * pair, pair), pair)

        def multiply(a):
            here = slice(a * TILE, (a + 1) * TILE)
            keys = slice(a * TILE, a * TILE + REACH)
            scores = mm(kx[keys, cols], both_heads(qt_ref[cols, here], 0, 1))
            slopes = mm(vx[keys, cols], both_heads(dot_ref[cols, here], 0, 1))
            return scores, slopes

        halo_grads = []

        def raise_and_mix(a, scores):
            here = slice(a * TILE, (a + 1) * TILE)
            keys = slice(a * TILE, a * TILE + REACH)
            raised = raised_scores(scores, a * TILE, begin)
            raised_ref[p * tiles + a] = raised
            mixed = mm(jnp.concatenate([vtx[cols, keys], ones], axis=0), raised)
            time = begin + a * TILE + iota2((1, 2 * TILE), 1) % TILE
            scale = jnp.where(time < length, 1.0 / mixed[pair : pair + 1], 0.0)
            scale_ref[p * tiles + a] = scale
            spread_scale = jnp.where(upper, scale[:, :TILE], scale[:, TILE:])
            mixed = jnp.where(upper, mixed[:pair, :TILE], mixed[:pair, TILE:]) * spread_scale
            ot_ref[cols, here] = mixed.astype(BF)
            return raised, mixed, spread_scale

        def finish(a, slopes, raised, mixed, spread_scale):
            here = slice(a * TILE, (a + 1) * TILE)
            out_grad = dot_ref[cols, here].astype(F32)
            product = mixed * out_grad
            grad_cols = []
            for h in range(2):
                at = slice(h * TILE, (h + 1) * TILE)
                centre = jnp.sum(product[h * head_size : (h + 1) * head_size], axis=0, keepdims=True)
                grad_cols.append(raised[:, at] * (slopes[:, at] - centre).astype(BF))
            grads = jnp.concatenate(grad_cols, axis=1)
            grads_ref[p * tiles + a] = grads
            far = WIN - a * TILE
            queries = (qt_ref[cols, here].astype(F32) * spread_scale).T.astype(BF)
            out_grad = (out_grad * spread_scale).T.astype(BF)
            q_ref[here, cols] = queries
            do_ref[here, cols] = out_grad
            halo_grads.append((
                mm(grads[:far], both_heads(queries, 1, 0)),
                mm(raised[:far], both_heads(out_grad, 1, 0)),
            ))

        scores, slopes = multiply(0)
        waiting = None
        for a in range(tiles):
            ahead = multiply(a + 1) if a + 1 < tiles else None
            mixed = raise_and_mix(a, scores)
            if waiting is not None:
                finish(*waiting)
            waiting = (a, slopes, *mixed)
            if ahead is not None:
                scores, slopes = ahead
        finish(*waiting)
        for which, scale, out in ((0, math.log(2.0), dkh_ref), (1, 1.0, dvh_ref)):
            for j in range(WIN // TILE):
                total = None
                for a in range(min(j + 1, tiles)):
                    piece = halo_grads[a][which][(j - a) * TILE : (j - a + 1) * TILE]
                    total = piece if total is None else total + piece
                out[j * TILE : (j + 1) * TILE, cols] = (total * scale).astype(BF)
        return carry

    for copy in copies:
        copy.wait()
    dot_ref[...] = mm(cot_ref[...], wo_ref[...], NT).astype(BF).T
    lax.fori_loop(0, width // pair, one_pair, 0)
    back_ref[...] = (mm(dkh_ref[...], wk_ref[...], NT) + mm(dvh_ref[...], wv_ref[...], NT)).astype(BF)


def weights_body(
    scale, rows, head_size, meta_ref, normed_turned_ref, halo_t_ref, frames_ref, cot_hbm,
    wq_hbm, wk_hbm, wv_hbm, wo_hbm,
    q_ref, kt_ref, khalo_t_ref, ot, do_ref, raised_ref, grads_ref, scale_ref, dkh_ref, dvh_ref,
    keep_ref, send_ref, out_ref, slope_ref,
    normed_t, halo_t, mixed_t, ktx, dqt, dk, dv,
    wq, wk, wv, wo, cot_ref, sems,
):
    span, width = q_ref.shape
    copies = fetch(
        [wq_hbm, wk_hbm, wv_hbm, wo_hbm, cot_hbm], [wq, wk, wv, wo, cot_ref], sems
    )
    ktx[:, :WIN] = khalo_t_ref[...]
    ktx[:, WIN:] = kt_ref[...]
    pair = 2 * head_size
    tiles = span // TILE
    upper = iota2((pair, TILE), 0) < head_size

    def one_pair(p, carry):
        cols = pl.ds(pl.multiple_of(p * pair, pair), pair)
        own_grads = []
        for a in range(tiles):
            here = slice(a * TILE, (a + 1) * TILE)
            keys = slice(a * TILE, a * TILE + REACH)
            at = p * tiles + a
            shrink = scale_ref[at]
            moved = mm(ktx[cols, keys], grads_ref[at]) * (shrink * head_size ** (-0.5))
            dqt[cols, here] = jnp.where(upper, moved[:, :TILE], moved[:, TILE:]).astype(BF)
            near = slice(WIN - a * TILE, REACH)
            own_grads.append((
                mm(grads_ref[at, near], both_heads(q_ref[here, cols], 1, 0)),
                mm(raised_ref[at, near], both_heads(do_ref[here, cols], 1, 0)),
            ))
        for which, factor, out in ((0, math.log(2.0), dk), (1, 1.0, dv)):
            for j in range(tiles):
                total = None
                for a in range(j, tiles):
                    piece = own_grads[a][which][j * TILE : (j + 1) * TILE]
                    total = piece if total is None else total + piece
                out[j * TILE : (j + 1) * TILE, cols] = (total * factor).astype(BF)
        return carry

    lax.fori_loop(0, width // pair, one_pair, 0)

    for copy in copies:
        copy.wait()
    chunks = width // (2 * rows)
    split = (chunks, 2, rows, span)
    normed_t[...] = normed_turned_ref[...].reshape(split)
    halo_t[...] = halo_t_ref[...].reshape(split)
    mixed_t[...] = ot[...].reshape(split)
    mine = meta_ref[2]
    for side, out in ((1 - mine, send_ref), (mine, keep_ref)):
        own = normed_t[:, side].reshape(width // 2, span)
        far = halo_t[:, side].reshape(width // 2, span)
        mixed = mixed_t[:, side].reshape(width // 2, span)
        for n, total in enumerate((
            mm(own, dqt[...], NT),
            mm(own, dk[...]) + mm(far, dkh_ref[...]),
            mm(own, dv[...]) + mm(far, dvh_ref[...]),
            mm(mixed, cot_ref[...]),
        )):
            out[:, n * width : (n + 1) * width] = (total * scale).astype(BF)
    slope = mm(dqt[...].T, wq[...], NT)
    slope = slope + mm(dk[...], wk[...], NT)
    slope_ref[...] = slope + mm(dv[...], wv[...], NT)
    out = mm(ot[...].T, wo[...]) + frames_ref[...].astype(F32)
    out_ref[...] = out.astype(BF)


def returning_body(
    frames_ref, slope_ref, extra_ref, cot_hbm, pick_t_hbm, out_ref, cot_ref, pick_t_ref, sems
):
    copies = fetch([cot_hbm, pick_t_hbm], [cot_ref, pick_t_ref], sems)
    _, inverse, normed32 = unit_frames(frames_ref[...])
    slope = slope_ref[...] + extra_ref[...].astype(F32)
    centre = jnp.mean(slope * normed32, axis=1, keepdims=True)
    copies[0].wait()
    grad = inverse * (slope - normed32 * centre) + cot_ref[...].astype(F32)
    copies[1].wait()
    out_ref[...] = mm(pick_t_ref[...], grad.astype(BF)).astype(BF)


def arrived_body(placing_t_ref, in_ref, out_ref):
    out_ref[...] = mm(placing_t_ref[...], in_ref[...]).astype(BF)


def passed_along(shard, by):
    devices = lax.axis_size("seq")
    pairs = [(i, i + by) for i in range(devices) if 0 <= i + by < devices]
    return lax.ppermute(shard, "seq", pairs)


def spread_body(place_ref, *refs):
    parts = refs[0].shape[0]
    inputs, outs = refs[:-parts], refs[-parts:]
    for k, out in enumerate(outs):
        at = place_ref[0] ^ k
        total = inputs[0][at].astype(F32)
        for ref in inputs[1:]:
            total = total + ref[at].astype(F32)
        out[...] = total.astype(BF)


def spread(inputs, place, parts, carry=()):
    columns = inputs[0].shape[-1]
    inputs = [shard.reshape(parts, -1, columns) for shard in inputs]
    piece = sds(inputs[0].shape[1:])
    return vmem_call(spread_body, [piece] * parts, [place.reshape(1)] + inputs, smem=(0,), carry=carry)


def swapped(pieces, axis, step):
    count = lax.axis_size(axis)
    return [pieces[0]] + [
        lax.ppermute(piece, axis, [(i, i ^ (k * step)) for i in range(count)])
        for k, piece in enumerate(pieces[1:], 1)
    ]


def shards(
    frame_rows, row_frame, frame_owner, lengths,
    query_weight, key_weight, value_weight, out_weight, cotangent,
):
    devices = lax.axis_size(AXES)
    row_count, width = frame_rows.shape
    span = frame_owner.shape[1]
    slots = row_count // devices
    slab = span * lax.axis_size("seq")
    head_size = width // H
    cube = 2 * span * width * width
    square = sds((span, width))
    begin = (lax.axis_index("seq") * span).astype(jnp.int32)
    rows = width // devices
    in_kernel = rows % 16 == 0
    core = (lax.axis_index("seq") & 1).astype(jnp.int32)
    meta = jnp.stack([begin, lengths[0], core if in_kernel else jnp.zeros((), jnp.int32)])
    cot = cotangent[0]

    def exchanged(shard):
        got = lax.all_to_all(
            shard.reshape(devices, slots, width), AXES, split_axis=0, concat_axis=0, tiled=True
        )
        return got.reshape(devices * slots, width)

    outgoing, = vmem_call(
        lambda *refs: outgoing_body(span, slots, *refs),
        [square],
        [row_frame.reshape(1, row_count), frame_rows],
        hbm=(1,),
        scratch=[pltpu.VMEM((row_count, width), BF), pltpu.SemaphoreType.DMA((1,))],
        flops=cube,
    )
    incoming = exchanged(outgoing)
    pick, pick_t = vmem_call(
        lambda *refs: early_body(slots, *refs),
        [square, square],
        [frame_owner.reshape(span, 1)],
        flops=cube,
    )
    frames, normed = vmem_call(frames_body, [square, square], [pick, incoming], flops=cube)
    halo = passed_along(normed, 1)
    query_scale = head_size ** (-0.5) * math.log2(math.e)
    qt, k, kt, v, vt, wk, wv, normed_turned = vmem_call(
        lambda *refs: project_body(query_scale, *refs),
        [square] * 8,
        [normed, query_weight, key_weight, value_weight],
        hbm=(1, 2, 3),
        scratch=[pltpu.VMEM((width, width), BF), pltpu.SemaphoreType.DMA((3,))],
        flops=3 * cube,
    )
    units = H // 2 * (span // TILE)
    saved = sds((units, REACH, 2 * TILE))
    raised, grads, scales, q, do, dkh, dvh, khalo_t, halo_t, ot, back = vmem_call(
        lambda *refs: scores_body(head_size, *refs),
        [saved, saved, sds((units, 1, 2 * TILE), F32)] + [square] * 8,
        [meta, halo, wk, wv, qt, k, v, vt, cot, out_weight],
        smem=(0,),
        hbm=(8, 9),
        scratch=[pltpu.VMEM((WIN + span, width), BF)] * 2 + [pltpu.VMEM((width, WIN + span), BF)]
        + [pltpu.VMEM((width, span), BF)] * 3 + [pltpu.SemaphoreType.DMA((2,))],
        flops=12 * cube,
        limit=24,
    )
    extra = passed_along(back, -1)
    chunk = rows if in_kernel else width // 2
    split = pltpu.VMEM((width // (2 * chunk), 2, chunk, span), BF)
    half = sds((width // 2, 4 * width))
    whole = pltpu.VMEM((width, width), BF)
    keep, send, out_frames, slope = vmem_call(
        lambda *refs: weights_body(slab ** (-0.5), chunk, head_size, *refs),
        [half, half, square, sds((span, width), F32)],
        [meta, normed_turned, halo_t, frames, cot, query_weight, key_weight, value_weight, out_weight,
         q, kt, khalo_t, ot, do, raised, grads, scales, dkh, dvh],
        smem=(0,),
        hbm=(4, 5, 6, 7, 8),
        scratch=[split] * 3 + [pltpu.VMEM((width, WIN + span), BF)] + [whole] * 8
        + [pltpu.SemaphoreType.DMA((5,))],
        flops=18 * cube,
        limit=26,
    )
    send, extra = lax.optimization_barrier((send, extra))
    if not in_kernel:
        sums = jnp.concatenate([keep, send], axis=0).reshape(-1, 2, rows, 4 * width)
        keep = lax.dynamic_index_in_dim(sums, core, 1, keepdims=False).reshape(half.shape)
        send = lax.dynamic_index_in_dim(sums, 1 - core, 1, keepdims=False).reshape(half.shape)
    seqs = lax.axis_size("seq")
    got = lax.ppermute(send, "seq", [(i, i ^ 1) for i in range(seqs)])
    seqs = lax.axis_size("seq")
    got = lax.ppermute(send, "seq", [(i, i ^ 1) for i in range(seqs)])
    returning, = vmem_call(
        returning_body,
        [square],
        [frames, slope, extra, cot, pick_t],
        hbm=(3, 4),
        scratch=[whole, whole, pltpu.SemaphoreType.DMA((2,))],
        flops=cube,
    )
    pieces = spread([keep, got], lax.axis_index("stream"), lax.axis_size("stream"))
    pieces = swapped(pieces, "stream", 1)
    late_rows, returning = lax.optimization_barrier((row_frame.reshape(1, row_count), returning))
    arrived = exchanged(returning)
    placing_t, = vmem_call(
        lambda *refs: placing_t_body(span, slots, *refs),
        [sds((row_count, devices * slots))],
        [late_rows],
        flops=40 * cube,
    )
    frame_grads, = vmem_call(arrived_body, [square], [placing_t, arrived], flops=cube)
    pieces = swapped(spread(pieces, lax.axis_index("seq") >> 1, seqs // 2), "seq", 2)
    weight_grads = pieces[0].astype(F32)
    for piece in pieces[1:]:
        weight_grads = weight_grads + piece.astype(F32)
    return (out_frames[None], frame_grads, weight_grads)


def solution(mesh):
    return jax.shard_map(
        shards,
        mesh=mesh,
        in_specs=(
            P(AXES, None), P(AXES), P("stream", "seq"), P("stream"),
            P(), P(), P(), P(), P("stream", "seq", None),
        ),
        out_specs=(P("stream", "seq", None), P(AXES, None), P(AXES, None)),
        check_vma=False,
    )
```

```python
import math

import jax
import jax.numpy as jnp
from jax import lax
from jax.experimental import pallas as pl
from jax.experimental.pallas import tpu as pltpu
from jax.sharding import PartitionSpec as P

H = 8
WIN = 512
NEG = -1e30
EPS_NORM = 1e-06
AXES = ("stream", "seq")
BF = jnp.bfloat16
F32 = jnp.float32

NN = (((1,), (0,)), ((), ()))
NT = (((1,), (1,)), ((), ()))


def mm(a, b, dims=NN):
    return lax.dot_general(a, b, dims, preferred_element_type=F32)


def iota2(shape, dim):
    return lax.broadcasted_iota(jnp.int32, shape, dim)


def vmem_call(body, outs, args, smem=(), hbm=(), scratch=(), carry=(), flops=0, limit=12):
    used, inner, args = len(args), body, list(args) + list(carry)

    def body(*refs):
        inner(*refs[:used], *refs[len(args) :])

    spaces = [pltpu.SMEM if i in smem else pltpu.HBM if i in hbm else pltpu.VMEM for i in range(len(args))]
    size = sum(math.prod(a.shape) * a.dtype.itemsize for a in list(args) + list(outs))
    return pl.pallas_call(
        body,
        out_shape=tuple(outs),
        in_specs=[pl.BlockSpec(memory_space=space) for space in spaces],
        out_specs=tuple(pl.BlockSpec(memory_space=pltpu.VMEM) for _ in outs),
        scratch_shapes=list(scratch),
        compiler_params=pltpu.CompilerParams(vmem_limit_bytes=limit * 2**20),
        cost_estimate=pl.CostEstimate(flops=flops, bytes_accessed=size, transcendentals=0),
    )(*args)


def fetch(sources, targets, sems):
    copies = [
        pltpu.make_async_copy(source, target, sems.at[n])
        for n, (source, target) in enumerate(zip(sources, targets))
    ]
    for copy in copies:
        copy.start()
    return copies


def sds(shape, dtype=BF):
    return jax.ShapeDtypeStruct(shape, dtype)


def placing_of(span, slots, rf, total):
    count = rf.shape[1]
    target = jnp.where(rf >= 0, lax.div(rf, span), 1 << 20)
    slot = iota2((total, count), 0)
    owner = lax.div(slot, slots)
    rank = slot - owner * slots
    start = jnp.sum(jnp.where(target < owner, 1.0, 0.0), axis=1, keepdims=True)
    here = iota2((total, count), 1) - start.astype(jnp.int32)
    return jnp.where((target == owner) & (here == rank), 1.0, 0.0)


def outgoing_body(span, slots, rf_ref, rows_hbm, out_ref, rows_ref, sems):
    (rows_copy,) = fetch([rows_hbm], [rows_ref], sems)
    placing = placing_of(span, slots, rf_ref[...], out_ref.shape[0]).astype(BF)
    rows_copy.wait()
    out_ref[...] = mm(placing, rows_ref[...]).astype(BF)


def placing_t_body(span, slots, rf_ref, out_ref):
    out_ref[...] = placing_of(span, slots, rf_ref[...], out_ref.shape[1]).T.astype(BF)


def early_body(slots, owner_ref, pick_ref, pick_t_ref):
    span, lanes = owner_ref.shape[0], 128
    total = pick_ref.shape[1]
    owner = owner_ref[...]
    device = iota2((span, lanes), 1)
    hot = jnp.where(owner == device, 1.0, 0.0)
    strict = jnp.where(iota2((span, span), 1) < iota2((span, span), 0), 1.0, 0.0).astype(BF)
    before = mm(strict, hot.astype(BF))
    slot = jnp.sum(hot * (before + (device * slots).astype(F32)), axis=1, keepdims=True)
    slot = jnp.where(owner >= 0, slot.astype(jnp.int32), -1)
    pick = jnp.where(iota2((span, total), 1) == slot, 1.0, 0.0)
    pick_ref[...] = pick.astype(BF)
    pick_t_ref[...] = pick.T.astype(BF)


def unit_frames(frames):
    frames32 = frames.astype(F32)
    inverse = lax.rsqrt(jnp.mean(frames32 * frames32, axis=1, keepdims=True) + EPS_NORM)
    return frames32, inverse, frames32 * inverse


def frames_body(pick_ref, in_ref, frames_ref, normed_ref):
    frames = mm(pick_ref[...], in_ref[...]).astype(BF)
    frames_ref[...] = frames
    normed_ref[...] = unit_frames(frames)[2].astype(BF)


def project_body(
    query_scale, normed_ref, wq_hbm, wk_hbm, wv_hbm,
    qt_ref, k_ref, kt_ref, v_ref, vt_ref, wk_ref, wv_ref, normed_t_ref, wq_ref, sems,
):
    copies = fetch([wq_hbm, wk_hbm, wv_hbm], [wq_ref, wk_ref, wv_ref], sems)
    normed = normed_ref[...]
    normed_t_ref[...] = normed.T
    copies[0].wait()
    qt_ref[...] = (mm(normed, wq_ref[...]) * query_scale).astype(BF).T
    copies[1].wait()
    k = mm(normed, wk_ref[...]).astype(BF)
    k_ref[...] = k
    kt_ref[...] = k.T
    copies[2].wait()
    v = mm(normed, wv_ref[...]).astype(BF)
    v_ref[...] = v
    vt_ref[...] = v.T


TILE = 128
REACH = WIN + TILE


def raised_scores(scores, first, begin):
    row = iota2((TILE, TILE), 0)
    col = iota2((TILE, TILE), 1)
    halo_bias = jnp.where(begin == 0, NEG, 0.0)
    count = REACH // TILE
    raised_cols = []
    for h in range(2):
        at = slice(h * TILE, (h + 1) * TILE)
        parts = []
        for n in range(count):
            part = scores[n * TILE : (n + 1) * TILE, at]
            if n == 0:
                part = jnp.where(row > col, part, NEG)
            if n == count - 1:
                part = jnp.where(row <= col, part, NEG)
            elif first + n * TILE < WIN:
                part = part + halo_bias
            parts.append(part)
        peak = parts[0]
        for part in parts[1:]:
            peak = jnp.maximum(peak, part)
        peak = jnp.max(peak, axis=0, keepdims=True)
        raised_cols.append(jnp.concatenate([jnp.exp2((part - peak).astype(BF)) for part in parts], axis=0))
    return jnp.concatenate(raised_cols, axis=1)


def both_heads(value, axis, along):
    place = iota2(value.shape, axis)
    half = value.shape[axis] // 2
    zero = jnp.zeros((), value.dtype)
    return jnp.concatenate([jnp.where(place < half, value, zero), jnp.where(place < half, zero, value)], axis=along)


def scores_body(
    head_size, meta_ref, halo_ref, wk_ref, wv_ref, qt_ref, k_ref, v_ref, vt_ref, cot_hbm, wo_hbm,
    raised_ref, grads_ref, scale_ref, q_ref, do_ref, dkh_ref, dvh_ref, khalo_t_ref, halo_t_ref, ot_ref, back_ref,
    kx, vx, vtx, dot_ref, cot_ref, wo_ref, sems,
):
    copies = fetch([cot_hbm, wo_hbm], [cot_ref, wo_ref], sems)
    span, width = k_ref.shape
    begin, length = meta_ref[0], meta_ref[1]
    halo = halo_ref[...]
    kh = mm(halo, wk_ref[...]).astype(BF)
    kx[:WIN] = kh
    khalo_t_ref[...] = kh.T
    vh = mm(halo, wv_ref[...]).astype(BF)
    vx[:WIN] = vh
    vtx[:, :WIN] = vh.T
    vtx[:, WIN:] = vt_ref[...]
    halo_t_ref[...] = halo.T
    kx[WIN:] = k_ref[...]
    vx[WIN:] = v_ref[...]

    pair = 2 * head_size
    tiles = span // TILE
    upper = iota2((pair, TILE), 0) < head_size
    ones = jnp.ones((16, REACH), BF)

    def one_pair(p, carry):
        cols = pl.ds(pl.multiple_of(p * pair, pair), pair)

        def multiply(a):
            here = slice(a * TILE, (a + 1) * TILE)
            keys = slice(a * TILE, a * TILE + REACH)
            scores = mm(kx[keys, cols], both_heads(qt_ref[cols, here], 0, 1))
            slopes = mm(vx[keys, cols], both_heads(dot_ref[cols, here], 0, 1))
            return scores, slopes

        halo_grads = []

        def raise_and_mix(a, scores):
            here = slice(a * TILE, (a + 1) * TILE)
            keys = slice(a * TILE, a * TILE + REACH)
            raised = raised_scores(scores, a * TILE, begin)
            raised_ref[p * tiles + a] = raised
            mixed = mm(jnp.concatenate([vtx[cols, keys], ones], axis=0), raised)
            time = begin + a * TILE + iota2((1, 2 * TILE), 1) % TILE
            scale = jnp.where(time < length, 1.0 / mixed[pair : pair + 1], 0.0)
            scale_ref[p * tiles + a] = scale
            spread_scale = jnp.where(upper, scale[:, :TILE], scale[:, TILE:])
            mixed = jnp.where(upper, mixed[:pair, :TILE], mixed[:pair, TILE:]) * spread_scale
            ot_ref[cols, here] = mixed.astype(BF)
            return raised, mixed, spread_scale

        def finish(a, slopes, raised, mixed, spread_scale):
            here = slice(a * TILE, (a + 1) * TILE)
            out_grad = dot_ref[cols, here].astype(F32)
            product = mixed * out_grad
            grad_cols = []
            for h in range(2):
                at = slice(h * TILE, (h + 1) * TILE)
                centre = jnp.sum(product[h * head_size : (h + 1) * head_size], axis=0, keepdims=True)
                grad_cols.append(raised[:, at] * (slopes[:, at] - centre).astype(BF))
            grads = jnp.concatenate(grad_cols, axis=1)
            grads_ref[p * tiles + a] = grads
            far = WIN - a * TILE
            queries = (qt_ref[cols, here].astype(F32) * spread_scale).T.astype(BF)
            out_grad = (out_grad * spread_scale).T.astype(BF)
            q_ref[here, cols] = queries
            do_ref[here, cols] = out_grad
            halo_grads.append((
                mm(grads[:far], both_heads(queries, 1, 0)),
                mm(raised[:far], both_heads(out_grad, 1, 0)),
            ))

        scores, slopes = multiply(0)
        waiting = None
        for a in range(tiles):
            ahead = multiply(a + 1) if a + 1 < tiles else None
            mixed = raise_and_mix(a, scores)
            if waiting is not None:
                finish(*waiting)
            waiting = (a, slopes, *mixed)
            if ahead is not None:
                scores, slopes = ahead
        finish(*waiting)
        for which, scale, out in ((0, math.log(2.0), dkh_ref), (1, 1.0, dvh_ref)):
            for j in range(WIN // TILE):
                total = None
                for a in range(min(j + 1, tiles)):
                    piece = halo_grads[a][which][(j - a) * TILE : (j - a + 1) * TILE]
                    total = piece if total is None else total + piece
                out[j * TILE : (j + 1) * TILE, cols] = (total * scale).astype(BF)
        return carry

    for copy in copies:
        copy.wait()
    dot_ref[...] = mm(cot_ref[...], wo_ref[...], NT).astype(BF).T
    lax.fori_loop(0, width // pair, one_pair, 0)
    back_ref[...] = (mm(dkh_ref[...], wk_ref[...], NT) + mm(dvh_ref[...], wv_ref[...], NT)).astype(BF)


def weights_body(
    scale, rows, head_size, meta_ref, normed_turned_ref, halo_t_ref, frames_ref, cot_hbm,
    wq_hbm, wk_hbm, wv_hbm, wo_hbm,
    q_ref, kt_ref, khalo_t_ref, ot, do_ref, raised_ref, grads_ref, scale_ref, dkh_ref, dvh_ref,
    keep_ref, send_ref, out_ref, slope_ref,
    normed_t, halo_t, mixed_t, ktx, dqt, dk, dv,
    wq, wk, wv, wo, cot_ref, sems,
):
    span, width = q_ref.shape
    copies = fetch(
        [wq_hbm, wk_hbm, wv_hbm, wo_hbm, cot_hbm], [wq, wk, wv, wo, cot_ref], sems
    )
    ktx[:, :WIN] = khalo_t_ref[...]
    ktx[:, WIN:] = kt_ref[...]
    pair = 2 * head_size
    tiles = span // TILE
    upper = iota2((pair, TILE), 0) < head_size

    def one_pair(p, carry):
        cols = pl.ds(pl.multiple_of(p * pair, pair), pair)
        own_grads = []
        for a in range(tiles):
            here = slice(a * TILE, (a + 1) * TILE)
            keys = slice(a * TILE, a * TILE + REACH)
            at = p * tiles + a
            shrink = scale_ref[at]
            moved = mm(ktx[cols, keys], grads_ref[at]) * (shrink * head_size ** (-0.5))
            dqt[cols, here] = jnp.where(upper, moved[:, :TILE], moved[:, TILE:]).astype(BF)
            near = slice(WIN - a * TILE, REACH)
            own_grads.append((
                mm(grads_ref[at, near], both_heads(q_ref[here, cols], 1, 0)),
                mm(raised_ref[at, near], both_heads(do_ref[here, cols], 1, 0)),
            ))
        for which, factor, out in ((0, math.log(2.0), dk), (1, 1.0, dv)):
            for j in range(tiles):
                total = None
                for a in range(j, tiles):
                    piece = own_grads[a][which][j * TILE : (j + 1) * TILE]
                    total = piece if total is None else total + piece
                out[j * TILE : (j + 1) * TILE, cols] = (total * factor).astype(BF)
        return carry

    lax.fori_loop(0, width // pair, one_pair, 0)

    for copy in copies:
        copy.wait()
    chunks = width // (2 * rows)
    split = (chunks, 2, rows, span)
    normed_t[...] = normed_turned_ref[...].reshape(split)
    halo_t[...] = halo_t_ref[...].reshape(split)
    mixed_t[...] = ot[...].reshape(split)
    mine = meta_ref[2]
    for side, out in ((1 - mine, send_ref), (mine, keep_ref)):
        own = normed_t[:, side].reshape(width // 2, span)
        far = halo_t[:, side].reshape(width // 2, span)
        mixed = mixed_t[:, side].reshape(width // 2, span)
        for n, total in enumerate((
            mm(own, dqt[...], NT),
            mm(own, dk[...]) + mm(far, dkh_ref[...]),
            mm(own, dv[...]) + mm(far, dvh_ref[...]),
            mm(mixed, cot_ref[...]),
        )):
            out[:, n * width : (n + 1) * width] = (total * scale).astype(BF)
    slope = mm(dqt[...].T, wq[...], NT)
    slope = slope + mm(dk[...], wk[...], NT)
    slope_ref[...] = slope + mm(dv[...], wv[...], NT)
    out = mm(ot[...].T, wo[...]) + frames_ref[...].astype(F32)
    out_ref[...] = out.astype(BF)


def returning_body(
    frames_ref, slope_ref, extra_ref, cot_ref, pick_t_ref, out_ref
):
    _, inverse, normed32 = unit_frames(frames_ref[...])
    slope = slope_ref[...] + extra_ref[...].astype(F32)
    centre = jnp.mean(slope * normed32, axis=1, keepdims=True)
    grad = inverse * (slope - normed32 * centre) + cot_ref[...].astype(F32)
    out_ref[...] = mm(pick_t_ref[...], grad.astype(BF)).astype(BF)


def arrived_body(placing_t_ref, in_ref, out_ref):
    out_ref[...] = mm(placing_t_ref[...], in_ref[...]).astype(BF)


def passed_along(shard, by):
    devices = lax.axis_size("seq")
    pairs = [(i, i + by) for i in range(devices) if 0 <= i + by < devices]
    return lax.ppermute(shard, "seq", pairs)


def spread_body(place_ref, *refs):
    parts = refs[0].shape[0]
    inputs, outs = refs[:-parts], refs[-parts:]
    for k, out in enumerate(outs):
        at = place_ref[0] ^ k
        total = inputs[0][at].astype(F32)
        for ref in inputs[1:]:
            total = total + ref[at].astype(F32)
        out[...] = total.astype(BF)


def spread(inputs, place, parts, carry=()):
    columns = inputs[0].shape[-1]
    inputs = [shard.reshape(parts, -1, columns) for shard in inputs]
    piece = sds(inputs[0].shape[1:])
    return vmem_call(spread_body, [piece] * parts, [place.reshape(1)] + inputs, smem=(0,), carry=carry)


def swapped(pieces, axis, step):
    count = lax.axis_size(axis)
    return [pieces[0]] + [
        lax.ppermute(piece, axis, [(i, i ^ (k * step)) for i in range(count)])
        for k, piece in enumerate(pieces[1:], 1)
    ]


def shards(
    frame_rows, row_frame, frame_owner, lengths,
    query_weight, key_weight, value_weight, out_weight, cotangent,
):
    devices = lax.axis_size(AXES)
    row_count, width = frame_rows.shape
    span = frame_owner.shape[1]
    slots = row_count // devices
    slab = span * lax.axis_size("seq")
    head_size = width // H
    cube = 2 * span * width * width
    square = sds((span, width))
    begin = (lax.axis_index("seq") * span).astype(jnp.int32)
    rows = width // devices
    in_kernel = rows % 16 == 0
    core = (lax.axis_index("seq") & 1).astype(jnp.int32)
    meta = jnp.stack([begin, lengths[0], core if in_kernel else jnp.zeros((), jnp.int32)])
    cot = cotangent[0]

    def exchanged(shard):
        got = lax.all_to_all(
            shard.reshape(devices, slots, width), AXES, split_axis=0, concat_axis=0, tiled=True
        )
        return got.reshape(devices * slots, width)

    outgoing, = vmem_call(
        lambda *refs: outgoing_body(span, slots, *refs),
        [square],
        [row_frame.reshape(1, row_count), frame_rows],
        hbm=(1,),
        scratch=[pltpu.VMEM((row_count, width), BF), pltpu.SemaphoreType.DMA((1,))],
        flops=cube,
    )
    incoming = exchanged(outgoing)
    pick, pick_t = vmem_call(
        lambda *refs: early_body(slots, *refs),
        [square, square],
        [frame_owner.reshape(span, 1)],
        flops=cube,
    )
    frames, normed = vmem_call(frames_body, [square, square], [pick, incoming], flops=cube)
    halo = passed_along(normed, 1)
    query_scale = head_size ** (-0.5) * math.log2(math.e)
    qt, k, kt, v, vt, wk, wv, normed_turned = vmem_call(
        lambda *refs: project_body(query_scale, *refs),
        [square] * 8,
        [normed, query_weight, key_weight, value_weight],
        hbm=(1, 2, 3),
        scratch=[pltpu.VMEM((width, width), BF), pltpu.SemaphoreType.DMA((3,))],
        flops=3 * cube,
    )
    units = H // 2 * (span // TILE)
    saved = sds((units, REACH, 2 * TILE))
    raised, grads, scales, q, do, dkh, dvh, khalo_t, halo_t, ot, back = vmem_call(
        lambda *refs: scores_body(head_size, *refs),
        [saved, saved, sds((units, 1, 2 * TILE), F32)] + [square] * 8,
        [meta, halo, wk, wv, qt, k, v, vt, cot, out_weight],
        smem=(0,),
        hbm=(8, 9),
        scratch=[pltpu.VMEM((WIN + span, width), BF)] * 2 + [pltpu.VMEM((width, WIN + span), BF)]
        + [pltpu.VMEM((width, span), BF)] * 3 + [pltpu.SemaphoreType.DMA((2,))],
        flops=12 * cube,
        limit=24,
    )
    extra = passed_along(back, -1)
    chunk = rows if in_kernel else width // 2
    split = pltpu.VMEM((width // (2 * chunk), 2, chunk, span), BF)
    half = sds((width // 2, 4 * width))
    whole = pltpu.VMEM((width, width), BF)
    keep, send, out_frames, slope = vmem_call(
        lambda *refs: weights_body(slab ** (-0.5), chunk, head_size, *refs),
        [half, half, square, sds((span, width), F32)],
        [meta, normed_turned, halo_t, frames, cot, query_weight, key_weight, value_weight, out_weight,
         q, kt, khalo_t, ot, do, raised, grads, scales, dkh, dvh],
        smem=(0,),
        hbm=(4, 5, 6, 7, 8),
        scratch=[split] * 3 + [pltpu.VMEM((width, WIN + span), BF)] + [whole] * 8
        + [pltpu.SemaphoreType.DMA((5,))],
        flops=18 * cube,
        limit=26,
    )
    if not in_kernel:
        sums = jnp.concatenate([keep, send], axis=0).reshape(-1, 2, rows, 4 * width)
        keep = lax.dynamic_index_in_dim(sums, core, 1, keepdims=False).reshape(half.shape)
        send = lax.dynamic_index_in_dim(sums, 1 - core, 1, keepdims=False).reshape(half.shape)
    seqs = lax.axis_size("seq")
    got = lax.ppermute(send, "seq", [(i, i ^ 1) for i in range(seqs)])
    seqs = lax.axis_size("seq")
    got = lax.ppermute(send, "seq", [(i, i ^ 1) for i in range(seqs)])
    returning, = vmem_call(
        returning_body,
        [square],
        [frames, slope, extra, cot, pick_t],
        flops=40 * cube,
    )
    pieces = spread([keep, got], lax.axis_index("stream"), lax.axis_size("stream"), [returning])
    pieces = swapped(pieces, "stream", 1)
    late_rows, returning = lax.optimization_barrier((row_frame.reshape(1, row_count), returning))
    arrived = exchanged(returning)
    placing_t, = vmem_call(
        lambda *refs: placing_t_body(span, slots, *refs),
        [sds((row_count, devices * slots))],
        [late_rows],
        flops=40 * cube,
    )
    frame_grads, = vmem_call(arrived_body, [square], [placing_t, arrived], flops=cube)
    pieces = swapped(spread(pieces, lax.axis_index("seq") >> 1, seqs // 2), "seq", 2)
    weight_grads = pieces[0].astype(F32)
    for piece in pieces[1:]:
        weight_grads = weight_grads + piece.astype(F32)
    return (out_frames[None], frame_grads, weight_grads)


def solution(mesh):
    return jax.shard_map(
        shards,
        mesh=mesh,
        in_specs=(
            P(AXES, None), P(AXES), P("stream", "seq"), P("stream"),
            P(), P(), P(), P(), P("stream", "seq", None),
        ),
        out_specs=(P("stream", "seq", None), P(AXES, None), P(AXES, None)),
        check_vma=False,
    )
```

```python
import math

import jax
import jax.numpy as jnp
from jax import lax
from jax.experimental import pallas as pl
from jax.experimental.pallas import tpu as pltpu
from jax.sharding import PartitionSpec as P

H = 8
WIN = 512
NEG = -1e30
EPS_NORM = 1e-06
AXES = ("stream", "seq")
BF = jnp.bfloat16
F32 = jnp.float32

NN = (((1,), (0,)), ((), ()))
NT = (((1,), (1,)), ((), ()))


def mm(a, b, dims=NN):
    return lax.dot_general(a, b, dims, preferred_element_type=F32)


def iota2(shape, dim):
    return lax.broadcasted_iota(jnp.int32, shape, dim)


def vmem_call(body, outs, args, smem=(), hbm=(), scratch=(), carry=(), flops=0, limit=12):
    used, inner, args = len(args), body, list(args) + list(carry)

    def body(*refs):
        inner(*refs[:used], *refs[len(args) :])

    spaces = [pltpu.SMEM if i in smem else pltpu.HBM if i in hbm else pltpu.VMEM for i in range(len(args))]
    size = sum(math.prod(a.shape) * a.dtype.itemsize for a in list(args) + list(outs))
    return pl.pallas_call(
        body,
        out_shape=tuple(outs),
        in_specs=[pl.BlockSpec(memory_space=space) for space in spaces],
        out_specs=tuple(pl.BlockSpec(memory_space=pltpu.VMEM) for _ in outs),
        scratch_shapes=list(scratch),
        compiler_params=pltpu.CompilerParams(vmem_limit_bytes=limit * 2**20),
        cost_estimate=pl.CostEstimate(flops=flops, bytes_accessed=size, transcendentals=0),
    )(*args)


def fetch(sources, targets, sems):
    copies = [
        pltpu.make_async_copy(source, target, sems.at[n])
        for n, (source, target) in enumerate(zip(sources, targets))
    ]
    for copy in copies:
        copy.start()
    return copies


def sds(shape, dtype=BF):
    return jax.ShapeDtypeStruct(shape, dtype)


def placing_of(span, slots, rf, total):
    count = rf.shape[1]
    target = jnp.where(rf >= 0, lax.div(rf, span), 1 << 20)
    slot = iota2((total, count), 0)
    owner = lax.div(slot, slots)
    rank = slot - owner * slots
    start = jnp.sum(jnp.where(target < owner, 1.0, 0.0), axis=1, keepdims=True)
    here = iota2((total, count), 1) - start.astype(jnp.int32)
    return jnp.where((target == owner) & (here == rank), 1.0, 0.0)


def outgoing_body(span, slots, rf_ref, rows_hbm, out_ref, rows_ref, sems):
    (rows_copy,) = fetch([rows_hbm], [rows_ref], sems)
    placing = placing_of(span, slots, rf_ref[...], out_ref.shape[0]).astype(BF)
    rows_copy.wait()
    out_ref[...] = mm(placing, rows_ref[...]).astype(BF)


def placing_t_body(span, slots, rf_ref, out_ref):
    out_ref[...] = placing_of(span, slots, rf_ref[...], out_ref.shape[1]).T.astype(BF)


def early_body(slots, owner_ref, pick_ref, pick_t_ref):
    span, lanes = owner_ref.shape[0], 128
    total = pick_ref.shape[1]
    owner = owner_ref[...]
    device = iota2((span, lanes), 1)
    hot = jnp.where(owner == device, 1.0, 0.0)
    strict = jnp.where(iota2((span, span), 1) < iota2((span, span), 0), 1.0, 0.0).astype(BF)
    before = mm(strict, hot.astype(BF))
    slot = jnp.sum(hot * (before + (device * slots).astype(F32)), axis=1, keepdims=True)
    slot = jnp.where(owner >= 0, slot.astype(jnp.int32), -1)
    pick = jnp.where(iota2((span, total), 1) == slot, 1.0, 0.0)
    pick_ref[...] = pick.astype(BF)
    pick_t_ref[...] = pick.T.astype(BF)


def unit_frames(frames):
    frames32 = frames.astype(F32)
    inverse = lax.rsqrt(jnp.mean(frames32 * frames32, axis=1, keepdims=True) + EPS_NORM)
    return frames32, inverse, frames32 * inverse


def frames_body(pick_ref, in_ref, frames_ref, normed_ref):
    frames = mm(pick_ref[...], in_ref[...]).astype(BF)
    frames_ref[...] = frames
    normed_ref[...] = unit_frames(frames)[2].astype(BF)


def project_body(
    query_scale, normed_ref, wq_hbm, wk_hbm, wv_hbm,
    qt_ref, k_ref, kt_ref, v_ref, vt_ref, wk_ref, wv_ref, normed_t_ref, wq_ref, sems,
):
    copies = fetch([wq_hbm, wk_hbm, wv_hbm], [wq_ref, wk_ref, wv_ref], sems)
    normed = normed_ref[...]
    normed_t_ref[...] = normed.T
    copies[0].wait()
    qt_ref[...] = (mm(normed, wq_ref[...]) * query_scale).astype(BF).T
    copies[1].wait()
    k = mm(normed, wk_ref[...]).astype(BF)
    k_ref[...] = k
    kt_ref[...] = k.T
    copies[2].wait()
    v = mm(normed, wv_ref[...]).astype(BF)
    v_ref[...] = v
    vt_ref[...] = v.T


TILE = 128
REACH = WIN + TILE


def raised_scores(scores, first, begin):
    row = iota2((TILE, TILE), 0)
    col = iota2((TILE, TILE), 1)
    halo_bias = jnp.where(begin == 0, NEG, 0.0)
    count = REACH // TILE
    raised_cols = []
    for h in range(2):
        at = slice(h * TILE, (h + 1) * TILE)
        parts = []
        for n in range(count):
            part = scores[n * TILE : (n + 1) * TILE, at]
            if n == 0:
                part = jnp.where(row > col, part, NEG)
            if n == count - 1:
                part = jnp.where(row <= col, part, NEG)
            elif first + n * TILE < WIN:
                part = part + halo_bias
            parts.append(part)
        peak = parts[0]
        for part in parts[1:]:
            peak = jnp.maximum(peak, part)
        peak = jnp.max(peak, axis=0, keepdims=True)
        raised_cols.append(jnp.concatenate([jnp.exp2((part - peak).astype(BF)) for part in parts], axis=0))
    return jnp.concatenate(raised_cols, axis=1)


def both_heads(value, axis, along):
    place = iota2(value.shape, axis)
    half = value.shape[axis] // 2
    zero = jnp.zeros((), value.dtype)
    return jnp.concatenate([jnp.where(place < half, value, zero), jnp.where(place < half, zero, value)], axis=along)


def scores_body(
    head_size, meta_ref, halo_ref, wk_ref, wv_ref, qt_ref, k_ref, v_ref, vt_ref, cot_hbm, wo_hbm,
    raised_ref, grads_ref, scale_ref, q_ref, do_ref, dkh_ref, dvh_ref, khalo_t_ref, halo_t_ref, ot_ref, back_ref,
    kx, vx, vtx, dot_ref, cot_ref, wo_ref, sems,
):
    copies = fetch([cot_hbm, wo_hbm], [cot_ref, wo_ref], sems)
    span, width = k_ref.shape
    begin, length = meta_ref[0], meta_ref[1]
    halo = halo_ref[...]
    kh = mm(halo, wk_ref[...]).astype(BF)
    kx[:WIN] = kh
    khalo_t_ref[...] = kh.T
    vh = mm(halo, wv_ref[...]).astype(BF)
    vx[:WIN] = vh
    vtx[:, :WIN] = vh.T
    vtx[:, WIN:] = vt_ref[...]
    halo_t_ref[...] = halo.T
    kx[WIN:] = k_ref[...]
    vx[WIN:] = v_ref[...]

    pair = 2 * head_size
    tiles = span // TILE
    upper = iota2((pair, TILE), 0) < head_size
    ones = jnp.ones((16, REACH), BF)

    def one_pair(p, carry):
        cols = pl.ds(pl.multiple_of(p * pair, pair), pair)

        def multiply(a):
            here = slice(a * TILE, (a + 1) * TILE)
            keys = slice(a * TILE, a * TILE + REACH)
            scores = mm(kx[keys, cols], both_heads(qt_ref[cols, here], 0, 1))
            slopes = mm(vx[keys, cols], both_heads(dot_ref[cols, here], 0, 1))
            return scores, slopes

        halo_grads = []

        def raise_and_mix(a, scores):
            here = slice(a * TILE, (a + 1) * TILE)
            keys = slice(a * TILE, a * TILE + REACH)
            raised = raised_scores(scores, a * TILE, begin)
            raised_ref[p * tiles + a] = raised
            mixed = mm(jnp.concatenate([vtx[cols, keys], ones], axis=0), raised)
            time = begin + a * TILE + iota2((1, 2 * TILE), 1) % TILE
            scale = jnp.where(time < length, 1.0 / mixed[pair : pair + 1], 0.0)
            scale_ref[p * tiles + a] = scale
            spread_scale = jnp.where(upper, scale[:, :TILE], scale[:, TILE:])
            mixed = jnp.where(upper, mixed[:pair, :TILE], mixed[:pair, TILE:]) * spread_scale
            ot_ref[cols, here] = mixed.astype(BF)
            return raised, mixed, spread_scale

        def finish(a, slopes, raised, mixed, spread_scale):
            here = slice(a * TILE, (a + 1) * TILE)
            out_grad = dot_ref[cols, here].astype(F32)
            product = mixed * out_grad
            grad_cols = []
            for h in range(2):
                at = slice(h * TILE, (h + 1) * TILE)
                centre = jnp.sum(product[h * head_size : (h + 1) * head_size], axis=0, keepdims=True)
                grad_cols.append(raised[:, at] * (slopes[:, at] - centre).astype(BF))
            grads = jnp.concatenate(grad_cols, axis=1)
            grads_ref[p * tiles + a] = grads
            far = WIN - a * TILE
            queries = (qt_ref[cols, here].astype(F32) * spread_scale).T.astype(BF)
            out_grad = (out_grad * spread_scale).T.astype(BF)
            q_ref[here, cols] = queries
            do_ref[here, cols] = out_grad
            halo_grads.append((
                mm(grads[:far], both_heads(queries, 1, 0)),
                mm(raised[:far], both_heads(out_grad, 1, 0)),
            ))

        scores, slopes = multiply(0)
        waiting = None
        for a in range(tiles):
            ahead = multiply(a + 1) if a + 1 < tiles else None
            mixed = raise_and_mix(a, scores)
            if waiting is not None:
                finish(*waiting)
            waiting = (a, slopes, *mixed)
            if ahead is not None:
                scores, slopes = ahead
        finish(*waiting)
        for which, scale, out in ((0, math.log(2.0), dkh_ref), (1, 1.0, dvh_ref)):
            for j in range(WIN // TILE):
                total = None
                for a in range(min(j + 1, tiles)):
                    piece = halo_grads[a][which][(j - a) * TILE : (j - a + 1) * TILE]
                    total = piece if total is None else total + piece
                out[j * TILE : (j + 1) * TILE, cols] = (total * scale).astype(BF)
        return carry

    for copy in copies:
        copy.wait()
    dot_ref[...] = mm(cot_ref[...], wo_ref[...], NT).astype(BF).T
    lax.fori_loop(0, width // pair, one_pair, 0)
    back_ref[...] = (mm(dkh_ref[...], wk_ref[...], NT) + mm(dvh_ref[...], wv_ref[...], NT)).astype(BF)


def weights_body(
    scale, rows, head_size, meta_ref, normed_turned_ref, halo_t_ref, frames_ref, cot_hbm,
    wq_hbm, wk_hbm, wv_hbm, wo_hbm,
    q_ref, kt_ref, khalo_t_ref, ot, do_ref, raised_ref, grads_ref, scale_ref, dkh_ref, dvh_ref,
    keep_ref, send_ref, out_ref, slope_ref,
    normed_t, halo_t, mixed_t, ktx, dqt, dk, dv,
    wq, wk, wv, wo, cot_ref, sems,
):
    span, width = q_ref.shape
    copies = fetch(
        [wq_hbm, wk_hbm, wv_hbm, wo_hbm, cot_hbm], [wq, wk, wv, wo, cot_ref], sems
    )
    ktx[:, :WIN] = khalo_t_ref[...]
    ktx[:, WIN:] = kt_ref[...]
    pair = 2 * head_size
    tiles = span // TILE
    upper = iota2((pair, TILE), 0) < head_size

    def one_pair(p, carry):
        cols = pl.ds(pl.multiple_of(p * pair, pair), pair)
        own_grads = []
        for a in range(tiles):
            here = slice(a * TILE, (a + 1) * TILE)
            keys = slice(a * TILE, a * TILE + REACH)
            at = p * tiles + a
            shrink = scale_ref[at]
            moved = mm(ktx[cols, keys], grads_ref[at]) * (shrink * head_size ** (-0.5))
            dqt[cols, here] = jnp.where(upper, moved[:, :TILE], moved[:, TILE:]).astype(BF)
            near = slice(WIN - a * TILE, REACH)
            own_grads.append((
                mm(grads_ref[at, near], both_heads(q_ref[here, cols], 1, 0)),
                mm(raised_ref[at, near], both_heads(do_ref[here, cols], 1, 0)),
            ))
        for which, factor, out in ((0, math.log(2.0), dk), (1, 1.0, dv)):
            for j in range(tiles):
                total = None
                for a in range(j, tiles):
                    piece = own_grads[a][which][j * TILE : (j + 1) * TILE]
                    total = piece if total is None else total + piece
                out[j * TILE : (j + 1) * TILE, cols] = (total * factor).astype(BF)
        return carry

    lax.fori_loop(0, width // pair, one_pair, 0)

    for copy in copies:
        copy.wait()
    chunks = width // (2 * rows)
    split = (chunks, 2, rows, span)
    normed_t[...] = normed_turned_ref[...].reshape(split)
    halo_t[...] = halo_t_ref[...].reshape(split)
    mixed_t[...] = ot[...].reshape(split)
    mine = meta_ref[2]
    for side, out in ((1 - mine, send_ref), (mine, keep_ref)):
        own = normed_t[:, side].reshape(width // 2, span)
        far = halo_t[:, side].reshape(width // 2, span)
        mixed = mixed_t[:, side].reshape(width // 2, span)
        for n, total in enumerate((
            mm(own, dqt[...], NT),
            mm(own, dk[...]) + mm(far, dkh_ref[...]),
            mm(own, dv[...]) + mm(far, dvh_ref[...]),
            mm(mixed, cot_ref[...]),
        )):
            out[:, n * width : (n + 1) * width] = (total * scale).astype(BF)
    slope = mm(dqt[...].T, wq[...], NT)
    slope = slope + mm(dk[...], wk[...], NT)
    slope_ref[...] = slope + mm(dv[...], wv[...], NT)
    out = mm(ot[...].T, wo[...]) + frames_ref[...].astype(F32)
    out_ref[...] = out.astype(BF)


def returning_body(
    frames_ref, slope_ref, extra_ref, cot_ref, pick_t_ref, out_ref
):
    _, inverse, normed32 = unit_frames(frames_ref[...])
    slope = slope_ref[...] + extra_ref[...].astype(F32)
    centre = jnp.mean(slope * normed32, axis=1, keepdims=True)
    grad = inverse * (slope - normed32 * centre) + cot_ref[...].astype(F32)
    out_ref[...] = mm(pick_t_ref[...], grad.astype(BF)).astype(BF)


def arrived_body(placing_t_ref, in_ref, out_ref):
    out_ref[...] = mm(placing_t_ref[...], in_ref[...]).astype(BF)


def passed_along(shard, by):
    devices = lax.axis_size("seq")
    pairs = [(i, i + by) for i in range(devices) if 0 <= i + by < devices]
    return lax.ppermute(shard, "seq", pairs)


def spread_body(place_ref, *refs):
    parts = refs[0].shape[0]
    inputs, outs = refs[:-parts], refs[-parts:]
    for k, out in enumerate(outs):
        at = place_ref[0] ^ k
        total = inputs[0][at].astype(F32)
        for ref in inputs[1:]:
            total = total + ref[at].astype(F32)
        out[...] = total.astype(BF)


def spread(inputs, place, parts, carry=()):
    columns = inputs[0].shape[-1]
    inputs = [shard.reshape(parts, -1, columns) for shard in inputs]
    piece = sds(inputs[0].shape[1:])
    return vmem_call(spread_body, [piece] * parts, [place.reshape(1)] + inputs, smem=(0,), carry=carry)


def swapped(pieces, axis, step):
    count = lax.axis_size(axis)
    return [pieces[0]] + [
        lax.ppermute(piece, axis, [(i, i ^ (k * step)) for i in range(count)])
        for k, piece in enumerate(pieces[1:], 1)
    ]


def shards(
    frame_rows, row_frame, frame_owner, lengths,
    query_weight, key_weight, value_weight, out_weight, cotangent,
):
    devices = lax.axis_size(AXES)
    row_count, width = frame_rows.shape
    span = frame_owner.shape[1]
    slots = row_count // devices
    slab = span * lax.axis_size("seq")
    head_size = width // H
    cube = 2 * span * width * width
    square = sds((span, width))
    begin = (lax.axis_index("seq") * span).astype(jnp.int32)
    rows = width // devices
    in_kernel = rows % 16 == 0
    core = (lax.axis_index("seq") & 1).astype(jnp.int32)
    meta = jnp.stack([begin, lengths[0], core if in_kernel else jnp.zeros((), jnp.int32)])
    cot = cotangent[0]

    def exchanged(shard):
        got = lax.all_to_all(
            shard.reshape(devices, slots, width), AXES, split_axis=0, concat_axis=0, tiled=True
        )
        return got.reshape(devices * slots, width)

    outgoing, = vmem_call(
        lambda *refs: outgoing_body(span, slots, *refs),
        [square],
        [row_frame.reshape(1, row_count), frame_rows],
        hbm=(1,),
        scratch=[pltpu.VMEM((row_count, width), BF), pltpu.SemaphoreType.DMA((1,))],
        flops=cube,
    )
    incoming = exchanged(outgoing)
    pick, pick_t = vmem_call(
        lambda *refs: early_body(slots, *refs),
        [square, square],
        [frame_owner.reshape(span, 1)],
        flops=cube,
    )
    frames, normed = vmem_call(frames_body, [square, square], [pick, incoming], flops=cube)
    halo = passed_along(normed, 1)
    query_scale = head_size ** (-0.5) * math.log2(math.e)
    qt, k, kt, v, vt, wk, wv, normed_turned = vmem_call(
        lambda *refs: project_body(query_scale, *refs),
        [square] * 8,
        [normed, query_weight, key_weight, value_weight],
        hbm=(1, 2, 3),
        scratch=[pltpu.VMEM((width, width), BF), pltpu.SemaphoreType.DMA((3,))],
        flops=3 * cube,
    )
    units = H // 2 * (span // TILE)
    saved = sds((units, REACH, 2 * TILE))
    raised, grads, scales, q, do, dkh, dvh, khalo_t, halo_t, ot, back = vmem_call(
        lambda *refs: scores_body(head_size, *refs),
        [saved, saved, sds((units, 1, 2 * TILE), F32)] + [square] * 8,
        [meta, halo, wk, wv, qt, k, v, vt, cot, out_weight],
        smem=(0,),
        hbm=(8, 9),
        scratch=[pltpu.VMEM((WIN + span, width), BF)] * 2 + [pltpu.VMEM((width, WIN + span), BF)]
        + [pltpu.VMEM((width, span), BF)] * 3 + [pltpu.SemaphoreType.DMA((2,))],
        flops=12 * cube,
        limit=24,
    )
    extra = passed_along(back, -1)
    chunk = rows if in_kernel else width // 2
    split = pltpu.VMEM((width // (2 * chunk), 2, chunk, span), BF)
    half = sds((width // 2, 4 * width))
    whole = pltpu.VMEM((width, width), BF)
    keep, send, out_frames, slope = vmem_call(
        lambda *refs: weights_body(slab ** (-0.5), chunk, head_size, *refs),
        [half, half, square, sds((span, width), F32)],
        [meta, normed_turned, halo_t, frames, cot, query_weight, key_weight, value_weight, out_weight,
         q, kt, khalo_t, ot, do, raised, grads, scales, dkh, dvh],
        smem=(0,),
        hbm=(4, 5, 6, 7, 8),
        scratch=[split] * 3 + [pltpu.VMEM((width, WIN + span), BF)] + [whole] * 8
        + [pltpu.SemaphoreType.DMA((5,))],
        flops=18 * cube,
        limit=26,
    )
    send, extra = lax.optimization_barrier((send, extra))
    if not in_kernel:
        sums = jnp.concatenate([keep, send], axis=0).reshape(-1, 2, rows, 4 * width)
        keep = lax.dynamic_index_in_dim(sums, core, 1, keepdims=False).reshape(half.shape)
        send = lax.dynamic_index_in_dim(sums, 1 - core, 1, keepdims=False).reshape(half.shape)
    seqs = lax.axis_size("seq")
    got = lax.ppermute(send, "seq", [(i, i ^ 1) for i in range(seqs)])
    seqs = lax.axis_size("seq")
    got = lax.ppermute(send, "seq", [(i, i ^ 1) for i in range(seqs)])
    returning, = vmem_call(
        returning_body,
        [square],
        [frames, slope, extra, cot, pick_t],
        flops=cube,
    )
    pieces = spread([keep, got], lax.axis_index("stream"), lax.axis_size("stream"), [returning])
    pieces = swapped(pieces, "stream", 1)
    late_rows, returning = lax.optimization_barrier((row_frame.reshape(1, row_count), returning))
    arrived = exchanged(returning)
    placing_t, = vmem_call(
        lambda *refs: placing_t_body(span, slots, *refs),
        [sds((row_count, devices * slots))],
        [late_rows],
        flops=40 * cube,
    )
    frame_grads, = vmem_call(arrived_body, [square], [placing_t, arrived], flops=cube)
    pieces = swapped(spread(pieces, lax.axis_index("seq") >> 1, seqs // 2), "seq", 2)
    weight_grads = pieces[0].astype(F32)
    for piece in pieces[1:]:
        weight_grads = weight_grads + piece.astype(F32)
    return (out_frames[None], frame_grads, weight_grads)


def solution(mesh):
    return jax.shard_map(
        shards,
        mesh=mesh,
        in_specs=(
            P(AXES, None), P(AXES), P("stream", "seq"), P("stream"),
            P(), P(), P(), P(), P("stream", "seq", None),
        ),
        out_specs=(P("stream", "seq", None), P(AXES, None), P(AXES, None)),
        check_vma=False,
    )
```

```python
import math

import jax
import jax.numpy as jnp
from jax import lax
from jax.experimental import pallas as pl
from jax.experimental.pallas import tpu as pltpu
from jax.sharding import PartitionSpec as P

H = 8
WIN = 512
NEG = -1e30
EPS_NORM = 1e-06
AXES = ("stream", "seq")
BF = jnp.bfloat16
F32 = jnp.float32

NN = (((1,), (0,)), ((), ()))
NT = (((1,), (1,)), ((), ()))


def mm(a, b, dims=NN):
    return lax.dot_general(a, b, dims, preferred_element_type=F32)


def iota2(shape, dim):
    return lax.broadcasted_iota(jnp.int32, shape, dim)


def vmem_call(body, outs, args, smem=(), hbm=(), scratch=(), carry=(), flops=0, limit=12):
    used, inner, args = len(args), body, list(args) + list(carry)

    def body(*refs):
        inner(*refs[:used], *refs[len(args) :])

    spaces = [pltpu.SMEM if i in smem else pltpu.HBM if i in hbm else pltpu.VMEM for i in range(len(args))]
    size = sum(math.prod(a.shape) * a.dtype.itemsize for a in list(args) + list(outs))
    return pl.pallas_call(
        body,
        out_shape=tuple(outs),
        in_specs=[pl.BlockSpec(memory_space=space) for space in spaces],
        out_specs=tuple(pl.BlockSpec(memory_space=pltpu.VMEM) for _ in outs),
        scratch_shapes=list(scratch),
        compiler_params=pltpu.CompilerParams(vmem_limit_bytes=limit * 2**20),
        cost_estimate=pl.CostEstimate(flops=flops, bytes_accessed=size, transcendentals=0),
    )(*args)


def fetch(sources, targets, sems):
    copies = [
        pltpu.make_async_copy(source, target, sems.at[n])
        for n, (source, target) in enumerate(zip(sources, targets))
    ]
    for copy in copies:
        copy.start()
    return copies


def sds(shape, dtype=BF):
    return jax.ShapeDtypeStruct(shape, dtype)


def placing_of(span, slots, rf, total):
    count = rf.shape[1]
    target = jnp.where(rf >= 0, lax.div(rf, span), 1 << 20)
    slot = iota2((total, count), 0)
    owner = lax.div(slot, slots)
    rank = slot - owner * slots
    start = jnp.sum(jnp.where(target < owner, 1.0, 0.0), axis=1, keepdims=True)
    here = iota2((total, count), 1) - start.astype(jnp.int32)
    return jnp.where((target == owner) & (here == rank), 1.0, 0.0)


def outgoing_body(span, slots, rf_ref, rows_hbm, out_ref, rows_ref, sems):
    (rows_copy,) = fetch([rows_hbm], [rows_ref], sems)
    placing = placing_of(span, slots, rf_ref[...], out_ref.shape[0]).astype(BF)
    rows_copy.wait()
    out_ref[...] = mm(placing, rows_ref[...]).astype(BF)


def placing_t_body(span, slots, rf_ref, out_ref):
    out_ref[...] = placing_of(span, slots, rf_ref[...], out_ref.shape[1]).T.astype(BF)


def early_body(slots, owner_ref, pick_ref, pick_t_ref):
    span, lanes = owner_ref.shape[0], 128
    total = pick_ref.shape[1]
    owner = owner_ref[...]
    device = iota2((span, lanes), 1)
    hot = jnp.where(owner == device, 1.0, 0.0)
    strict = jnp.where(iota2((span, span), 1) < iota2((span, span), 0), 1.0, 0.0).astype(BF)
    before = mm(strict, hot.astype(BF))
    slot = jnp.sum(hot * (before + (device * slots).astype(F32)), axis=1, keepdims=True)
    slot = jnp.where(owner >= 0, slot.astype(jnp.int32), -1)
    pick = jnp.where(iota2((span, total), 1) == slot, 1.0, 0.0)
    pick_ref[...] = pick.astype(BF)
    pick_t_ref[...] = pick.T.astype(BF)


def unit_frames(frames):
    frames32 = frames.astype(F32)
    inverse = lax.rsqrt(jnp.mean(frames32 * frames32, axis=1, keepdims=True) + EPS_NORM)
    return frames32, inverse, frames32 * inverse


def frames_body(pick_ref, in_ref, frames_ref, normed_ref):
    frames = mm(pick_ref[...], in_ref[...]).astype(BF)
    frames_ref[...] = frames
    normed_ref[...] = unit_frames(frames)[2].astype(BF)


def project_body(
    query_scale, normed_ref, wq_hbm, wk_hbm, wv_hbm,
    qt_ref, k_ref, kt_ref, v_ref, vt_ref, wk_ref, wv_ref, normed_t_ref, wq_ref, sems,
):
    copies = fetch([wq_hbm, wk_hbm, wv_hbm], [wq_ref, wk_ref, wv_ref], sems)
    normed = normed_ref[...]
    normed_t_ref[...] = normed.T
    copies[0].wait()
    qt_ref[...] = (mm(normed, wq_ref[...]) * query_scale).astype(BF).T
    copies[1].wait()
    k = mm(normed, wk_ref[...]).astype(BF)
    k_ref[...] = k
    kt_ref[...] = k.T
    copies[2].wait()
    v = mm(normed, wv_ref[...]).astype(BF)
    v_ref[...] = v
    vt_ref[...] = v.T


TILE = 128
REACH = WIN + TILE


def raised_scores(scores, first, begin):
    row = iota2((TILE, TILE), 0)
    col = iota2((TILE, TILE), 1)
    halo_bias = jnp.where(begin == 0, NEG, 0.0)
    count = REACH // TILE
    raised_cols = []
    for h in range(2):
        at = slice(h * TILE, (h + 1) * TILE)
        parts = []
        for n in range(count):
            part = scores[n * TILE : (n + 1) * TILE, at]
            if n == 0:
                part = jnp.where(row > col, part, NEG)
            if n == count - 1:
                part = jnp.where(row <= col, part, NEG)
            elif first + n * TILE < WIN:
                part = part + halo_bias
            parts.append(part)
        peak = parts[0]
        for part in parts[1:]:
            peak = jnp.maximum(peak, part)
        peak = jnp.max(peak, axis=0, keepdims=True)
        raised_cols.append(jnp.concatenate([jnp.exp2((part - peak).astype(BF)) for part in parts], axis=0))
    return jnp.concatenate(raised_cols, axis=1)


def both_heads(value, axis, along):
    place = iota2(value.shape, axis)
    half = value.shape[axis] // 2
    zero = jnp.zeros((), value.dtype)
    return jnp.concatenate([jnp.where(place < half, value, zero), jnp.where(place < half, zero, value)], axis=along)


def scores_body(
    head_size, meta_ref, halo_ref, wk_ref, wv_ref, qt_ref, k_ref, v_ref, vt_ref, cot_hbm, wo_hbm,
    raised_ref, grads_ref, scale_ref, q_ref, do_ref, dkh_ref, dvh_ref, khalo_t_ref, halo_t_ref, ot_ref, back_ref,
    kx, vx, vtx, dot_ref, cot_ref, wo_ref, sems,
):
    copies = fetch([cot_hbm, wo_hbm], [cot_ref, wo_ref], sems)
    span, width = k_ref.shape
    begin, length = meta_ref[0], meta_ref[1]
    halo = halo_ref[...]
    kh = mm(halo, wk_ref[...]).astype(BF)
    kx[:WIN] = kh
    khalo_t_ref[...] = kh.T
    vh = mm(halo, wv_ref[...]).astype(BF)
    vx[:WIN] = vh
    vtx[:, :WIN] = vh.T
    vtx[:, WIN:] = vt_ref[...]
    halo_t_ref[...] = halo.T
    kx[WIN:] = k_ref[...]
    vx[WIN:] = v_ref[...]

    pair = 2 * head_size
    tiles = span // TILE
    upper = iota2((pair, TILE), 0) < head_size
    ones = jnp.ones((16, REACH), BF)

    def one_pair(p, carry):
        cols = pl.ds(pl.multiple_of(p * pair, pair), pair)

        def multiply(a):
            here = slice(a * TILE, (a + 1) * TILE)
            keys = slice(a * TILE, a * TILE + REACH)
            scores = mm(kx[keys, cols], both_heads(qt_ref[cols, here], 0, 1))
            slopes = mm(vx[keys, cols], both_heads(dot_ref[cols, here], 0, 1))
            return scores, slopes

        halo_grads = []

        def raise_and_mix(a, scores):
            here = slice(a * TILE, (a + 1) * TILE)
            keys = slice(a * TILE, a * TILE + REACH)
            raised = raised_scores(scores, a * TILE, begin)
            raised_ref[p * tiles + a] = raised
            mixed = mm(jnp.concatenate([vtx[cols, keys], ones], axis=0), raised)
            time = begin + a * TILE + iota2((1, 2 * TILE), 1) % TILE
            scale = jnp.where(time < length, 1.0 / mixed[pair : pair + 1], 0.0)
            scale_ref[p * tiles + a] = scale
            spread_scale = jnp.where(upper, scale[:, :TILE], scale[:, TILE:])
            mixed = jnp.where(upper, mixed[:pair, :TILE], mixed[:pair, TILE:]) * spread_scale
            ot_ref[cols, here] = mixed.astype(BF)
            return raised, mixed, spread_scale

        def finish(a, slopes, raised, mixed, spread_scale):
            here = slice(a * TILE, (a + 1) * TILE)
            out_grad = dot_ref[cols, here].astype(F32)
            product = mixed * out_grad
            grad_cols = []
            for h in range(2):
                at = slice(h * TILE, (h + 1) * TILE)
                centre = jnp.sum(product[h * head_size : (h + 1) * head_size], axis=0, keepdims=True)
                grad_cols.append(raised[:, at] * (slopes[:, at] - centre).astype(BF))
            grads = jnp.concatenate(grad_cols, axis=1)
            grads_ref[p * tiles + a] = grads
            far = WIN - a * TILE
            queries = (qt_ref[cols, here].astype(F32) * spread_scale).T.astype(BF)
            out_grad = (out_grad * spread_scale).T.astype(BF)
            q_ref[here, cols] = queries
            do_ref[here, cols] = out_grad
            halo_grads.append((
                mm(grads[:far], both_heads(queries, 1, 0)),
                mm(raised[:far], both_heads(out_grad, 1, 0)),
            ))

        scores, slopes = multiply(0)
        waiting = None
        for a in range(tiles):
            ahead = multiply(a + 1) if a + 1 < tiles else None
            mixed = raise_and_mix(a, scores)
            if waiting is not None:
                finish(*waiting)
            waiting = (a, slopes, *mixed)
            if ahead is not None:
                scores, slopes = ahead
        finish(*waiting)
        for which, scale, out in ((0, math.log(2.0), dkh_ref), (1, 1.0, dvh_ref)):
            for j in range(WIN // TILE):
                total = None
                for a in range(min(j + 1, tiles)):
                    piece = halo_grads[a][which][(j - a) * TILE : (j - a + 1) * TILE]
                    total = piece if total is None else total + piece
                out[j * TILE : (j + 1) * TILE, cols] = (total * scale).astype(BF)
        return carry

    for copy in copies:
        copy.wait()
    dot_ref[...] = mm(cot_ref[...], wo_ref[...], NT).astype(BF).T
    lax.fori_loop(0, width // pair, one_pair, 0, unroll=2)
    back_ref[...] = (mm(dkh_ref[...], wk_ref[...], NT) + mm(dvh_ref[...], wv_ref[...], NT)).astype(BF)


def weights_body(
    scale, rows, head_size, meta_ref, normed_turned_ref, halo_t_ref, frames_ref, cot_hbm,
    wq_hbm, wk_hbm, wv_hbm, wo_hbm,
    q_ref, kt_ref, khalo_t_ref, ot, do_ref, raised_ref, grads_ref, scale_ref, dkh_ref, dvh_ref,
    keep_ref, send_ref, out_ref, slope_ref,
    normed_t, halo_t, mixed_t, ktx, dqt, dk, dv,
    wq, wk, wv, wo, cot_ref, sems,
):
    span, width = q_ref.shape
    copies = fetch(
        [wq_hbm, wk_hbm, wv_hbm, wo_hbm, cot_hbm], [wq, wk, wv, wo, cot_ref], sems
    )
    ktx[:, :WIN] = khalo_t_ref[...]
    ktx[:, WIN:] = kt_ref[...]
    pair = 2 * head_size
    tiles = span // TILE
    upper = iota2((pair, TILE), 0) < head_size

    def one_pair(p, carry):
        cols = pl.ds(pl.multiple_of(p * pair, pair), pair)
        own_grads = []
        for a in range(tiles):
            here = slice(a * TILE, (a + 1) * TILE)
            keys = slice(a * TILE, a * TILE + REACH)
            at = p * tiles + a
            shrink = scale_ref[at]
            moved = mm(ktx[cols, keys], grads_ref[at]) * (shrink * head_size ** (-0.5))
            dqt[cols, here] = jnp.where(upper, moved[:, :TILE], moved[:, TILE:]).astype(BF)
            near = slice(WIN - a * TILE, REACH)
            own_grads.append((
                mm(grads_ref[at, near], both_heads(q_ref[here, cols], 1, 0)),
                mm(raised_ref[at, near], both_heads(do_ref[here, cols], 1, 0)),
            ))
        for which, factor, out in ((0, math.log(2.0), dk), (1, 1.0, dv)):
            for j in range(tiles):
                total = None
                for a in range(j, tiles):
                    piece = own_grads[a][which][j * TILE : (j + 1) * TILE]
                    total = piece if total is None else total + piece
                out[j * TILE : (j + 1) * TILE, cols] = (total * factor).astype(BF)
        return carry

    lax.fori_loop(0, width // pair, one_pair, 0, unroll=2)

    for copy in copies:
        copy.wait()
    chunks = width // (2 * rows)
    split = (chunks, 2, rows, span)
    normed_t[...] = normed_turned_ref[...].reshape(split)
    halo_t[...] = halo_t_ref[...].reshape(split)
    mixed_t[...] = ot[...].reshape(split)
    mine = meta_ref[2]
    for side, out in ((1 - mine, send_ref), (mine, keep_ref)):
        own = normed_t[:, side].reshape(width // 2, span)
        far = halo_t[:, side].reshape(width // 2, span)
        mixed = mixed_t[:, side].reshape(width // 2, span)
        for n, total in enumerate((
            mm(own, dqt[...], NT),
            mm(own, dk[...]) + mm(far, dkh_ref[...]),
            mm(own, dv[...]) + mm(far, dvh_ref[...]),
            mm(mixed, cot_ref[...]),
        )):
            out[:, n * width : (n + 1) * width] = (total * scale).astype(BF)
    slope = mm(dqt[...].T, wq[...], NT)
    slope = slope + mm(dk[...], wk[...], NT)
    slope_ref[...] = slope + mm(dv[...], wv[...], NT)
    out = mm(ot[...].T, wo[...]) + frames_ref[...].astype(F32)
    out_ref[...] = out.astype(BF)


def returning_body(
    frames_ref, slope_ref, extra_ref, cot_ref, pick_t_ref, out_ref
):
    _, inverse, normed32 = unit_frames(frames_ref[...])
    slope = slope_ref[...] + extra_ref[...].astype(F32)
    centre = jnp.mean(slope * normed32, axis=1, keepdims=True)
    grad = inverse * (slope - normed32 * centre) + cot_ref[...].astype(F32)
    out_ref[...] = mm(pick_t_ref[...], grad.astype(BF)).astype(BF)


def arrived_body(placing_t_ref, in_ref, out_ref):
    out_ref[...] = mm(placing_t_ref[...], in_ref[...]).astype(BF)


def passed_along(shard, by):
    devices = lax.axis_size("seq")
    pairs = [(i, i + by) for i in range(devices) if 0 <= i + by < devices]
    return lax.ppermute(shard, "seq", pairs)


def spread_body(place_ref, *refs):
    parts = refs[0].shape[0]
    inputs, outs = refs[:-parts], refs[-parts:]
    for k, out in enumerate(outs):
        at = place_ref[0] ^ k
        total = inputs[0][at].astype(F32)
        for ref in inputs[1:]:
            total = total + ref[at].astype(F32)
        out[...] = total.astype(BF)


def spread(inputs, place, parts, carry=()):
    columns = inputs[0].shape[-1]
    inputs = [shard.reshape(parts, -1, columns) for shard in inputs]
    piece = sds(inputs[0].shape[1:])
    return vmem_call(spread_body, [piece] * parts, [place.reshape(1)] + inputs, smem=(0,), carry=carry)


def swapped(pieces, axis, step):
    count = lax.axis_size(axis)
    return [pieces[0]] + [
        lax.ppermute(piece, axis, [(i, i ^ (k * step)) for i in range(count)])
        for k, piece in enumerate(pieces[1:], 1)
    ]


def shards(
    frame_rows, row_frame, frame_owner, lengths,
    query_weight, key_weight, value_weight, out_weight, cotangent,
):
    devices = lax.axis_size(AXES)
    row_count, width = frame_rows.shape
    span = frame_owner.shape[1]
    slots = row_count // devices
    slab = span * lax.axis_size("seq")
    head_size = width // H
    cube = 2 * span * width * width
    square = sds((span, width))
    begin = (lax.axis_index("seq") * span).astype(jnp.int32)
    rows = width // devices
    in_kernel = rows % 16 == 0
    core = (lax.axis_index("seq") & 1).astype(jnp.int32)
    meta = jnp.stack([begin, lengths[0], core if in_kernel else jnp.zeros((), jnp.int32)])
    cot = cotangent[0]

    def exchanged(shard):
        got = lax.all_to_all(
            shard.reshape(devices, slots, width), AXES, split_axis=0, concat_axis=0, tiled=True
        )
        return got.reshape(devices * slots, width)

    outgoing, = vmem_call(
        lambda *refs: outgoing_body(span, slots, *refs),
        [square],
        [row_frame.reshape(1, row_count), frame_rows],
        hbm=(1,),
        scratch=[pltpu.VMEM((row_count, width), BF), pltpu.SemaphoreType.DMA((1,))],
        flops=cube,
    )
    incoming = exchanged(outgoing)
    pick, pick_t = vmem_call(
        lambda *refs: early_body(slots, *refs),
        [square, square],
        [frame_owner.reshape(span, 1)],
        flops=cube,
    )
    frames, normed = vmem_call(frames_body, [square, square], [pick, incoming], flops=cube)
    halo = passed_along(normed, 1)
    query_scale = head_size ** (-0.5) * math.log2(math.e)
    qt, k, kt, v, vt, wk, wv, normed_turned = vmem_call(
        lambda *refs: project_body(query_scale, *refs),
        [square] * 8,
        [normed, query_weight, key_weight, value_weight],
        hbm=(1, 2, 3),
        scratch=[pltpu.VMEM((width, width), BF), pltpu.SemaphoreType.DMA((3,))],
        flops=3 * cube,
    )
    units = H // 2 * (span // TILE)
    saved = sds((units, REACH, 2 * TILE))
    raised, grads, scales, q, do, dkh, dvh, khalo_t, halo_t, ot, back = vmem_call(
        lambda *refs: scores_body(head_size, *refs),
        [saved, saved, sds((units, 1, 2 * TILE), F32)] + [square] * 8,
        [meta, halo, wk, wv, qt, k, v, vt, cot, out_weight],
        smem=(0,),
        hbm=(8, 9),
        scratch=[pltpu.VMEM((WIN + span, width), BF)] * 2 + [pltpu.VMEM((width, WIN + span), BF)]
        + [pltpu.VMEM((width, span), BF)] * 3 + [pltpu.SemaphoreType.DMA((2,))],
        flops=12 * cube,
        limit=24,
    )
    extra = passed_along(back, -1)
    chunk = rows if in_kernel else width // 2
    split = pltpu.VMEM((width // (2 * chunk), 2, chunk, span), BF)
    half = sds((width // 2, 4 * width))
    whole = pltpu.VMEM((width, width), BF)
    keep, send, out_frames, slope = vmem_call(
        lambda *refs: weights_body(slab ** (-0.5), chunk, head_size, *refs),
        [half, half, square, sds((span, width), F32)],
        [meta, normed_turned, halo_t, frames, cot, query_weight, key_weight, value_weight, out_weight,
         q, kt, khalo_t, ot, do, raised, grads, scales, dkh, dvh],
        smem=(0,),
        hbm=(4, 5, 6, 7, 8),
        scratch=[split] * 3 + [pltpu.VMEM((width, WIN + span), BF)] + [whole] * 8
        + [pltpu.SemaphoreType.DMA((5,))],
        flops=18 * cube,
        limit=26,
    )
    send, extra = lax.optimization_barrier((send, extra))
    if not in_kernel:
        sums = jnp.concatenate([keep, send], axis=0).reshape(-1, 2, rows, 4 * width)
        keep = lax.dynamic_index_in_dim(sums, core, 1, keepdims=False).reshape(half.shape)
        send = lax.dynamic_index_in_dim(sums, 1 - core, 1, keepdims=False).reshape(half.shape)
    seqs = lax.axis_size("seq")
    got = lax.ppermute(send, "seq", [(i, i ^ 1) for i in range(seqs)])
    seqs = lax.axis_size("seq")
    got = lax.ppermute(send, "seq", [(i, i ^ 1) for i in range(seqs)])
    returning, = vmem_call(
        returning_body,
        [square],
        [frames, slope, extra, cot, pick_t],
        flops=cube,
    )
    pieces = spread([keep, got], lax.axis_index("stream"), lax.axis_size("stream"), [returning])
    pieces = swapped(pieces, "stream", 1)
    late_rows, returning = lax.optimization_barrier((row_frame.reshape(1, row_count), returning))
    arrived = exchanged(returning)
    placing_t, = vmem_call(
        lambda *refs: placing_t_body(span, slots, *refs),
        [sds((row_count, devices * slots))],
        [late_rows],
        flops=40 * cube,
    )
    frame_grads, = vmem_call(arrived_body, [square], [placing_t, arrived], flops=cube)
    pieces = swapped(spread(pieces, lax.axis_index("seq") >> 1, seqs // 2), "seq", 2)
    weight_grads = pieces[0].astype(F32)
    for piece in pieces[1:]:
        weight_grads = weight_grads + piece.astype(F32)
    return (out_frames[None], frame_grads, weight_grads)


def solution(mesh):
    return jax.shard_map(
        shards,
        mesh=mesh,
        in_specs=(
            P(AXES, None), P(AXES), P("stream", "seq"), P("stream"),
            P(), P(), P(), P(), P("stream", "seq", None),
        ),
        out_specs=(P("stream", "seq", None), P(AXES, None), P(AXES, None)),
        check_vma=False,
    )
```

```python
import math

import jax
import jax.numpy as jnp
from jax import lax
from jax.experimental import pallas as pl
from jax.experimental.pallas import tpu as pltpu
from jax.sharding import PartitionSpec as P

H = 8
WIN = 512
NEG = -1e30
EPS_NORM = 1e-06
AXES = ("stream", "seq")
BF = jnp.bfloat16
F32 = jnp.float32

NN = (((1,), (0,)), ((), ()))
NT = (((1,), (1,)), ((), ()))


def mm(a, b, dims=NN):
    return lax.dot_general(a, b, dims, preferred_element_type=F32)


def iota2(shape, dim):
    return lax.broadcasted_iota(jnp.int32, shape, dim)


def vmem_call(body, outs, args, smem=(), hbm=(), scratch=(), carry=(), flops=0, limit=12):
    used, inner, args = len(args), body, list(args) + list(carry)

    def body(*refs):
        inner(*refs[:used], *refs[len(args) :])

    spaces = [pltpu.SMEM if i in smem else pltpu.HBM if i in hbm else pltpu.VMEM for i in range(len(args))]
    size = sum(math.prod(a.shape) * a.dtype.itemsize for a in list(args) + list(outs))
    return pl.pallas_call(
        body,
        out_shape=tuple(outs),
        in_specs=[pl.BlockSpec(memory_space=space) for space in spaces],
        out_specs=tuple(pl.BlockSpec(memory_space=pltpu.VMEM) for _ in outs),
        scratch_shapes=list(scratch),
        compiler_params=pltpu.CompilerParams(vmem_limit_bytes=limit * 2**20),
        cost_estimate=pl.CostEstimate(flops=flops, bytes_accessed=size, transcendentals=0),
    )(*args)


def fetch(sources, targets, sems):
    copies = [
        pltpu.make_async_copy(source, target, sems.at[n])
        for n, (source, target) in enumerate(zip(sources, targets))
    ]
    for copy in copies:
        copy.start()
    return copies


def sds(shape, dtype=BF):
    return jax.ShapeDtypeStruct(shape, dtype)


def placing_of(span, slots, rf, total):
    count = rf.shape[1]
    target = jnp.where(rf >= 0, lax.div(rf, span), 1 << 20)
    slot = iota2((total, count), 0)
    owner = lax.div(slot, slots)
    rank = slot - owner * slots
    start = jnp.sum(jnp.where(target < owner, 1.0, 0.0), axis=1, keepdims=True)
    here = iota2((total, count), 1) - start.astype(jnp.int32)
    return jnp.where((target == owner) & (here == rank), 1.0, 0.0)


def outgoing_body(span, slots, rf_ref, rows_hbm, out_ref, rows_ref, sems):
    (rows_copy,) = fetch([rows_hbm], [rows_ref], sems)
    placing = placing_of(span, slots, rf_ref[...], out_ref.shape[0]).astype(BF)
    rows_copy.wait()
    out_ref[...] = mm(placing, rows_ref[...]).astype(BF)


def placing_t_body(span, slots, rf_ref, out_ref):
    out_ref[...] = placing_of(span, slots, rf_ref[...], out_ref.shape[1]).T.astype(BF)


def early_body(slots, owner_ref, pick_ref, pick_t_ref):
    span, lanes = owner_ref.shape[0], 128
    total = pick_ref.shape[1]
    owner = owner_ref[...]
    device = iota2((span, lanes), 1)
    hot = jnp.where(owner == device, 1.0, 0.0)
    strict = jnp.where(iota2((span, span), 1) < iota2((span, span), 0), 1.0, 0.0).astype(BF)
    before = mm(strict, hot.astype(BF))
    slot = jnp.sum(hot * (before + (device * slots).astype(F32)), axis=1, keepdims=True)
    slot = jnp.where(owner >= 0, slot.astype(jnp.int32), -1)
    pick = jnp.where(iota2((span, total), 1) == slot, 1.0, 0.0)
    pick_ref[...] = pick.astype(BF)
    pick_t_ref[...] = pick.T.astype(BF)


def unit_frames(frames):
    frames32 = frames.astype(F32)
    inverse = lax.rsqrt(jnp.mean(frames32 * frames32, axis=1, keepdims=True) + EPS_NORM)
    return frames32, inverse, frames32 * inverse


def frames_body(pick_ref, in_ref, frames_ref, normed_ref):
    frames = mm(pick_ref[...], in_ref[...]).astype(BF)
    frames_ref[...] = frames
    normed_ref[...] = unit_frames(frames)[2].astype(BF)


def project_body(
    query_scale, normed_ref, wq_hbm, wk_hbm, wv_hbm,
    qt_ref, k_ref, kt_ref, v_ref, vt_ref, wk_ref, wv_ref, normed_t_ref, wq_ref, sems,
):
    copies = fetch([wq_hbm, wk_hbm, wv_hbm], [wq_ref, wk_ref, wv_ref], sems)
    normed = normed_ref[...]
    normed_t_ref[...] = normed.T
    copies[0].wait()
    qt_ref[...] = (mm(normed, wq_ref[...]) * query_scale).astype(BF).T
    copies[1].wait()
    k = mm(normed, wk_ref[...]).astype(BF)
    k_ref[...] = k
    kt_ref[...] = k.T
    copies[2].wait()
    v = mm(normed, wv_ref[...]).astype(BF)
    v_ref[...] = v
    vt_ref[...] = v.T


TILE = 128
REACH = WIN + TILE


def raised_scores(scores, first, begin):
    row = iota2((TILE, TILE), 0)
    col = iota2((TILE, TILE), 1)
    halo_bias = jnp.where(begin == 0, NEG, 0.0)
    count = REACH // TILE
    raised_cols = []
    for h in range(2):
        at = slice(h * TILE, (h + 1) * TILE)
        parts = []
        for n in range(count):
            part = scores[n * TILE : (n + 1) * TILE, at]
            if n == 0:
                part = jnp.where(row > col, part, NEG)
            if n == count - 1:
                part = jnp.where(row <= col, part, NEG)
            elif first + n * TILE < WIN:
                part = part + halo_bias
            parts.append(part)
        peak = parts[0]
        for part in parts[1:]:
            peak = jnp.maximum(peak, part)
        peak = jnp.max(peak, axis=0, keepdims=True)
        raised_cols.append(jnp.concatenate([jnp.exp2((part - peak).astype(BF)) for part in parts], axis=0))
    return jnp.concatenate(raised_cols, axis=1)


def both_heads(value, axis, along):
    place = iota2(value.shape, axis)
    half = value.shape[axis] // 2
    zero = jnp.zeros((), value.dtype)
    return jnp.concatenate([jnp.where(place < half, value, zero), jnp.where(place < half, zero, value)], axis=along)


def scores_body(
    head_size, meta_ref, halo_ref, wk_ref, wv_ref, qt_ref, k_ref, v_ref, vt_ref, cot_hbm, wo_hbm,
    raised_ref, grads_ref, scale_ref, q_ref, do_ref, dkh_ref, dvh_ref, khalo_t_ref, halo_t_ref, ot_ref, back_ref,
    kx, vx, vtx, dot_ref, cot_ref, wo_ref, sems,
):
    copies = fetch([cot_hbm, wo_hbm], [cot_ref, wo_ref], sems)
    span, width = k_ref.shape
    begin, length = meta_ref[0], meta_ref[1]
    halo = halo_ref[...]
    kh = mm(halo, wk_ref[...]).astype(BF)
    kx[:WIN] = kh
    khalo_t_ref[...] = kh.T
    vh = mm(halo, wv_ref[...]).astype(BF)
    vx[:WIN] = vh
    vtx[:, :WIN] = vh.T
    vtx[:, WIN:] = vt_ref[...]
    halo_t_ref[...] = halo.T
    kx[WIN:] = k_ref[...]
    vx[WIN:] = v_ref[...]

    pair = 2 * head_size
    tiles = span // TILE
    upper = iota2((pair, TILE), 0) < head_size
    ones = jnp.ones((16, REACH), BF)

    def one_pair(p, carry):
        cols = pl.ds(pl.multiple_of(p * pair, pair), pair)

        def multiply(a):
            here = slice(a * TILE, (a + 1) * TILE)
            keys = slice(a * TILE, a * TILE + REACH)
            scores = mm(kx[keys, cols], both_heads(qt_ref[cols, here], 0, 1))
            slopes = mm(vx[keys, cols], both_heads(dot_ref[cols, here], 0, 1))
            return scores, slopes

        halo_grads = []

        def raise_and_mix(a, scores):
            here = slice(a * TILE, (a + 1) * TILE)
            keys = slice(a * TILE, a * TILE + REACH)
            raised = raised_scores(scores, a * TILE, begin)
            raised_ref[p * tiles + a] = raised
            mixed = mm(jnp.concatenate([vtx[cols, keys], ones], axis=0), raised)
            time = begin + a * TILE + iota2((1, 2 * TILE), 1) % TILE
            scale = jnp.where(time < length, 1.0 / mixed[pair : pair + 1], 0.0)
            scale_ref[p * tiles + a] = scale
            spread_scale = jnp.where(upper, scale[:, :TILE], scale[:, TILE:])
            mixed = jnp.where(upper, mixed[:pair, :TILE], mixed[:pair, TILE:]) * spread_scale
            ot_ref[cols, here] = mixed.astype(BF)
            return raised, mixed, spread_scale

        def finish(a, slopes, raised, mixed, spread_scale):
            here = slice(a * TILE, (a + 1) * TILE)
            out_grad = dot_ref[cols, here].astype(F32)
            product = mixed * out_grad
            grad_cols = []
            for h in range(2):
                at = slice(h * TILE, (h + 1) * TILE)
                centre = jnp.sum(product[h * head_size : (h + 1) * head_size], axis=0, keepdims=True)
                grad_cols.append(raised[:, at] * (slopes[:, at] - centre).astype(BF))
            grads = jnp.concatenate(grad_cols, axis=1)
            grads_ref[p * tiles + a] = grads
            far = WIN - a * TILE
            queries = (qt_ref[cols, here].astype(F32) * spread_scale).T.astype(BF)
            out_grad = (out_grad * spread_scale).T.astype(BF)
            q_ref[here, cols] = queries
            do_ref[here, cols] = out_grad
            halo_grads.append((
                mm(grads[:far], both_heads(queries, 1, 0)),
                mm(raised[:far], both_heads(out_grad, 1, 0)),
            ))

        scores, slopes = multiply(0)
        waiting = None
        for a in range(tiles):
            ahead = multiply(a + 1) if a + 1 < tiles else None
            mixed = raise_and_mix(a, scores)
            if waiting is not None:
                finish(*waiting)
            waiting = (a, slopes, *mixed)
            if ahead is not None:
                scores, slopes = ahead
        finish(*waiting)
        for which, scale, out in ((0, math.log(2.0), dkh_ref), (1, 1.0, dvh_ref)):
            for j in range(WIN // TILE):
                total = None
                for a in range(min(j + 1, tiles)):
                    piece = halo_grads[a][which][(j - a) * TILE : (j - a + 1) * TILE]
                    total = piece if total is None else total + piece
                out[j * TILE : (j + 1) * TILE, cols] = (total * scale).astype(BF)
        return carry

    for copy in copies:
        copy.wait()
    dot_ref[...] = mm(cot_ref[...], wo_ref[...], NT).astype(BF).T
    lax.fori_loop(0, width // pair, one_pair, 0, unroll=4)
    back_ref[...] = (mm(dkh_ref[...], wk_ref[...], NT) + mm(dvh_ref[...], wv_ref[...], NT)).astype(BF)


def weights_body(
    scale, rows, head_size, meta_ref, normed_turned_ref, halo_t_ref, frames_ref, cot_hbm,
    wq_hbm, wk_hbm, wv_hbm, wo_hbm,
    q_ref, kt_ref, khalo_t_ref, ot, do_ref, raised_ref, grads_ref, scale_ref, dkh_ref, dvh_ref,
    keep_ref, send_ref, out_ref, slope_ref,
    normed_t, halo_t, mixed_t, ktx, dqt, dk, dv,
    wq, wk, wv, wo, cot_ref, sems,
):
    span, width = q_ref.shape
    copies = fetch(
        [wq_hbm, wk_hbm, wv_hbm, wo_hbm, cot_hbm], [wq, wk, wv, wo, cot_ref], sems
    )
    ktx[:, :WIN] = khalo_t_ref[...]
    ktx[:, WIN:] = kt_ref[...]
    pair = 2 * head_size
    tiles = span // TILE
    upper = iota2((pair, TILE), 0) < head_size

    def one_pair(p, carry):
        cols = pl.ds(pl.multiple_of(p * pair, pair), pair)
        own_grads = []
        for a in range(tiles):
            here = slice(a * TILE, (a + 1) * TILE)
            keys = slice(a * TILE, a * TILE + REACH)
            at = p * tiles + a
            shrink = scale_ref[at]
            moved = mm(ktx[cols, keys], grads_ref[at]) * (shrink * head_size ** (-0.5))
            dqt[cols, here] = jnp.where(upper, moved[:, :TILE], moved[:, TILE:]).astype(BF)
            near = slice(WIN - a * TILE, REACH)
            own_grads.append((
                mm(grads_ref[at, near], both_heads(q_ref[here, cols], 1, 0)),
                mm(raised_ref[at, near], both_heads(do_ref[here, cols], 1, 0)),
            ))
        for which, factor, out in ((0, math.log(2.0), dk), (1, 1.0, dv)):
            for j in range(tiles):
                total = None
                for a in range(j, tiles):
                    piece = own_grads[a][which][j * TILE : (j + 1) * TILE]
                    total = piece if total is None else total + piece
                out[j * TILE : (j + 1) * TILE, cols] = (total * factor).astype(BF)
        return carry

    lax.fori_loop(0, width // pair, one_pair, 0, unroll=4)

    for copy in copies:
        copy.wait()
    chunks = width // (2 * rows)
    split = (chunks, 2, rows, span)
    normed_t[...] = normed_turned_ref[...].reshape(split)
    halo_t[...] = halo_t_ref[...].reshape(split)
    mixed_t[...] = ot[...].reshape(split)
    mine = meta_ref[2]
    for side, out in ((1 - mine, send_ref), (mine, keep_ref)):
        own = normed_t[:, side].reshape(width // 2, span)
        far = halo_t[:, side].reshape(width // 2, span)
        mixed = mixed_t[:, side].reshape(width // 2, span)
        for n, total in enumerate((
            mm(own, dqt[...], NT),
            mm(own, dk[...]) + mm(far, dkh_ref[...]),
            mm(own, dv[...]) + mm(far, dvh_ref[...]),
            mm(mixed, cot_ref[...]),
        )):
            out[:, n * width : (n + 1) * width] = (total * scale).astype(BF)
    slope = mm(dqt[...].T, wq[...], NT)
    slope = slope + mm(dk[...], wk[...], NT)
    slope_ref[...] = slope + mm(dv[...], wv[...], NT)
    out = mm(ot[...].T, wo[...]) + frames_ref[...].astype(F32)
    out_ref[...] = out.astype(BF)


def returning_body(
    frames_ref, slope_ref, extra_ref, cot_ref, pick_t_ref, out_ref
):
    _, inverse, normed32 = unit_frames(frames_ref[...])
    slope = slope_ref[...] + extra_ref[...].astype(F32)
    centre = jnp.mean(slope * normed32, axis=1, keepdims=True)
    grad = inverse * (slope - normed32 * centre) + cot_ref[...].astype(F32)
    out_ref[...] = mm(pick_t_ref[...], grad.astype(BF)).astype(BF)


def arrived_body(placing_t_ref, in_ref, out_ref):
    out_ref[...] = mm(placing_t_ref[...], in_ref[...]).astype(BF)


def passed_along(shard, by):
    devices = lax.axis_size("seq")
    pairs = [(i, i + by) for i in range(devices) if 0 <= i + by < devices]
    return lax.ppermute(shard, "seq", pairs)


def spread_body(place_ref, *refs):
    parts = refs[0].shape[0]
    inputs, outs = refs[:-parts], refs[-parts:]
    for k, out in enumerate(outs):
        at = place_ref[0] ^ k
        total = inputs[0][at].astype(F32)
        for ref in inputs[1:]:
            total = total + ref[at].astype(F32)
        out[...] = total.astype(BF)


def spread(inputs, place, parts, carry=()):
    columns = inputs[0].shape[-1]
    inputs = [shard.reshape(parts, -1, columns) for shard in inputs]
    piece = sds(inputs[0].shape[1:])
    return vmem_call(spread_body, [piece] * parts, [place.reshape(1)] + inputs, smem=(0,), carry=carry)


def swapped(pieces, axis, step):
    count = lax.axis_size(axis)
    return [pieces[0]] + [
        lax.ppermute(piece, axis, [(i, i ^ (k * step)) for i in range(count)])
        for k, piece in enumerate(pieces[1:], 1)
    ]


def shards(
    frame_rows, row_frame, frame_owner, lengths,
    query_weight, key_weight, value_weight, out_weight, cotangent,
):
    devices = lax.axis_size(AXES)
    row_count, width = frame_rows.shape
    span = frame_owner.shape[1]
    slots = row_count // devices
    slab = span * lax.axis_size("seq")
    head_size = width // H
    cube = 2 * span * width * width
    square = sds((span, width))
    begin = (lax.axis_index("seq") * span).astype(jnp.int32)
    rows = width // devices
    in_kernel = rows % 16 == 0
    core = (lax.axis_index("seq") & 1).astype(jnp.int32)
    meta = jnp.stack([begin, lengths[0], core if in_kernel else jnp.zeros((), jnp.int32)])
    cot = cotangent[0]

    def exchanged(shard):
        got = lax.all_to_all(
            shard.reshape(devices, slots, width), AXES, split_axis=0, concat_axis=0, tiled=True
        )
        return got.reshape(devices * slots, width)

    outgoing, = vmem_call(
        lambda *refs: outgoing_body(span, slots, *refs),
        [square],
        [row_frame.reshape(1, row_count), frame_rows],
        hbm=(1,),
        scratch=[pltpu.VMEM((row_count, width), BF), pltpu.SemaphoreType.DMA((1,))],
        flops=cube,
    )
    incoming = exchanged(outgoing)
    pick, pick_t = vmem_call(
        lambda *refs: early_body(slots, *refs),
        [square, square],
        [frame_owner.reshape(span, 1)],
        flops=cube,
    )
    frames, normed = vmem_call(frames_body, [square, square], [pick, incoming], flops=cube)
    halo = passed_along(normed, 1)
    query_scale = head_size ** (-0.5) * math.log2(math.e)
    qt, k, kt, v, vt, wk, wv, normed_turned = vmem_call(
        lambda *refs: project_body(query_scale, *refs),
        [square] * 8,
        [normed, query_weight, key_weight, value_weight],
        hbm=(1, 2, 3),
        scratch=[pltpu.VMEM((width, width), BF), pltpu.SemaphoreType.DMA((3,))],
        flops=3 * cube,
    )
    units = H // 2 * (span // TILE)
    saved = sds((units, REACH, 2 * TILE))
    raised, grads, scales, q, do, dkh, dvh, khalo_t, halo_t, ot, back = vmem_call(
        lambda *refs: scores_body(head_size, *refs),
        [saved, saved, sds((units, 1, 2 * TILE), F32)] + [square] * 8,
        [meta, halo, wk, wv, qt, k, v, vt, cot, out_weight],
        smem=(0,),
        hbm=(8, 9),
        scratch=[pltpu.VMEM((WIN + span, width), BF)] * 2 + [pltpu.VMEM((width, WIN + span), BF)]
        + [pltpu.VMEM((width, span), BF)] * 3 + [pltpu.SemaphoreType.DMA((2,))],
        flops=12 * cube,
        limit=24,
    )
    extra = passed_along(back, -1)
    chunk = rows if in_kernel else width // 2
    split = pltpu.VMEM((width // (2 * chunk), 2, chunk, span), BF)
    half = sds((width // 2, 4 * width))
    whole = pltpu.VMEM((width, width), BF)
    keep, send, out_frames, slope = vmem_call(
        lambda *refs: weights_body(slab ** (-0.5), chunk, head_size, *refs),
        [half, half, square, sds((span, width), F32)],
        [meta, normed_turned, halo_t, frames, cot, query_weight, key_weight, value_weight, out_weight,
         q, kt, khalo_t, ot, do, raised, grads, scales, dkh, dvh],
        smem=(0,),
        hbm=(4, 5, 6, 7, 8),
        scratch=[split] * 3 + [pltpu.VMEM((width, WIN + span), BF)] + [whole] * 8
        + [pltpu.SemaphoreType.DMA((5,))],
        flops=18 * cube,
        limit=26,
    )
    send, extra = lax.optimization_barrier((send, extra))
    if not in_kernel:
        sums = jnp.concatenate([keep, send], axis=0).reshape(-1, 2, rows, 4 * width)
        keep = lax.dynamic_index_in_dim(sums, core, 1, keepdims=False).reshape(half.shape)
        send = lax.dynamic_index_in_dim(sums, 1 - core, 1, keepdims=False).reshape(half.shape)
    seqs = lax.axis_size("seq")
    got = lax.ppermute(send, "seq", [(i, i ^ 1) for i in range(seqs)])
    seqs = lax.axis_size("seq")
    got = lax.ppermute(send, "seq", [(i, i ^ 1) for i in range(seqs)])
    returning, = vmem_call(
        returning_body,
        [square],
        [frames, slope, extra, cot, pick_t],
        flops=cube,
    )
    pieces = spread([keep, got], lax.axis_index("stream"), lax.axis_size("stream"), [returning])
    pieces = swapped(pieces, "stream", 1)
    late_rows, returning = lax.optimization_barrier((row_frame.reshape(1, row_count), returning))
    arrived = exchanged(returning)
    placing_t, = vmem_call(
        lambda *refs: placing_t_body(span, slots, *refs),
        [sds((row_count, devices * slots))],
        [late_rows],
        flops=40 * cube,
    )
    frame_grads, = vmem_call(arrived_body, [square], [placing_t, arrived], flops=cube)
    pieces = swapped(spread(pieces, lax.axis_index("seq") >> 1, seqs // 2), "seq", 2)
    weight_grads = pieces[0].astype(F32)
    for piece in pieces[1:]:
        weight_grads = weight_grads + piece.astype(F32)
    return (out_frames[None], frame_grads, weight_grads)


def solution(mesh):
    return jax.shard_map(
        shards,
        mesh=mesh,
        in_specs=(
            P(AXES, None), P(AXES), P("stream", "seq"), P("stream"),
            P(), P(), P(), P(), P("stream", "seq", None),
        ),
        out_specs=(P("stream", "seq", None), P(AXES, None), P(AXES, None)),
        check_vma=False,
    )
```

```python
import math

import jax
import jax.numpy as jnp
from jax import lax
from jax.experimental import pallas as pl
from jax.experimental.pallas import tpu as pltpu
from jax.sharding import PartitionSpec as P

H = 8
WIN = 512
NEG = -1e30
EPS_NORM = 1e-06
AXES = ("stream", "seq")
BF = jnp.bfloat16
F32 = jnp.float32

NN = (((1,), (0,)), ((), ()))
NT = (((1,), (1,)), ((), ()))


def mm(a, b, dims=NN):
    return lax.dot_general(a, b, dims, preferred_element_type=F32)


def iota2(shape, dim):
    return lax.broadcasted_iota(jnp.int32, shape, dim)


def vmem_call(body, outs, args, smem=(), hbm=(), scratch=(), carry=(), flops=0, limit=12):
    used, inner, args = len(args), body, list(args) + list(carry)

    def body(*refs):
        inner(*refs[:used], *refs[len(args) :])

    spaces = [pltpu.SMEM if i in smem else pltpu.HBM if i in hbm else pltpu.VMEM for i in range(len(args))]
    size = sum(math.prod(a.shape) * a.dtype.itemsize for a in list(args) + list(outs))
    return pl.pallas_call(
        body,
        out_shape=tuple(outs),
        in_specs=[pl.BlockSpec(memory_space=space) for space in spaces],
        out_specs=tuple(pl.BlockSpec(memory_space=pltpu.VMEM) for _ in outs),
        scratch_shapes=list(scratch),
        compiler_params=pltpu.CompilerParams(vmem_limit_bytes=limit * 2**20),
        cost_estimate=pl.CostEstimate(flops=flops, bytes_accessed=size, transcendentals=0),
    )(*args)


def fetch(sources, targets, sems):
    copies = [
        pltpu.make_async_copy(source, target, sems.at[n])
        for n, (source, target) in enumerate(zip(sources, targets))
    ]
    for copy in copies:
        copy.start()
    return copies


def sds(shape, dtype=BF):
    return jax.ShapeDtypeStruct(shape, dtype)


def placing_of(span, slots, rf, total):
    count = rf.shape[1]
    target = jnp.where(rf >= 0, lax.div(rf, span), 1 << 20)
    slot = iota2((total, count), 0)
    owner = lax.div(slot, slots)
    rank = slot - owner * slots
    start = jnp.sum(jnp.where(target < owner, 1.0, 0.0), axis=1, keepdims=True)
    here = iota2((total, count), 1) - start.astype(jnp.int32)
    return jnp.where((target == owner) & (here == rank), 1.0, 0.0)


def outgoing_body(span, slots, rf_ref, rows_hbm, out_ref, rows_ref, sems):
    (rows_copy,) = fetch([rows_hbm], [rows_ref], sems)
    placing = placing_of(span, slots, rf_ref[...], out_ref.shape[0]).astype(BF)
    rows_copy.wait()
    out_ref[...] = mm(placing, rows_ref[...]).astype(BF)


def placing_t_body(span, slots, rf_ref, out_ref):
    out_ref[...] = placing_of(span, slots, rf_ref[...], out_ref.shape[1]).T.astype(BF)


def early_body(slots, owner_ref, pick_ref, pick_t_ref):
    span, lanes = owner_ref.shape[0], 128
    total = pick_ref.shape[1]
    owner = owner_ref[...]
    device = iota2((span, lanes), 1)
    hot = jnp.where(owner == device, 1.0, 0.0)
    strict = jnp.where(iota2((span, span), 1) < iota2((span, span), 0), 1.0, 0.0).astype(BF)
    before = mm(strict, hot.astype(BF))
    slot = jnp.sum(hot * (before + (device * slots).astype(F32)), axis=1, keepdims=True)
    slot = jnp.where(owner >= 0, slot.astype(jnp.int32), -1)
    pick = jnp.where(iota2((span, total), 1) == slot, 1.0, 0.0)
    pick_ref[...] = pick.astype(BF)
    pick_t_ref[...] = pick.T.astype(BF)


def unit_frames(frames):
    frames32 = frames.astype(F32)
    inverse = lax.rsqrt(jnp.mean(frames32 * frames32, axis=1, keepdims=True) + EPS_NORM)
    return frames32, inverse, frames32 * inverse


def frames_body(pick_ref, in_ref, frames_ref, normed_ref):
    frames = mm(pick_ref[...], in_ref[...]).astype(BF)
    frames_ref[...] = frames
    normed_ref[...] = unit_frames(frames)[2].astype(BF)


def project_body(
    query_scale, normed_ref, wq_hbm, wk_hbm, wv_hbm,
    qt_ref, k_ref, kt_ref, v_ref, vt_ref, wk_ref, wv_ref, normed_t_ref, wq_ref, sems,
):
    copies = fetch([wq_hbm, wk_hbm, wv_hbm], [wq_ref, wk_ref, wv_ref], sems)
    normed = normed_ref[...]
    normed_t_ref[...] = normed.T
    copies[0].wait()
    qt_ref[...] = (mm(normed, wq_ref[...]) * query_scale).astype(BF).T
    copies[1].wait()
    k = mm(normed, wk_ref[...]).astype(BF)
    k_ref[...] = k
    kt_ref[...] = k.T
    copies[2].wait()
    v = mm(normed, wv_ref[...]).astype(BF)
    v_ref[...] = v
    vt_ref[...] = v.T


TILE = 128
REACH = WIN + TILE


def raised_scores(scores, first, begin):
    row = iota2((TILE, TILE), 0)
    col = iota2((TILE, TILE), 1)
    halo_bias = jnp.where(begin == 0, NEG, 0.0)
    count = REACH // TILE
    raised_cols = []
    for h in range(2):
        at = slice(h * TILE, (h + 1) * TILE)
        parts = []
        for n in range(count):
            part = scores[n * TILE : (n + 1) * TILE, at]
            if n == 0:
                part = jnp.where(row > col, part, NEG)
            if n == count - 1:
                part = jnp.where(row <= col, part, NEG)
            elif first + n * TILE < WIN:
                part = part + halo_bias
            parts.append(part)
        peak = parts[0]
        for part in parts[1:]:
            peak = jnp.maximum(peak, part)
        peak = jnp.max(peak, axis=0, keepdims=True)
        raised_cols.append(jnp.concatenate([jnp.exp2((part - peak).astype(BF)) for part in parts], axis=0))
    return jnp.concatenate(raised_cols, axis=1)


def both_heads(value, axis, along):
    place = iota2(value.shape, axis)
    half = value.shape[axis] // 2
    zero = jnp.zeros((), value.dtype)
    return jnp.concatenate([jnp.where(place < half, value, zero), jnp.where(place < half, zero, value)], axis=along)


def scores_body(
    head_size, meta_ref, halo_ref, wk_ref, wv_ref, qt_ref, k_ref, v_ref, vt_ref, cot_hbm, wo_hbm,
    raised_ref, grads_ref, scale_ref, q_ref, do_ref, dkh_ref, dvh_ref, khalo_t_ref, halo_t_ref, ot_ref, back_ref,
    kx, vx, vtx, dot_ref, cot_ref, wo_ref, sems,
):
    copies = fetch([cot_hbm, wo_hbm], [cot_ref, wo_ref], sems)
    span, width = k_ref.shape
    begin, length = meta_ref[0], meta_ref[1]
    halo = halo_ref[...]
    kh = mm(halo, wk_ref[...]).astype(BF)
    kx[:WIN] = kh
    khalo_t_ref[...] = kh.T
    vh = mm(halo, wv_ref[...]).astype(BF)
    vx[:WIN] = vh
    vtx[:, :WIN] = vh.T
    vtx[:, WIN:] = vt_ref[...]
    halo_t_ref[...] = halo.T
    kx[WIN:] = k_ref[...]
    vx[WIN:] = v_ref[...]

    pair = 2 * head_size
    tiles = span // TILE
    upper = iota2((pair, TILE), 0) < head_size
    ones = jnp.ones((16, REACH), BF)

    def one_pair(p, carry):
        cols = pl.ds(pl.multiple_of(p * pair, pair), pair)

        def multiply(a):
            here = slice(a * TILE, (a + 1) * TILE)
            keys = slice(a * TILE, a * TILE + REACH)
            scores = mm(kx[keys, cols], both_heads(qt_ref[cols, here], 0, 1))
            slopes = mm(vx[keys, cols], both_heads(dot_ref[cols, here], 0, 1))
            return scores, slopes

        halo_grads = []

        def raise_and_mix(a, scores):
            here = slice(a * TILE, (a + 1) * TILE)
            keys = slice(a * TILE, a * TILE + REACH)
            raised = raised_scores(scores, a * TILE, begin)
            raised_ref[p * tiles + a] = raised
            mixed = mm(jnp.concatenate([vtx[cols, keys], ones], axis=0), raised)
            time = begin + a * TILE + iota2((1, 2 * TILE), 1) % TILE
            scale = jnp.where(time < length, 1.0 / mixed[pair : pair + 1], 0.0)
            scale_ref[p * tiles + a] = scale
            spread_scale = jnp.where(upper, scale[:, :TILE], scale[:, TILE:])
            mixed = jnp.where(upper, mixed[:pair, :TILE], mixed[:pair, TILE:]) * spread_scale
            ot_ref[cols, here] = mixed.astype(BF)
            return raised, mixed, spread_scale

        def finish(a, slopes, raised, mixed, spread_scale):
            here = slice(a * TILE, (a + 1) * TILE)
            out_grad = dot_ref[cols, here].astype(F32)
            product = mixed * out_grad
            grad_cols = []
            for h in range(2):
                at = slice(h * TILE, (h + 1) * TILE)
                centre = jnp.sum(product[h * head_size : (h + 1) * head_size], axis=0, keepdims=True)
                grad_cols.append(raised[:, at] * (slopes[:, at] - centre).astype(BF))
            grads = jnp.concatenate(grad_cols, axis=1)
            grads_ref[p * tiles + a] = grads
            far = WIN - a * TILE
            queries = (qt_ref[cols, here].astype(F32) * spread_scale).T.astype(BF)
            out_grad = (out_grad * spread_scale).T.astype(BF)
            q_ref[here, cols] = queries
            do_ref[here, cols] = out_grad
            halo_grads.append((
                mm(grads[:far], both_heads(queries, 1, 0)),
                mm(raised[:far], both_heads(out_grad, 1, 0)),
            ))

        scores, slopes = multiply(0)
        waiting = None
        for a in range(tiles):
            ahead = multiply(a + 1) if a + 1 < tiles else None
            if waiting is not None:
                finish(*waiting)
            mixed = raise_and_mix(a, scores)
            waiting = (a, slopes, *mixed)
            if ahead is not None:
                scores, slopes = ahead
        finish(*waiting)
        for which, scale, out in ((0, math.log(2.0), dkh_ref), (1, 1.0, dvh_ref)):
            for j in range(WIN // TILE):
                total = None
                for a in range(min(j + 1, tiles)):
                    piece = halo_grads[a][which][(j - a) * TILE : (j - a + 1) * TILE]
                    total = piece if total is None else total + piece
                out[j * TILE : (j + 1) * TILE, cols] = (total * scale).astype(BF)
        return carry

    for copy in copies:
        copy.wait()
    dot_ref[...] = mm(cot_ref[...], wo_ref[...], NT).astype(BF).T
    lax.fori_loop(0, width // pair, one_pair, 0, unroll=4)
    back_ref[...] = (mm(dkh_ref[...], wk_ref[...], NT) + mm(dvh_ref[...], wv_ref[...], NT)).astype(BF)


def weights_body(
    scale, rows, head_size, meta_ref, normed_turned_ref, halo_t_ref, frames_ref, cot_hbm,
    wq_hbm, wk_hbm, wv_hbm, wo_hbm,
    q_ref, kt_ref, khalo_t_ref, ot, do_ref, raised_ref, grads_ref, scale_ref, dkh_ref, dvh_ref,
    keep_ref, send_ref, out_ref, slope_ref,
    normed_t, halo_t, mixed_t, ktx, dqt, dk, dv,
    wq, wk, wv, wo, cot_ref, sems,
):
    span, width = q_ref.shape
    copies = fetch(
        [wq_hbm, wk_hbm, wv_hbm, wo_hbm, cot_hbm], [wq, wk, wv, wo, cot_ref], sems
    )
    ktx[:, :WIN] = khalo_t_ref[...]
    ktx[:, WIN:] = kt_ref[...]
    pair = 2 * head_size
    tiles = span // TILE
    upper = iota2((pair, TILE), 0) < head_size

    def one_pair(p, carry):
        cols = pl.ds(pl.multiple_of(p * pair, pair), pair)
        own_grads = []
        for a in range(tiles):
            here = slice(a * TILE, (a + 1) * TILE)
            keys = slice(a * TILE, a * TILE + REACH)
            at = p * tiles + a
            shrink = scale_ref[at]
            moved = mm(ktx[cols, keys], grads_ref[at]) * (shrink * head_size ** (-0.5))
            dqt[cols, here] = jnp.where(upper, moved[:, :TILE], moved[:, TILE:]).astype(BF)
            near = slice(WIN - a * TILE, REACH)
            own_grads.append((
                mm(grads_ref[at, near], both_heads(q_ref[here, cols], 1, 0)),
                mm(raised_ref[at, near], both_heads(do_ref[here, cols], 1, 0)),
            ))
        for which, factor, out in ((0, math.log(2.0), dk), (1, 1.0, dv)):
            for j in range(tiles):
                total = None
                for a in range(j, tiles):
                    piece = own_grads[a][which][j * TILE : (j + 1) * TILE]
                    total = piece if total is None else total + piece
                out[j * TILE : (j + 1) * TILE, cols] = (total * factor).astype(BF)
        return carry

    lax.fori_loop(0, width // pair, one_pair, 0, unroll=4)

    for copy in copies:
        copy.wait()
    chunks = width // (2 * rows)
    split = (chunks, 2, rows, span)
    normed_t[...] = normed_turned_ref[...].reshape(split)
    halo_t[...] = halo_t_ref[...].reshape(split)
    mixed_t[...] = ot[...].reshape(split)
    mine = meta_ref[2]
    for side, out in ((1 - mine, send_ref), (mine, keep_ref)):
        own = normed_t[:, side].reshape(width // 2, span)
        far = halo_t[:, side].reshape(width // 2, span)
        mixed = mixed_t[:, side].reshape(width // 2, span)
        for n, total in enumerate((
            mm(own, dqt[...], NT),
            mm(own, dk[...]) + mm(far, dkh_ref[...]),
            mm(own, dv[...]) + mm(far, dvh_ref[...]),
            mm(mixed, cot_ref[...]),
        )):
            out[:, n * width : (n + 1) * width] = (total * scale).astype(BF)
    slope = mm(dqt[...].T, wq[...], NT)
    slope = slope + mm(dk[...], wk[...], NT)
    slope_ref[...] = slope + mm(dv[...], wv[...], NT)
    out = mm(ot[...].T, wo[...]) + frames_ref[...].astype(F32)
    out_ref[...] = out.astype(BF)


def returning_body(
    frames_ref, slope_ref, extra_ref, cot_ref, pick_t_ref, out_ref
):
    _, inverse, normed32 = unit_frames(frames_ref[...])
    slope = slope_ref[...] + extra_ref[...].astype(F32)
    centre = jnp.mean(slope * normed32, axis=1, keepdims=True)
    grad = inverse * (slope - normed32 * centre) + cot_ref[...].astype(F32)
    out_ref[...] = mm(pick_t_ref[...], grad.astype(BF)).astype(BF)


def arrived_body(placing_t_ref, in_ref, out_ref):
    out_ref[...] = mm(placing_t_ref[...], in_ref[...]).astype(BF)


def passed_along(shard, by):
    devices = lax.axis_size("seq")
    pairs = [(i, i + by) for i in range(devices) if 0 <= i + by < devices]
    return lax.ppermute(shard, "seq", pairs)


def spread_body(place_ref, *refs):
    parts = refs[0].shape[0]
    inputs, outs = refs[:-parts], refs[-parts:]
    for k, out in enumerate(outs):
        at = place_ref[0] ^ k
        total = inputs[0][at].astype(F32)
        for ref in inputs[1:]:
            total = total + ref[at].astype(F32)
        out[...] = total.astype(BF)


def spread(inputs, place, parts, carry=()):
    columns = inputs[0].shape[-1]
    inputs = [shard.reshape(parts, -1, columns) for shard in inputs]
    piece = sds(inputs[0].shape[1:])
    return vmem_call(spread_body, [piece] * parts, [place.reshape(1)] + inputs, smem=(0,), carry=carry)


def swapped(pieces, axis, step):
    count = lax.axis_size(axis)
    return [pieces[0]] + [
        lax.ppermute(piece, axis, [(i, i ^ (k * step)) for i in range(count)])
        for k, piece in enumerate(pieces[1:], 1)
    ]


def shards(
    frame_rows, row_frame, frame_owner, lengths,
    query_weight, key_weight, value_weight, out_weight, cotangent,
):
    devices = lax.axis_size(AXES)
    row_count, width = frame_rows.shape
    span = frame_owner.shape[1]
    slots = row_count // devices
    slab = span * lax.axis_size("seq")
    head_size = width // H
    cube = 2 * span * width * width
    square = sds((span, width))
    begin = (lax.axis_index("seq") * span).astype(jnp.int32)
    rows = width // devices
    in_kernel = rows % 16 == 0
    core = (lax.axis_index("seq") & 1).astype(jnp.int32)
    meta = jnp.stack([begin, lengths[0], core if in_kernel else jnp.zeros((), jnp.int32)])
    cot = cotangent[0]

    def exchanged(shard):
        got = lax.all_to_all(
            shard.reshape(devices, slots, width), AXES, split_axis=0, concat_axis=0, tiled=True
        )
        return got.reshape(devices * slots, width)

    outgoing, = vmem_call(
        lambda *refs: outgoing_body(span, slots, *refs),
        [square],
        [row_frame.reshape(1, row_count), frame_rows],
        hbm=(1,),
        scratch=[pltpu.VMEM((row_count, width), BF), pltpu.SemaphoreType.DMA((1,))],
        flops=cube,
    )
    incoming = exchanged(outgoing)
    pick, pick_t = vmem_call(
        lambda *refs: early_body(slots, *refs),
        [square, square],
        [frame_owner.reshape(span, 1)],
        flops=cube,
    )
    frames, normed = vmem_call(frames_body, [square, square], [pick, incoming], flops=cube)
    halo = passed_along(normed, 1)
    query_scale = head_size ** (-0.5) * math.log2(math.e)
    qt, k, kt, v, vt, wk, wv, normed_turned = vmem_call(
        lambda *refs: project_body(query_scale, *refs),
        [square] * 8,
        [normed, query_weight, key_weight, value_weight],
        hbm=(1, 2, 3),
        scratch=[pltpu.VMEM((width, width), BF), pltpu.SemaphoreType.DMA((3,))],
        flops=3 * cube,
    )
    units = H // 2 * (span // TILE)
    saved = sds((units, REACH, 2 * TILE))
    raised, grads, scales, q, do, dkh, dvh, khalo_t, halo_t, ot, back = vmem_call(
        lambda *refs: scores_body(head_size, *refs),
        [saved, saved, sds((units, 1, 2 * TILE), F32)] + [square] * 8,
        [meta, halo, wk, wv, qt, k, v, vt, cot, out_weight],
        smem=(0,),
        hbm=(8, 9),
        scratch=[pltpu.VMEM((WIN + span, width), BF)] * 2 + [pltpu.VMEM((width, WIN + span), BF)]
        + [pltpu.VMEM((width, span), BF)] * 3 + [pltpu.SemaphoreType.DMA((2,))],
        flops=12 * cube,
        limit=24,
    )
    extra = passed_along(back, -1)
    chunk = rows if in_kernel else width // 2
    split = pltpu.VMEM((width // (2 * chunk), 2, chunk, span), BF)
    half = sds((width // 2, 4 * width))
    whole = pltpu.VMEM((width, width), BF)
    keep, send, out_frames, slope = vmem_call(
        lambda *refs: weights_body(slab ** (-0.5), chunk, head_size, *refs),
        [half, half, square, sds((span, width), F32)],
        [meta, normed_turned, halo_t, frames, cot, query_weight, key_weight, value_weight, out_weight,
         q, kt, khalo_t, ot, do, raised, grads, scales, dkh, dvh],
        smem=(0,),
        hbm=(4, 5, 6, 7, 8),
        scratch=[split] * 3 + [pltpu.VMEM((width, WIN + span), BF)] + [whole] * 8
        + [pltpu.SemaphoreType.DMA((5,))],
        flops=18 * cube,
        limit=26,
    )
    send, extra = lax.optimization_barrier((send, extra))
    if not in_kernel:
        sums = jnp.concatenate([keep, send], axis=0).reshape(-1, 2, rows, 4 * width)
        keep = lax.dynamic_index_in_dim(sums, core, 1, keepdims=False).reshape(half.shape)
        send = lax.dynamic_index_in_dim(sums, 1 - core, 1, keepdims=False).reshape(half.shape)
    seqs = lax.axis_size("seq")
    got = lax.ppermute(send, "seq", [(i, i ^ 1) for i in range(seqs)])
    seqs = lax.axis_size("seq")
    got = lax.ppermute(send, "seq", [(i, i ^ 1) for i in range(seqs)])
    returning, = vmem_call(
        returning_body,
        [square],
        [frames, slope, extra, cot, pick_t],
        flops=cube,
    )
    pieces = spread([keep, got], lax.axis_index("stream"), lax.axis_size("stream"), [returning])
    pieces = swapped(pieces, "stream", 1)
    late_rows, returning = lax.optimization_barrier((row_frame.reshape(1, row_count), returning))
    arrived = exchanged(returning)
    placing_t, = vmem_call(
        lambda *refs: placing_t_body(span, slots, *refs),
        [sds((row_count, devices * slots))],
        [late_rows],
        flops=40 * cube,
    )
    frame_grads, = vmem_call(arrived_body, [square], [placing_t, arrived], flops=cube)
    pieces = swapped(spread(pieces, lax.axis_index("seq") >> 1, seqs // 2), "seq", 2)
    weight_grads = pieces[0].astype(F32)
    for piece in pieces[1:]:
        weight_grads = weight_grads + piece.astype(F32)
    return (out_frames[None], frame_grads, weight_grads)


def solution(mesh):
    return jax.shard_map(
        shards,
        mesh=mesh,
        in_specs=(
            P(AXES, None), P(AXES), P("stream", "seq"), P("stream"),
            P(), P(), P(), P(), P("stream", "seq", None),
        ),
        out_specs=(P("stream", "seq", None), P(AXES, None), P(AXES, None)),
        check_vma=False,
    )
```
